32 devices in a mesh: bulk: 8 (over z, core), blk: 4 (over y, x).
Axes of the slice: x: 2, y: 2, z: 4, core: 2. Of those that a mesh axis runs over, the one named last changes fastest.
Arguments:
- factor: float32 [32768, 4096], P(('bulk', 'blk')), parts along dimension 0, as said below
- initial: float32 [32768, 128], P(('bulk', 'blk')), parts along dimension 0, may hold values from -6 to 6
- bounds: float32 [16], P('bulk'), parts along dimension 0, may hold values from 0 to 15.5, as said below
Outputs:
- basis_rows: float32 [32768, 128], P(('bulk', 'blk')), parts along dimension 0
- projected: float32 [1024, 128], P('bulk'), parts along dimension 0
- residual: float32 [32768, 128], P(('bulk', 'blk')), parts along dimension 0
The draws below stay inside these ranges and needn't reach their ends.
There are 8 independent parts, one for each index of `bulk`. The reference program is written for one: setup_inputs(seed, part) draws one part's arguments, and reference() takes and returns one part's arrays. A program takes and returns all parts, laid end to end along the dimension named above; each array names one. Nothing has to cross between parts.
Inputs may be any that keep to these rules, and one draw needn't show every extreme that they name: factor is symmetric. `bounds`: the upper end exceeds the lower end by 14 or more.
All inputs are finite; a program needn't handle non-finite values.
Results may differ from the reference program's by a relative error of at most 0.0003.
Values sent between devices are 32-bit elements; how exact they have to be, the bound alone decides.
No kernel may reach another device: no remote copies, remote signals or barrier semaphores. Data moves between devices by JAX's collectives and lax.ppermute only.
A program may use at most 64 MiB of HBM per device.

```python
import jax
import jax.numpy as jnp
from jax import lax

N = 4096
K = 128
DEGREE = 8


def draw_factor(key, part):
    first_key = jax.random.fold_in(key, 11)
    second_key = jax.random.fold_in(key, 12)
    entries = jax.random.normal(first_key, (N, N), jnp.float32)
    symmetric_part = (entries + entries.T) * (0.70710678 * 1.6 / jnp.sqrt(jnp.float32(N)))
    diagonal = jnp.exp(jax.random.uniform(second_key, (N,), jnp.float32, jnp.log(4.0), jnp.log(11.0)))
    return symmetric_part + jnp.diag(diagonal)


def draw_bounds(key, part):
    low_key = jax.random.fold_in(key, 21)
    high_key = jax.random.fold_in(key, 22)
    low_end = jax.random.uniform(low_key, (1,), jnp.float32, 0.0, 0.5)
    high_end = jax.random.uniform(high_key, (1,), jnp.float32, 14.8, 15.3)
    return jnp.concatenate([low_end, high_end])


def shard_levels(stream_key, extent, shards, low, largest):
    gain, own = 1.0, jax.random.fold_in(stream_key, 6)
    for axis_at, parts in shards:
        heights = jnp.exp(jax.random.uniform(jax.random.fold_in(own, axis_at), (parts,), jnp.float32, low / len(shards), largest / len(shards)))
        gain = gain * jnp.repeat(heights, extent[axis_at] // parts).reshape([-1 if axis == axis_at else 1 for axis in range(len(extent))])
    return gain


def normal_values(own_key, shape, deviation, reach, split=(), held_as=jnp.bfloat16):
    drawn = deviation * jax.random.normal(own_key, shape, jnp.float32)
    if split:
        drawn = drawn * shard_levels(own_key, shape, split, -0.22, 0.18)
    return jnp.clip(drawn, -reach, reach).astype(held_as)


def setup_inputs(seed: int = 0, part: int = 0) -> dict:
    key_list = jax.random.split(jax.random.key(seed), 4)
    part_keys = jax.random.split(jax.random.fold_in(key_list[3], part), 4)
    factor = draw_factor(jax.random.fold_in(jax.random.fold_in(key_list[3], part), 71), part)
    initial = normal_values(part_keys[1], (N, K), 1.0, 6.0, ((0, 4),), jnp.float32)
    bounds = draw_bounds(jax.random.fold_in(jax.random.fold_in(key_list[3], part), 71), part)
    return dict(factor=factor, initial=initial, bounds=bounds)


def product(factor, vectors):
    return jnp.dot(factor.astype(jnp.float32), vectors.astype(jnp.float32), precision=lax.Precision.HIGHEST, preferred_element_type=jnp.float32)

def lower_solve(cholesky_low, right_side):
    return lax.linalg.triangular_solve(cholesky_low, right_side, left_side=True, lower=True)

def reference(factor, initial, bounds):
    centre = (bounds[0] + bounds[1]) / 2.0
    radius = (bounds[1] - bounds[0]) / 2.0
    previous = initial
    current = (product(factor, initial) - centre * initial) / radius
    for order_step in range(DEGREE - 1):
        scaled = (product(factor, current) - centre * current) / radius
        following = 2.0 * scaled - previous
        previous = current
        current = following
    filtered = current
    gram_matrix = jnp.dot(filtered.T.astype(jnp.float32), filtered.astype(jnp.float32), precision=lax.Precision.HIGHEST, preferred_element_type=jnp.float32)
    cholesky_low = jnp.linalg.cholesky(gram_matrix)
    basis_rows = lower_solve(cholesky_low, filtered.T).T
    mapped = product(factor, basis_rows)
    projected = jnp.dot(basis_rows.T.astype(jnp.float32), mapped.astype(jnp.float32), precision=lax.Precision.HIGHEST, preferred_element_type=jnp.float32)
    residual = mapped - jnp.dot(basis_rows.astype(jnp.float32), projected.astype(jnp.float32), precision=lax.Precision.HIGHEST, preferred_element_type=jnp.float32)
    return (basis_rows, projected, residual)
```

```python
import functools

import jax
import jax.numpy as jnp
from jax import lax
from jax.experimental import pallas as pl
from jax.experimental.pallas import tpu as pltpu
from jax.sharding import PartitionSpec as P

DEGREE = 8
HIGHEST = lax.Precision.HIGHEST
WHOLE = pl.BlockSpec(memory_space=pltpu.VMEM)
SCALARS = pl.BlockSpec(memory_space=pltpu.SMEM)
VMEM_LIMIT = 16 * 2**20


def params():
    return pltpu.CompilerParams(vmem_limit_bytes=VMEM_LIMIT)


def high_low(values):
    high = values.astype(jnp.bfloat16)
    low = (values - high.astype(jnp.float32)).astype(jnp.bfloat16)
    return high, low


def split_piece(factor, piece, width):
    rows = factor.shape[0]
    tile = min(rows, 256)

    def kernel(piece_ref, factor_ref, out_ref):
        high, low = high_low(factor_ref[...])
        out_ref[:, :width] = high
        out_ref[:, width:] = low

    return pl.pallas_call(
        kernel,
        out_shape=jax.ShapeDtypeStruct((rows, 2 * width), jnp.bfloat16),
        grid_spec=pltpu.PrefetchScalarGridSpec(
            num_scalar_prefetch=1,
            grid=(rows // tile,),
            in_specs=[pl.BlockSpec((tile, width), lambda i, piece_ref: (i, piece_ref[0]))],
            out_specs=pl.BlockSpec((tile, 2 * width), lambda i, piece_ref: (i, 0)),
        ),
        compiler_params=params(),
        cost_estimate=pl.CostEstimate(flops=0, bytes_accessed=8 * rows * width, transcendentals=0),
    )(piece.reshape(1), factor)


def stack_vectors(stacked_ref, at, vectors):
    width, columns = vectors.shape
    high, low = high_low(vectors)
    for start in (0, width):
        stacked_ref[at, start : start + width, :columns] = high
        stacked_ref[at, start : start + width, columns:] = low


def product_tile(pieces, stacked_ref, rows, columns):
    total = None
    for at, piece in enumerate(pieces):
        term = jnp.dot(piece[rows, :], stacked_ref[at], preferred_element_type=jnp.float32)
        total = term if total is None else total + term
    return total[:, :columns] + total[:, columns:]


def row_tiles(rows):
    tile = min(rows // 2, 256)
    return [slice(start, start + tile) for start in range(0, rows, tile)]


def product_cost(pieces):
    rows, doubled = pieces[0].shape
    return pl.CostEstimate(
        flops=2 * rows * doubled * 256 * len(pieces),
        bytes_accessed=2 * rows * doubled * len(pieces),
        transcendentals=0,
    )


def partial_product(total, pieces, vectors):
    n = len(pieces)
    rows, (width, columns) = pieces[0].shape[0], vectors[0].shape

    def kernel(*refs):
        piece_refs, vector_refs = refs[:n], refs[n : 2 * n]
        total_ref = refs[2 * n] if total is not None else None
        out_ref, stacked_ref = refs[-2:]
        for at in range(n):
            stack_vectors(stacked_ref, at, vector_refs[at][...])
        for tile in row_tiles(rows):
            value = product_tile(piece_refs, stacked_ref, tile, columns)
            out_ref[tile, :] = value if total_ref is None else total_ref[tile, :] + value

    operands = [*pieces, *vectors] + ([] if total is None else [total])
    return pl.pallas_call(
        kernel,
        out_shape=jax.ShapeDtypeStruct((rows, columns), jnp.float32),
        in_specs=[WHOLE] * len(operands),
        out_specs=WHOLE,
        scratch_shapes=[pltpu.VMEM((n, 2 * width, 2 * columns), jnp.bfloat16)],
        compiler_params=params(),
        cost_estimate=product_cost(pieces),
    )(*operands)


def recurrence_step(coefficients, total, pieces, vectors, current, previous):
    n, halves = len(pieces), len(current)
    rows, (width, columns) = pieces[0].shape[0], vectors[0].shape
    half = rows // halves

    def kernel(coefficient_ref, *refs):
        piece_refs, refs = refs[:n], refs[n:]
        vector_refs, refs = refs[:n], refs[n:]
        total_ref, refs = (refs[0], refs[1:]) if total is not None else (None, refs)
        current_refs, refs = refs[:halves], refs[halves:]
        previous_refs, refs = (refs[:halves], refs[halves:]) if previous else (None, refs)
        out_refs, stacked_ref = refs[:halves], refs[halves]
        for at in range(n):
            stack_vectors(stacked_ref, at, vector_refs[at][...])
        centre, inverse_radius = coefficient_ref[0], coefficient_ref[1]
        for tile in row_tiles(rows):
            value = product_tile(piece_refs, stacked_ref, tile, columns)
            if total_ref is not None:
                value = value + total_ref[tile, :]
            at, start = divmod(tile.start, half)
            own = slice(start, start + tile.stop - tile.start)
            value = (value - centre * current_refs[at][own, :]) * inverse_radius
            if previous_refs is not None:
                value = 2.0 * value - previous_refs[at][own, :]
            out_refs[at][own, :] = value

    operands = [*pieces, *vectors] + ([] if total is None else [total])
    operands += [*current, *(previous or ())]
    return pl.pallas_call(
        kernel,
        out_shape=[jax.ShapeDtypeStruct((half, columns), jnp.float32)] * halves,
        in_specs=[SCALARS] + [WHOLE] * len(operands),
        out_specs=[WHOLE] * halves,
        scratch_shapes=[pltpu.VMEM((n, 2 * width, 2 * columns), jnp.bfloat16)],
        compiler_params=params(),
        cost_estimate=product_cost(pieces),
    )(coefficients, *operands)


def dot_high(left_side, right_side, contract):
    return lax.dot_general(
        left_side, right_side, (contract, ((), ())), precision=HIGHEST, preferred_element_type=jnp.float32
    )


def gram_of(halves):
    def kernel(*refs):
        *in_refs, out_ref = refs
        total = None
        for ref in in_refs:
            term = dot_high(ref[...], ref[...], ((0,), (0,)))
            total = term if total is None else total + term
        out_ref[...] = total

    columns = halves[0].shape[1]
    return pl.pallas_call(
        kernel,
        out_shape=jax.ShapeDtypeStruct((columns, columns), jnp.float32),
        in_specs=[WHOLE] * len(halves),
        out_specs=WHOLE,
        compiler_params=params(),
    )(*halves)


def basis_of(halves, inverse_low):
    def kernel(inverse_ref, *refs):
        *in_refs, out_ref = refs
        at = 0
        for ref in in_refs:
            out_ref[at : at + ref.shape[0], :] = dot_high(ref[...], inverse_ref[...], ((1,), (1,)))
            at += ref.shape[0]

    rows, columns = sum(half.shape[0] for half in halves), halves[0].shape[1]
    return pl.pallas_call(
        kernel,
        out_shape=jax.ShapeDtypeStruct((rows, columns), jnp.float32),
        in_specs=[WHOLE] * (1 + len(halves)),
        out_specs=WHOLE,
        compiler_params=params(),
    )(inverse_low, *halves)


def mapped_and_projected(total, pieces, vectors, inverse_low, basis_rows):
    n = len(pieces)
    rows, (width, columns) = pieces[0].shape[0], vectors[0].shape

    def kernel(*refs):
        piece_refs, refs = refs[:n], refs[n:]
        vector_refs, refs = refs[:n], refs[n:]
        total_ref, refs = (refs[0], refs[1:]) if total is not None else (None, refs)
        inverse_ref, basis_ref, mapped_ref, projected_ref, stacked_ref = refs
        for at in range(n):
            stack_vectors(stacked_ref, at, vector_refs[at][...])
        projected = None
        for tile in row_tiles(rows):
            value = product_tile(piece_refs, stacked_ref, tile, columns)
            if total_ref is not None:
                value = value + total_ref[tile, :]
            mapped = dot_high(value, inverse_ref[...], ((1,), (1,)))
            mapped_ref[tile, :] = mapped
            term = dot_high(basis_ref[tile, :], mapped, ((0,), (0,)))
            projected = term if projected is None else projected + term
        projected_ref[...] = projected

    operands = [*pieces, *vectors] + ([] if total is None else [total]) + [inverse_low, basis_rows]
    return pl.pallas_call(
        kernel,
        out_shape=[
            jax.ShapeDtypeStruct((rows, columns), jnp.float32),
            jax.ShapeDtypeStruct((columns, columns), jnp.float32),
        ],
        in_specs=[WHOLE] * len(operands),
        out_specs=[WHOLE] * 2,
        scratch_shapes=[pltpu.VMEM((n, 2 * width, 2 * columns), jnp.bfloat16)],
        compiler_params=params(),
        cost_estimate=product_cost(pieces),
    )(*operands)


def residual_of(mapped, basis_rows, terms):
    def kernel(mapped_ref, basis_ref, *refs):
        *term_refs, projected_ref, residual_ref = refs
        values = [ref[...] for ref in term_refs]
        while len(values) > 1:
            values = [values[at] + values[at + 1] for at in range(0, len(values) - 1, 2)] + (
                [values[-1]] if len(values) % 2 else []
            )
        projected_ref[...] = values[0]
        residual_ref[...] = mapped_ref[...] - dot_high(basis_ref[...], values[0], ((1,), (0,)))

    return pl.pallas_call(
        kernel,
        out_shape=[
            jax.ShapeDtypeStruct(terms[0].shape, jnp.float32),
            jax.ShapeDtypeStruct(mapped.shape, jnp.float32),
        ],
        in_specs=[WHOLE] * (2 + len(terms)),
        out_specs=[WHOLE] * 2,
        compiler_params=params(),
    )(mapped, basis_rows, *terms)


def exchange(value, offset, n):
    return lax.ppermute(value, "blk", [(at, at ^ offset) for at in range(n)])


def sum_of(terms):
    return (terms[0] + terms[1]) + (terms[2] + terms[3])


def local(n, factor, initial, bounds):
    centre = (bounds[0] + bounds[1]) / 2.0
    radius = (bounds[1] - bounds[0]) / 2.0
    coefficients = jnp.stack([centre, 1.0 / radius])
    rows, columns = initial.shape
    half = rows // 2
    me = lax.axis_index("blk")
    square = n == 4

    if square:
        pieces = [
            [split_piece(factor, 2 * jnp.bitwise_xor(me, offset) + h, half) for h in range(2)] for offset in range(4)
        ]

        def gather_product(halves, last):
            top, bottom = halves
            x_top, y_bottom = exchange(top, 1, n), exchange(bottom, 2, n)
            x_bottom, y_top = exchange(bottom, 1, n), exchange(top, 2, n)
            total = partial_product(None, pieces[0], [top, bottom])
            xy_top, xy_bottom = exchange(x_top, 2, n), exchange(y_bottom, 1, n)
            total = partial_product(total, [pieces[1][0], pieces[2][1]], [x_top, y_bottom])
            total = partial_product(total, [pieces[1][1], pieces[2][0]], [x_bottom, y_top])
            return last(total, pieces[3], [xy_top, xy_bottom])

        def all_terms(term):
            return [term] + [exchange(term, offset, n) for offset in (1, 2, 3)]
    else:
        pieces = [split_piece(factor, jnp.int32(at), 2 * half) for at in range(n)]

        def gather_product(halves, last):
            gathered = lax.all_gather(jnp.concatenate(halves), "blk")
            return last(None, pieces, [gathered[at] for at in range(n)])

        def all_terms(term):
            gathered = lax.all_gather(term, "blk")
            return [gathered[at] for at in range(n)]

    previous, current = None, [initial[:half], initial[half:]]
    for order_step in range(DEGREE):
        following = gather_product(
            current,
            lambda total, last_pieces, vectors: recurrence_step(
                coefficients, total, last_pieces, vectors, current, previous
            ),
        )
        previous, current = current, following

    gram_terms = all_terms(gram_of(current))
    gram_matrix = sum_of(gram_terms) if square else sum(gram_terms)
    cholesky_low = lax.linalg.cholesky(gram_matrix, symmetrize_input=False)
    inverse_low = lax.linalg.triangular_solve(
        cholesky_low, jnp.eye(columns, dtype=jnp.float32), left_side=True, lower=True
    )
    basis_rows = basis_of(current, inverse_low)
    mapped, projected_term = gather_product(
        current,
        lambda total, last_pieces, vectors: mapped_and_projected(
            total, last_pieces, vectors, inverse_low, basis_rows
        ),
    )
    projected, residual = residual_of(mapped, basis_rows, all_terms(projected_term))
    return (basis_rows, projected, residual)


def solution(mesh):
    in_specs = (P(("bulk", "blk"), None), P(("bulk", "blk"), None), P("bulk"))
    out_specs = (P(("bulk", "blk"), None), P("bulk", None), P(("bulk", "blk"), None))
    return jax.shard_map(
        functools.partial(local, mesh.shape["blk"]),
        mesh=mesh,
        in_specs=in_specs,
        out_specs=out_specs,
        check_vma=False,
    )
```

```python
import functools

import jax
import jax.numpy as jnp
from jax import lax
from jax.experimental import pallas as pl
from jax.experimental.pallas import tpu as pltpu
from jax.sharding import PartitionSpec as P

DEGREE = 8
HIGHEST = lax.Precision.HIGHEST
WHOLE = pl.BlockSpec(memory_space=pltpu.VMEM)
SCALARS = pl.BlockSpec(memory_space=pltpu.SMEM)
VMEM_LIMIT = 16 * 2**20


def params():
    return pltpu.CompilerParams(vmem_limit_bytes=VMEM_LIMIT)


def high_low(values):
    high = values.astype(jnp.bfloat16)
    low = (values - high.astype(jnp.float32)).astype(jnp.bfloat16)
    return high, low


def split_factor(factor, bounds, n):
    rows, order = factor.shape
    width = order // (2 * n)
    count = 2 * n

    def kernel(bounds_ref, factor_ref, *refs):
        out_refs, coefficient_ref = refs[:count], refs[count]
        slots, arrived = refs[count + 1 :]
        me = lax.axis_index("blk")

        def fetch(at):
            owner = jnp.bitwise_xor(me, at // 2)
            start = pl.multiple_of((2 * owner + at % 2) * width, width)
            return pltpu.make_async_copy(
                factor_ref.at[:, pl.ds(start, width)], slots.at[at % 3], arrived.at[at % 3]
            )

        fetch(0).start()
        fetch(1).start()
        centre = (bounds_ref[0] + bounds_ref[1]) / 2.0
        radius = (bounds_ref[1] - bounds_ref[0]) / 2.0
        coefficient_ref[0:1, :] = jnp.full((1, 128), centre, jnp.float32)
        coefficient_ref[1:2, :] = 1.0 / jnp.full((1, 128), radius, jnp.float32)
        for at in range(count):
            if at + 2 < count:
                fetch(at + 2).start()
            fetch(at).wait()

            @pl.loop(0, rows // 64)
            def _(tile):
                own = pl.ds(pl.multiple_of(tile * 64, 64), 64)
                high, low = high_low(slots[at % 3, own, :])
                out_refs[at][own, :width] = high
                out_refs[at][own, width:] = low

    *pieces, coefficients = pl.pallas_call(
        kernel,
        out_shape=[jax.ShapeDtypeStruct((rows, 2 * width), jnp.bfloat16)] * count
        + [jax.ShapeDtypeStruct((2, 128), jnp.float32)],
        in_specs=[SCALARS, pl.BlockSpec(memory_space=pltpu.HBM)],
        out_specs=[WHOLE] * (count + 1),
        scratch_shapes=[pltpu.VMEM((3, rows, width), jnp.float32), pltpu.SemaphoreType.DMA((3,))],
        compiler_params=pltpu.CompilerParams(vmem_limit_bytes=28 * 2**20),
        cost_estimate=pl.CostEstimate(flops=0, bytes_accessed=4 * rows * order, transcendentals=0),
    )(bounds, factor)
    return [pieces[2 * offset : 2 * offset + 2] for offset in range(n)], coefficients


def stack_vectors(stacked_ref, at, vectors):
    width, columns = vectors.shape
    high, low = high_low(vectors)
    for start in (0, width):
        stacked_ref[at, start : start + width, :columns] = high
        stacked_ref[at, start : start + width, columns:] = low


def product_tile(pieces, stacked_ref, rows, columns):
    total = None
    for at, piece in enumerate(pieces):
        term = jnp.dot(piece[rows, :], stacked_ref[at], preferred_element_type=jnp.float32)
        total = term if total is None else total + term
    return total[:, :columns] + total[:, columns:]


def row_tiles(rows):
    tile = min(rows, 256)
    return [slice(start, start + tile) for start in range(0, rows, tile)]


def product_cost(pieces, rows):
    doubled = pieces[0].shape[1]
    return pl.CostEstimate(
        flops=2 * rows * doubled * 256 * len(pieces),
        bytes_accessed=2 * rows * doubled * len(pieces),
        transcendentals=0,
    )


def partial_product(total, pieces, vectors):
    n = len(pieces)
    rows, (width, columns) = pieces[0].shape[0], vectors[0].shape

    def kernel(*refs):
        piece_refs, vector_refs = refs[:n], refs[n : 2 * n]
        total_ref = refs[2 * n] if total is not None else None
        out_ref, stacked_ref = refs[-2:]
        for at in range(n):
            stack_vectors(stacked_ref, at, vector_refs[at][...])
        for tile in row_tiles(rows):
            value = product_tile(piece_refs, stacked_ref, tile, columns)
            out_ref[tile, :] = value if total_ref is None else total_ref[tile, :] + value

    operands = [*pieces, *vectors] + ([] if total is None else [total])
    return pl.pallas_call(
        kernel,
        out_shape=jax.ShapeDtypeStruct((rows, columns), jnp.float32),
        in_specs=[WHOLE] * len(operands),
        out_specs=WHOLE,
        scratch_shapes=[pltpu.VMEM((n, 2 * width, 2 * columns), jnp.bfloat16)],
        compiler_params=params(),
        cost_estimate=product_cost(pieces, rows),
    )(*operands)


def recurrence_step(coefficients, total, pieces, vectors, current, previous, at):
    n = len(pieces)
    half, (width, columns) = current[at].shape[0], vectors[0].shape

    def kernel(coefficient_ref, *refs):
        piece_refs, refs = refs[:n], refs[n:]
        vector_refs, refs = refs[:n], refs[n:]
        total_ref, refs = (refs[0], refs[1:]) if total is not None else (None, refs)
        current_ref, refs = refs[0], refs[1:]
        previous_ref, refs = (refs[0], refs[1:]) if previous else (None, refs)
        out_ref, stacked_ref = refs
        for term in range(n):
            stack_vectors(stacked_ref, term, vector_refs[term][...])
        centre, inverse_radius = coefficient_ref[0:1, :columns], coefficient_ref[1:2, :columns]
        for own in row_tiles(half):
            tile = slice(at * half + own.start, at * half + own.stop)
            value = product_tile(piece_refs, stacked_ref, tile, columns)
            if total_ref is not None:
                value = value + total_ref[tile, :]
            value = (value - centre * current_ref[own, :]) * inverse_radius
            if previous_ref is not None:
                value = 2.0 * value - previous_ref[own, :]
            out_ref[own, :] = value

    operands = [*pieces, *vectors] + ([] if total is None else [total])
    operands += [current[at]] + ([previous[at]] if previous else [])
    return pl.pallas_call(
        kernel,
        out_shape=jax.ShapeDtypeStruct((half, columns), jnp.float32),
        in_specs=[WHOLE] * (1 + len(operands)),
        out_specs=WHOLE,
        scratch_shapes=[pltpu.VMEM((n, 2 * width, 2 * columns), jnp.bfloat16)],
        compiler_params=params(),
        cost_estimate=product_cost(pieces, half),
    )(coefficients, *operands)


def dot_high(left_side, right_side, contract):
    return lax.dot_general(
        left_side, right_side, (contract, ((), ())), precision=HIGHEST, preferred_element_type=jnp.float32
    )


def tree_sum(values):
    while len(values) > 1:
        values = [values[at] + values[at + 1] for at in range(0, len(values), 2)]
    return values[0]


def gram_of(halves):
    def kernel(*refs):
        *in_refs, out_ref = refs
        total = None
        for ref in in_refs:
            term = dot_high(ref[...], ref[...], ((0,), (0,)))
            total = term if total is None else total + term
        out_ref[...] = total

    columns = halves[0].shape[1]
    return pl.pallas_call(
        kernel,
        out_shape=jax.ShapeDtypeStruct((columns, columns), jnp.float32),
        in_specs=[WHOLE] * len(halves),
        out_specs=WHOLE,
        compiler_params=params(),
    )(*halves)


def inverse_cholesky(terms):
    columns = terms[0].shape[0]
    high = 8

    def kernel(*refs):
        *term_refs, out_ref, gram_ref = refs
        gram_ref[...] = tree_sum([ref[...] for ref in term_refs])
        row_at = lax.broadcasted_iota(jnp.int32, (columns, columns), 0)
        column_at = lax.broadcasted_iota(jnp.int32, (columns, columns), 1)
        out_ref[...] = jnp.where(row_at == column_at, 1.0, 0.0)
        sub_row = lax.broadcasted_iota(jnp.int32, (high, columns), 0)
        for start in range(0, columns, high):
            stop = start + high
            own, inverse = gram_ref[start:stop, :], out_ref[start:stop, :]
            spread = [
                jnp.broadcast_to(own[:, start + at : start + at + 1], (high, columns)) for at in range(high)
            ]
            pivots = jnp.ones((high, columns), jnp.float32)
            for at in range(high):
                pivot = jnp.broadcast_to(spread[at][at : at + 1, :], (high, columns))
                pivots = jnp.where(sub_row == at, pivot, pivots)
                if at + 1 == high:
                    break
                factor = jnp.where(sub_row > at, spread[at] / pivot, 0.0)
                for later in range(at + 1, high):
                    spread[later] = spread[later] - factor * spread[later][at : at + 1, :]
                own = own - factor * own[at : at + 1, :]
                inverse = inverse - factor * inverse[at : at + 1, :]
            out_ref[start:stop, :] = inverse / jnp.sqrt(pivots)
            if stop < columns:
                both = jnp.concatenate([own, inverse], axis=1)
                update = dot_high(own / pivots, both, ((0,), (0,)))
                gram_ref[stop:, :] = gram_ref[stop:, :] - update[stop:, :columns]
                out_ref[stop:, :] = out_ref[stop:, :] - update[stop:, columns:]

    return pl.pallas_call(
        kernel,
        out_shape=jax.ShapeDtypeStruct((columns, columns), jnp.float32),
        in_specs=[WHOLE] * len(terms),
        out_specs=WHOLE,
        scratch_shapes=[pltpu.VMEM((columns, columns), jnp.float32)],
        compiler_params=params(),
        cost_estimate=pl.CostEstimate(flops=8 * 10**9, bytes_accessed=0, transcendentals=0),
    )(*terms)


def basis_of(halves, inverse_low):
    def kernel(inverse_ref, *refs):
        *in_refs, out_ref = refs
        at = 0
        for ref in in_refs:
            out_ref[at : at + ref.shape[0], :] = dot_high(ref[...], inverse_ref[...], ((1,), (1,)))
            at += ref.shape[0]

    rows, columns = sum(half.shape[0] for half in halves), halves[0].shape[1]
    return pl.pallas_call(
        kernel,
        out_shape=jax.ShapeDtypeStruct((rows, columns), jnp.float32),
        in_specs=[WHOLE] * (1 + len(halves)),
        out_specs=WHOLE,
        compiler_params=params(),
    )(inverse_low, *halves)


def mapped_and_projected(total, pieces, vectors, inverse_low, basis_rows):
    n = len(pieces)
    rows, (width, columns) = pieces[0].shape[0], vectors[0].shape

    def kernel(*refs):
        piece_refs, refs = refs[:n], refs[n:]
        vector_refs, refs = refs[:n], refs[n:]
        total_ref, refs = (refs[0], refs[1:]) if total is not None else (None, refs)
        inverse_ref, basis_ref, mapped_ref, projected_ref, stacked_ref = refs
        for at in range(n):
            stack_vectors(stacked_ref, at, vector_refs[at][...])
        projected = None
        for tile in row_tiles(rows):
            value = product_tile(piece_refs, stacked_ref, tile, columns)
            if total_ref is not None:
                value = value + total_ref[tile, :]
            mapped = dot_high(value, inverse_ref[...], ((1,), (1,)))
            mapped_ref[tile, :] = mapped
            term = dot_high(basis_ref[tile, :], mapped, ((0,), (0,)))
            projected = term if projected is None else projected + term
        projected_ref[...] = projected

    operands = [*pieces, *vectors] + ([] if total is None else [total]) + [inverse_low, basis_rows]
    return pl.pallas_call(
        kernel,
        out_shape=[
            jax.ShapeDtypeStruct((rows, columns), jnp.float32),
            jax.ShapeDtypeStruct((columns, columns), jnp.float32),
        ],
        in_specs=[WHOLE] * len(operands),
        out_specs=[WHOLE] * 2,
        scratch_shapes=[pltpu.VMEM((n, 2 * width, 2 * columns), jnp.bfloat16)],
        compiler_params=params(),
        cost_estimate=product_cost(pieces, rows),
    )(*operands)


def residual_of(mapped, basis_rows, terms):
    def kernel(mapped_ref, basis_ref, *refs):
        *term_refs, projected_ref, residual_ref = refs
        projected = tree_sum([ref[...] for ref in term_refs])
        projected_ref[...] = projected
        residual_ref[...] = mapped_ref[...] - dot_high(basis_ref[...], projected, ((1,), (0,)))

    return pl.pallas_call(
        kernel,
        out_shape=[
            jax.ShapeDtypeStruct(terms[0].shape, jnp.float32),
            jax.ShapeDtypeStruct(mapped.shape, jnp.float32),
        ],
        in_specs=[WHOLE] * (2 + len(terms)),
        out_specs=[WHOLE] * 2,
        compiler_params=params(),
    )(mapped, basis_rows, *terms)


def exchange(value, offset, n):
    return lax.ppermute(value, "blk", [(at, at ^ offset) for at in range(n)])


def local(n, factor, initial, bounds):
    rows, columns = initial.shape
    half = rows // 2
    halves_at = range(2)
    pieces, coefficients = split_factor(factor, bounds, n)

    if n == 4:

        def gather_product(halves):
            top, bottom = halves
            x_top, y_bottom = exchange(top, 1, n), exchange(bottom, 2, n)
            x_bottom, y_top = exchange(bottom, 1, n), exchange(top, 2, n)
            total = partial_product(None, pieces[0], [top, bottom])
            xy_top, xy_bottom = exchange(x_top, 2, n), exchange(y_bottom, 1, n)
            total = partial_product(total, [pieces[1][0], pieces[2][1]], [x_top, y_bottom])
            total = partial_product(total, [pieces[1][1], pieces[2][0]], [x_bottom, y_top])
            return total, pieces[3], [xy_top, xy_bottom]

        def all_terms(term):
            return [term] + [exchange(term, offset, n) for offset in (1, 2, 3)]
    else:

        def by_offset(value):
            gathered = lax.all_gather(value, "blk")
            me = lax.axis_index("blk")
            return [gathered[jnp.bitwise_xor(me, offset)] for offset in range(n)]

        def gather_product(halves):
            vectors = [block[at * half : (at + 1) * half] for block in by_offset(jnp.concatenate(halves)) for at in halves_at]
            return None, [piece for pair in pieces for piece in pair], vectors

        all_terms = by_offset

    previous, current = None, [initial[:half], initial[half:]]
    for order_step in range(DEGREE):
        product = gather_product(current)
        following = [recurrence_step(coefficients, *product, current, previous, at) for at in halves_at]
        previous, current = current, following

    inverse_low = inverse_cholesky(all_terms(gram_of(current)))
    basis_rows = basis_of(current, inverse_low)
    mapped, projected_term = mapped_and_projected(*gather_product(current), inverse_low, basis_rows)
    projected, residual = residual_of(mapped, basis_rows, all_terms(projected_term))
    return (basis_rows, projected, residual)


def solution(mesh):
    in_specs = (P(("bulk", "blk"), None), P(("bulk", "blk"), None), P("bulk"))
    out_specs = (P(("bulk", "blk"), None), P("bulk", None), P(("bulk", "blk"), None))
    return jax.shard_map(
        functools.partial(local, mesh.shape["blk"]),
        mesh=mesh,
        in_specs=in_specs,
        out_specs=out_specs,
        check_vma=False,
    )
```

```python
import functools

import jax
import jax.numpy as jnp
from jax import lax
from jax.experimental import pallas as pl
from jax.experimental.pallas import tpu as pltpu
from jax.sharding import PartitionSpec as P

DEGREE = 8
HIGHEST = lax.Precision.HIGHEST
WHOLE = pl.BlockSpec(memory_space=pltpu.VMEM)
HBM = pl.BlockSpec(memory_space=pltpu.HBM)
SCALARS = pl.BlockSpec(memory_space=pltpu.SMEM)
VMEM_LIMIT = 16 * 2**20


def params():
    return pltpu.CompilerParams(vmem_limit_bytes=VMEM_LIMIT)


def high_low(values):
    high = values.astype(jnp.bfloat16)
    low = (values - high.astype(jnp.float32)).astype(jnp.bfloat16)
    return high, low


def splitter(factor_ref, slots, arrived, count, emit):
    rows, width = slots.shape[1:]
    me = lax.axis_index("blk")

    def fetch(at):
        owner = jnp.bitwise_xor(me, at // 2)
        start = pl.multiple_of((2 * owner + at % 2) * width, width)
        return pltpu.make_async_copy(factor_ref.at[:, pl.ds(start, width)], slots.at[at % 3], arrived.at[at % 3])

    fetch(0).start()
    fetch(1).start()
    for at in range(count):
        if at + 2 < count:
            fetch(at + 2).start()
        fetch(at).wait()

        @pl.loop(0, rows // 64)
        def _(tile):
            own = pl.ds(pl.multiple_of(tile * 64, 64), 64)
            emit(at, own, *high_low(slots[at % 3, own, :]))

        yield at


def starts_late():
    return lax.rem(lax.axis_index("bulk"), 2) == 1


def first_vectors(factor, initial, n):
    (rows, order), columns = factor.shape, initial.shape[1]
    width, count, half = order // (2 * n), 2 * n, rows // 2

    def kernel(initial_ref, factor_ref, top_ref, bottom_ref, *refs):
        piece_refs = refs[:count]
        slots, arrived, split, sent, loaded = refs[count:]
        loads = [
            pltpu.make_async_copy(initial_ref.at[pl.ds(at * half, half), :], ref, loaded.at[at])
            for at, ref in enumerate((top_ref, bottom_ref))
        ]
        for load in loads:
            load.start()

        @pl.when(starts_late())
        def _():
            def store(at):
                return pltpu.make_async_copy(split.at[at % 2], piece_refs[at], sent.at[at % 2])

            def emit(at, own, high, low):
                split[at % 2, own, :width] = high
                split[at % 2, own, width:] = low

            for at in splitter(factor_ref, slots, arrived, count, emit):
                store(at).start()
                if at >= 1:
                    store(at - 1).wait()
            store(count - 1).wait()

        for load in loads:
            load.wait()

    top, bottom, *pieces = pl.pallas_call(
        kernel,
        out_shape=[jax.ShapeDtypeStruct((half, columns), jnp.float32)] * 2
        + [jax.ShapeDtypeStruct((rows, 2 * width), jnp.bfloat16)] * count,
        in_specs=[HBM] * 2,
        out_specs=[WHOLE] * 2 + [HBM] * count,
        scratch_shapes=[
            pltpu.VMEM((3, rows, width), jnp.float32),
            pltpu.SemaphoreType.DMA((3,)),
            pltpu.VMEM((2, rows, 2 * width), jnp.bfloat16),
            pltpu.SemaphoreType.DMA((2,)),
            pltpu.SemaphoreType.DMA((2,)),
        ],
        compiler_params=params(),
    )(initial, factor)
    return [top, bottom], pieces


def split_factor(factor, bounds, early, n):
    rows, order = factor.shape
    width, count = order // (2 * n), 2 * n

    def kernel(bounds_ref, factor_ref, *refs):
        early_refs, refs = refs[:count], refs[count:]
        out_refs, coefficient_ref = refs[:count], refs[count]
        slots, arrived, loaded = refs[count + 1 :]
        centre = (bounds_ref[0] + bounds_ref[1]) / 2.0
        radius = (bounds_ref[1] - bounds_ref[0]) / 2.0
        coefficient_ref[0:1, :] = jnp.full((1, 128), centre, jnp.float32)
        coefficient_ref[1:2, :] = 1.0 / jnp.full((1, 128), radius, jnp.float32)

        @pl.when(starts_late())
        def _():
            loads = [
                pltpu.make_async_copy(early_refs[at], out_refs[at], loaded.at[at]) for at in range(count)
            ]
            for load in loads:
                load.start()
            for load in loads:
                load.wait()

        @pl.when(jnp.logical_not(starts_late()))
        def _():
            def emit(at, own, high, low):
                out_refs[at][own, :width] = high
                out_refs[at][own, width:] = low

            for _ in splitter(factor_ref, slots, arrived, count, emit):
                pass

    *pieces, coefficients = pl.pallas_call(
        kernel,
        out_shape=[jax.ShapeDtypeStruct((rows, 2 * width), jnp.bfloat16)] * count
        + [jax.ShapeDtypeStruct((2, 128), jnp.float32)],
        in_specs=[SCALARS] + [HBM] * (1 + count),
        out_specs=[WHOLE] * (count + 1),
        scratch_shapes=[
            pltpu.VMEM((3, rows, width), jnp.float32),
            pltpu.SemaphoreType.DMA((3,)),
            pltpu.SemaphoreType.DMA((count,)),
        ],
        compiler_params=pltpu.CompilerParams(vmem_limit_bytes=28 * 2**20),
        cost_estimate=pl.CostEstimate(flops=0, bytes_accessed=4 * rows * order, transcendentals=0),
    )(bounds, factor, *early)
    return [pieces[2 * offset : 2 * offset + 2] for offset in range(n)], coefficients


def stack_vectors(stacked_ref, at, vectors):
    width, columns = vectors.shape
    high, low = high_low(vectors)
    for start in (0, width):
        stacked_ref[at, start : start + width, :columns] = high
        stacked_ref[at, start : start + width, columns:] = low


def product_tile(pieces, stacked_ref, rows, columns):
    total = None
    for at, piece in enumerate(pieces):
        term = jnp.dot(piece[rows, :], stacked_ref[at], preferred_element_type=jnp.float32)
        total = term if total is None else total + term
    return total[:, :columns] + total[:, columns:]


def row_tiles(rows):
    tile = min(rows, 256)
    return [slice(start, start + tile) for start in range(0, rows, tile)]


def product_cost(pieces, rows):
    doubled = pieces[0].shape[1]
    return pl.CostEstimate(
        flops=2 * rows * doubled * 256 * len(pieces),
        bytes_accessed=2 * rows * doubled * len(pieces),
        transcendentals=0,
    )


def partial_product(total, pieces, vectors):
    n = len(pieces)
    rows, (width, columns) = pieces[0].shape[0], vectors[0].shape

    def kernel(*refs):
        piece_refs, vector_refs = refs[:n], refs[n : 2 * n]
        total_ref = refs[2 * n] if total is not None else None
        out_ref, stacked_ref = refs[-2:]
        for at in range(n):
            stack_vectors(stacked_ref, at, vector_refs[at][...])
        for tile in row_tiles(rows):
            value = product_tile(piece_refs, stacked_ref, tile, columns)
            out_ref[tile, :] = value if total_ref is None else total_ref[tile, :] + value

    operands = [*pieces, *vectors] + ([] if total is None else [total])
    return pl.pallas_call(
        kernel,
        out_shape=jax.ShapeDtypeStruct((rows, columns), jnp.float32),
        in_specs=[WHOLE] * len(operands),
        out_specs=WHOLE,
        scratch_shapes=[pltpu.VMEM((n, 2 * width, 2 * columns), jnp.bfloat16)],
        compiler_params=params(),
        cost_estimate=product_cost(pieces, rows),
    )(*operands)


def recurrence_step(coefficients, total, pieces, vectors, current, previous, at):
    n = len(pieces)
    half, (width, columns) = current[at].shape[0], vectors[0].shape

    def kernel(coefficient_ref, *refs):
        piece_refs, refs = refs[:n], refs[n:]
        vector_refs, refs = refs[:n], refs[n:]
        total_ref, refs = (refs[0], refs[1:]) if total is not None else (None, refs)
        current_ref, refs = refs[0], refs[1:]
        previous_ref, refs = (refs[0], refs[1:]) if previous else (None, refs)
        out_ref, stacked_ref = refs
        for term in range(n):
            stack_vectors(stacked_ref, term, vector_refs[term][...])
        centre, inverse_radius = coefficient_ref[0:1, :columns], coefficient_ref[1:2, :columns]
        for own in row_tiles(half):
            tile = slice(at * half + own.start, at * half + own.stop)
            value = product_tile(piece_refs, stacked_ref, tile, columns)
            if total_ref is not None:
                value = value + total_ref[tile, :]
            value = (value - centre * current_ref[own, :]) * inverse_radius
            if previous_ref is not None:
                value = 2.0 * value - previous_ref[own, :]
            out_ref[own, :] = value

    operands = [*pieces, *vectors] + ([] if total is None else [total])
    operands += [current[at]] + ([previous[at]] if previous else [])
    return pl.pallas_call(
        kernel,
        out_shape=jax.ShapeDtypeStruct((half, columns), jnp.float32),
        in_specs=[WHOLE] * (1 + len(operands)),
        out_specs=WHOLE,
        scratch_shapes=[pltpu.VMEM((n, 2 * width, 2 * columns), jnp.bfloat16)],
        compiler_params=params(),
        cost_estimate=product_cost(pieces, half),
    )(coefficients, *operands)


def dot_high(left_side, right_side, contract):
    return lax.dot_general(
        left_side, right_side, (contract, ((), ())), precision=HIGHEST, preferred_element_type=jnp.float32
    )


def tree_sum(values):
    while len(values) > 1:
        values = [values[at] + values[at + 1] for at in range(0, len(values), 2)]
    return values[0]


def gram_of(halves):
    def kernel(*refs):
        *in_refs, out_ref = refs
        total = None
        for ref in in_refs:
            term = dot_high(ref[...], ref[...], ((0,), (0,)))
            total = term if total is None else total + term
        out_ref[...] = total

    columns = halves[0].shape[1]
    return pl.pallas_call(
        kernel,
        out_shape=jax.ShapeDtypeStruct((columns, columns), jnp.float32),
        in_specs=[WHOLE] * len(halves),
        out_specs=WHOLE,
        compiler_params=params(),
    )(*halves)


def inverse_cholesky(terms):
    columns = terms[0].shape[0]
    high = 8

    def kernel(*refs):
        *term_refs, out_ref, gram_ref, inverse_ref = refs
        gram_ref[...] = tree_sum([ref[...] for ref in term_refs])
        row_at = lax.broadcasted_iota(jnp.int32, (columns, columns), 0)
        column_at = lax.broadcasted_iota(jnp.int32, (columns, columns), 1)
        inverse_ref[...] = jnp.where(row_at == column_at, 1.0, 0.0)
        sub_row = lax.broadcasted_iota(jnp.int32, (high, columns), 0)
        for start in range(0, columns, high):
            stop = start + high
            own, inverse = gram_ref[start:stop, :], inverse_ref[start:stop, :]
            spread = [
                jnp.broadcast_to(own[:, start + at : start + at + 1], (high, columns)) for at in range(high)
            ]
            pivots = jnp.ones((high, columns), jnp.float32)
            for at in range(high):
                pivot = jnp.broadcast_to(spread[at][at : at + 1, :], (high, columns))
                pivots = jnp.where(sub_row == at, pivot, pivots)
                if at + 1 == high:
                    break
                factor = jnp.where(sub_row > at, spread[at] / pivot, 0.0)
                for later in range(at + 1, high):
                    spread[later] = spread[later] - factor * spread[later][at : at + 1, :]
                own = own - factor * own[at : at + 1, :]
                inverse = inverse - factor * inverse[at : at + 1, :]
            inverse_ref[start:stop, :] = inverse / jnp.sqrt(pivots)
            if stop < columns:
                both = jnp.concatenate([own, inverse], axis=1)
                update = dot_high(own / pivots, both, ((0,), (0,)))
                gram_ref[stop:, :] = gram_ref[stop:, :] - update[stop:, :columns]
                inverse_ref[stop:, :] = inverse_ref[stop:, :] - update[stop:, columns:]
        out_ref[...] = inverse_ref[...].T

    return pl.pallas_call(
        kernel,
        out_shape=jax.ShapeDtypeStruct((columns, columns), jnp.float32),
        in_specs=[WHOLE] * len(terms),
        out_specs=WHOLE,
        scratch_shapes=[pltpu.VMEM((columns, columns), jnp.float32)] * 2,
        compiler_params=params(),
        cost_estimate=pl.CostEstimate(flops=8 * 10**9, bytes_accessed=0, transcendentals=0),
    )(*terms)


def two_parts(values):
    return jnp.concatenate(high_low(values), axis=1)


def dot_parts(left_side, right_side):
    columns = right_side.shape[1]
    right_parts = two_parts(right_side)
    product = jnp.dot(
        two_parts(left_side),
        jnp.concatenate([right_parts, right_parts], axis=0),
        preferred_element_type=jnp.float32,
    )
    return product[:, :columns] + product[:, columns:]


def dot_rows(left_side, right_side):
    left_columns, columns = left_side.shape[1], right_side.shape[1]
    product = lax.dot_general(
        two_parts(left_side),
        two_parts(right_side),
        (((0,), (0,)), ((), ())),
        preferred_element_type=jnp.float32,
    )
    product = product[:left_columns, :] + product[left_columns:, :]
    return product[:, :columns] + product[:, columns:]


def times_right(halves, right_side):
    def kernel(right_ref, *refs):
        *in_refs, out_ref = refs
        at = 0
        for ref in in_refs:
            for tile in row_tiles(ref.shape[0]):
                out_ref[at + tile.start : at + tile.stop, :] = dot_parts(ref[tile, :], right_ref[...])
            at += ref.shape[0]

    rows, columns = sum(half.shape[0] for half in halves), halves[0].shape[1]
    return pl.pallas_call(
        kernel,
        out_shape=jax.ShapeDtypeStruct((rows, columns), jnp.float32),
        in_specs=[WHOLE] * (1 + len(halves)),
        out_specs=WHOLE,
        compiler_params=params(),
        cost_estimate=pl.CostEstimate(flops=2 * rows * 256 * 256, bytes_accessed=0, transcendentals=0),
    )(right_side, *halves)


def image_and_projected(total, pieces, vectors, inverse_upper, basis_rows):
    n = len(pieces)
    rows, (width, columns) = pieces[0].shape[0], vectors[0].shape

    def kernel(*refs):
        piece_refs, refs = refs[:n], refs[n:]
        vector_refs, refs = refs[:n], refs[n:]
        total_ref, refs = (refs[0], refs[1:]) if total is not None else (None, refs)
        inverse_ref, basis_ref, image_ref, projected_ref, stacked_ref = refs
        for at in range(n):
            stack_vectors(stacked_ref, at, vector_refs[at][...])
        projected = None
        for tile in row_tiles(rows):
            image = product_tile(piece_refs, stacked_ref, tile, columns)
            if total_ref is not None:
                image = image + total_ref[tile, :]
            image_ref[tile, :] = image
            term = dot_rows(basis_ref[tile, :], image)
            projected = term if projected is None else projected + term
        projected_ref[...] = dot_parts(projected, inverse_ref[...])

    operands = [*pieces, *vectors] + ([] if total is None else [total]) + [inverse_upper, basis_rows]
    return pl.pallas_call(
        kernel,
        out_shape=[
            jax.ShapeDtypeStruct((rows, columns), jnp.float32),
            jax.ShapeDtypeStruct((columns, columns), jnp.float32),
        ],
        in_specs=[WHOLE] * len(operands),
        out_specs=[WHOLE] * 2,
        scratch_shapes=[pltpu.VMEM((n, 2 * width, 2 * columns), jnp.bfloat16)],
        compiler_params=params(),
        cost_estimate=product_cost(pieces, rows),
    )(*operands)


def residual_of(mapped, basis_rows, terms):
    def kernel(mapped_ref, basis_ref, *refs):
        *term_refs, projected_ref, residual_ref = refs
        projected = tree_sum([ref[...] for ref in term_refs])
        projected_ref[...] = projected
        for tile in row_tiles(mapped.shape[0]):
            residual_ref[tile, :] = mapped_ref[tile, :] - dot_parts(basis_ref[tile, :], projected)

    return pl.pallas_call(
        kernel,
        out_shape=[
            jax.ShapeDtypeStruct(terms[0].shape, jnp.float32),
            jax.ShapeDtypeStruct(mapped.shape, jnp.float32),
        ],
        in_specs=[WHOLE] * (2 + len(terms)),
        out_specs=[WHOLE] * 2,
        compiler_params=params(),
    )(mapped, basis_rows, *terms)


def exchange(value, offset, n):
    return lax.ppermute(value, "blk", [(at, at ^ offset) for at in range(n)])


def local(n, factor, initial, bounds):
    rows, columns = initial.shape
    half = rows // 2
    halves_at = range(2)
    first, early = first_vectors(factor, initial, n)
    pieces, coefficients = split_factor(factor, bounds, early, n)

    if n == 4:

        def gather_product(halves):
            top, bottom = halves
            x_top, y_bottom = exchange(top, 1, n), exchange(bottom, 2, n)
            x_bottom, y_top = exchange(bottom, 1, n), exchange(top, 2, n)
            total = partial_product(None, pieces[0], [top, bottom])
            xy_top, xy_bottom = exchange(x_top, 2, n), exchange(y_bottom, 1, n)
            total = partial_product(total, [pieces[1][0], pieces[2][1]], [x_top, y_bottom])
            total = partial_product(total, [pieces[1][1], pieces[2][0]], [x_bottom, y_top])
            return total, pieces[3], [xy_top, xy_bottom]

        def all_terms(term):
            return [term] + [exchange(term, offset, n) for offset in (1, 2, 3)]
    else:

        def by_offset(value):
            gathered = lax.all_gather(value, "blk")
            me = lax.axis_index("blk")
            return [gathered[jnp.bitwise_xor(me, offset)] for offset in range(n)]

        def gather_product(halves):
            vectors = [block[at * half : (at + 1) * half] for block in by_offset(jnp.concatenate(halves)) for at in halves_at]
            return None, [piece for pair in pieces for piece in pair], vectors

        all_terms = by_offset

    previous, current = None, first
    for order_step in range(DEGREE):
        product = gather_product(current)
        following = [recurrence_step(coefficients, *product, current, previous, at) for at in halves_at]
        previous, current = current, following

    inverse_upper = inverse_cholesky(all_terms(gram_of(current)))
    basis_rows = times_right(current, inverse_upper)
    image, projected_term = image_and_projected(*gather_product(current), inverse_upper, basis_rows)
    projected_terms = all_terms(projected_term)
    mapped = times_right([image], inverse_upper)
    projected, residual = residual_of(mapped, basis_rows, projected_terms)
    return (basis_rows, projected, residual)


def solution(mesh):
    in_specs = (P(("bulk", "blk"), None), P(("bulk", "blk"), None), P("bulk"))
    out_specs = (P(("bulk", "blk"), None), P("bulk", None), P(("bulk", "blk"), None))
    return jax.shard_map(
        functools.partial(local, mesh.shape["blk"]),
        mesh=mesh,
        in_specs=in_specs,
        out_specs=out_specs,
        check_vma=False,
    )
```

```python
import functools

import jax
import jax.numpy as jnp
from jax import lax
from jax.experimental import pallas as pl
from jax.experimental.pallas import tpu as pltpu
from jax.sharding import PartitionSpec as P

DEGREE = 8
HIGHEST = lax.Precision.HIGHEST
WHOLE = pl.BlockSpec(memory_space=pltpu.VMEM)
HBM = pl.BlockSpec(memory_space=pltpu.HBM)
SCALARS = pl.BlockSpec(memory_space=pltpu.SMEM)
VMEM_LIMIT = 16 * 2**20


def params():
    return pltpu.CompilerParams(vmem_limit_bytes=VMEM_LIMIT)


def high_low(values):
    high = values.astype(jnp.bfloat16)
    low = (values - high.astype(jnp.float32)).astype(jnp.bfloat16)
    return high, low


def splitter(factor_ref, slots, arrived, count, emit):
    rows, width = slots.shape[1:]
    me = lax.axis_index("blk")

    def fetch(at):
        owner = jnp.bitwise_xor(me, at // 2)
        start = pl.multiple_of((2 * owner + at % 2) * width, width)
        return pltpu.make_async_copy(factor_ref.at[:, pl.ds(start, width)], slots.at[at % 3], arrived.at[at % 3])

    fetch(0).start()
    fetch(1).start()
    for at in range(count):
        if at + 2 < count:
            fetch(at + 2).start()
        fetch(at).wait()

        @pl.loop(0, rows // 64)
        def _(tile):
            own = pl.ds(pl.multiple_of(tile * 64, 64), 64)
            emit(at, own, *high_low(slots[at % 3, own, :]))

        yield at


def starts_late():
    return lax.rem(lax.axis_index("bulk"), 2) == 1


def first_vectors(factor, initial, n):
    (rows, order), columns = factor.shape, initial.shape[1]
    width, count, half = order // (2 * n), 2 * n, rows // 2

    def kernel(initial_ref, factor_ref, top_ref, bottom_ref, piece_ref, slots, arrived, split, sent, loaded):
        loads = [
            pltpu.make_async_copy(initial_ref.at[pl.ds(at * half, half), :], ref, loaded.at[at])
            for at, ref in enumerate((top_ref, bottom_ref))
        ]
        for load in loads:
            load.start()

        @pl.when(starts_late())
        def _():
            def store(at):
                return pltpu.make_async_copy(split.at[at % 2], piece_ref.at[at], sent.at[at % 2])

            def emit(at, own, high, low):
                split[at % 2, own, :width] = high
                split[at % 2, own, width:] = low

            for at in splitter(factor_ref, slots, arrived, count, emit):
                store(at).start()
                if at >= 1:
                    store(at - 1).wait()
            store(count - 1).wait()

        for load in loads:
            load.wait()

    top, bottom, pieces = pl.pallas_call(
        kernel,
        out_shape=[jax.ShapeDtypeStruct((half, columns), jnp.float32)] * 2
        + [jax.ShapeDtypeStruct((count, rows, 2 * width), jnp.bfloat16)],
        in_specs=[HBM] * 2,
        out_specs=[WHOLE] * 2 + [HBM],
        scratch_shapes=[
            pltpu.VMEM((3, rows, width), jnp.float32),
            pltpu.SemaphoreType.DMA((3,)),
            pltpu.VMEM((2, rows, 2 * width), jnp.bfloat16),
            pltpu.SemaphoreType.DMA((2,)),
            pltpu.SemaphoreType.DMA((2,)),
        ],
        compiler_params=pltpu.CompilerParams(vmem_limit_bytes=56 * 2**20),
    )(initial, factor)
    return [top, bottom], pieces


def split_factor(factor, bounds, early, n):
    rows, order = factor.shape
    width, count = order // (2 * n), 2 * n

    def kernel(bounds_ref, factor_ref, early_ref, *refs):
        out_refs, coefficient_ref = refs[:count], refs[count]
        slots, arrived, loaded = refs[count + 1 :]
        centre = (bounds_ref[0] + bounds_ref[1]) / 2.0
        radius = (bounds_ref[1] - bounds_ref[0]) / 2.0
        coefficient_ref[0:1, :] = jnp.full((1, 128), centre, jnp.float32)
        coefficient_ref[1:2, :] = 1.0 / jnp.full((1, 128), radius, jnp.float32)

        @pl.when(starts_late())
        def _():
            loads = [
                pltpu.make_async_copy(early_ref.at[at], out_refs[at], loaded.at[at]) for at in range(count)
            ]
            for load in loads:
                load.start()
            for load in loads:
                load.wait()

        @pl.when(jnp.logical_not(starts_late()))
        def _():
            def emit(at, own, high, low):
                out_refs[at][own, :width] = high
                out_refs[at][own, width:] = low

            for _ in splitter(factor_ref, slots, arrived, count, emit):
                pass

    *pieces, coefficients = pl.pallas_call(
        kernel,
        out_shape=[jax.ShapeDtypeStruct((rows, 2 * width), jnp.bfloat16)] * count
        + [jax.ShapeDtypeStruct((2, 128), jnp.float32)],
        in_specs=[SCALARS] + [HBM] * 2,
        out_specs=[WHOLE] * (count + 1),
        scratch_shapes=[
            pltpu.VMEM((3, rows, width), jnp.float32),
            pltpu.SemaphoreType.DMA((3,)),
            pltpu.SemaphoreType.DMA((count,)),
        ],
        compiler_params=pltpu.CompilerParams(vmem_limit_bytes=28 * 2**20),
        cost_estimate=pl.CostEstimate(flops=0, bytes_accessed=4 * rows * order, transcendentals=0),
    )(bounds, factor, early)
    return [pieces[2 * offset : 2 * offset + 2] for offset in range(n)], coefficients


def stack_vectors(stacked_ref, at, vectors):
    width, columns = vectors.shape
    high, low = high_low(vectors)
    for start in (0, width):
        stacked_ref[at, start : start + width, :columns] = high
        stacked_ref[at, start : start + width, columns:] = low


def product_tile(pieces, stacked_ref, rows, columns):
    total = None
    for at, piece in enumerate(pieces):
        term = jnp.dot(piece[rows, :], stacked_ref[at], preferred_element_type=jnp.float32)
        total = term if total is None else total + term
    return total[:, :columns] + total[:, columns:]


def row_tiles(rows):
    tile = min(rows, 256)
    return [slice(start, start + tile) for start in range(0, rows, tile)]


def product_cost(pieces, rows):
    doubled = pieces[0].shape[1]
    return pl.CostEstimate(
        flops=2 * rows * doubled * 256 * len(pieces),
        bytes_accessed=2 * rows * doubled * len(pieces),
        transcendentals=0,
    )


def partial_product(total, pieces, vectors):
    n = len(pieces)
    rows, (width, columns) = pieces[0].shape[0], vectors[0].shape

    def kernel(*refs):
        piece_refs, vector_refs = refs[:n], refs[n : 2 * n]
        total_ref = refs[2 * n] if total is not None else None
        out_ref, stacked_ref = refs[-2:]
        for at in range(n):
            stack_vectors(stacked_ref, at, vector_refs[at][...])
        for tile in row_tiles(rows):
            value = product_tile(piece_refs, stacked_ref, tile, columns)
            out_ref[tile, :] = value if total_ref is None else total_ref[tile, :] + value

    operands = [*pieces, *vectors] + ([] if total is None else [total])
    return pl.pallas_call(
        kernel,
        out_shape=jax.ShapeDtypeStruct((rows, columns), jnp.float32),
        in_specs=[WHOLE] * len(operands),
        out_specs=WHOLE,
        scratch_shapes=[pltpu.VMEM((n, 2 * width, 2 * columns), jnp.bfloat16)],
        compiler_params=params(),
        cost_estimate=product_cost(pieces, rows),
    )(*operands)


def recurrence_step(coefficients, total, pieces, vectors, current, previous, at):
    n = len(pieces)
    half, (width, columns) = current[at].shape[0], vectors[0].shape

    def kernel(coefficient_ref, *refs):
        piece_refs, refs = refs[:n], refs[n:]
        vector_refs, refs = refs[:n], refs[n:]
        total_ref, refs = (refs[0], refs[1:]) if total is not None else (None, refs)
        current_ref, refs = refs[0], refs[1:]
        previous_ref, refs = (refs[0], refs[1:]) if previous else (None, refs)
        out_ref, stacked_ref = refs
        for term in range(n):
            stack_vectors(stacked_ref, term, vector_refs[term][...])
        centre, inverse_radius = coefficient_ref[0:1, :columns], coefficient_ref[1:2, :columns]
        for own in row_tiles(half):
            tile = slice(at * half + own.start, at * half + own.stop)
            value = product_tile(piece_refs, stacked_ref, tile, columns)
            if total_ref is not None:
                value = value + total_ref[tile, :]
            value = (value - centre * current_ref[own, :]) * inverse_radius
            if previous_ref is not None:
                value = 2.0 * value - previous_ref[own, :]
            out_ref[own, :] = value

    operands = [*pieces, *vectors] + ([] if total is None else [total])
    operands += [current[at]] + ([previous[at]] if previous else [])
    return pl.pallas_call(
        kernel,
        out_shape=jax.ShapeDtypeStruct((half, columns), jnp.float32),
        in_specs=[WHOLE] * (1 + len(operands)),
        out_specs=WHOLE,
        scratch_shapes=[pltpu.VMEM((n, 2 * width, 2 * columns), jnp.bfloat16)],
        compiler_params=params(),
        cost_estimate=product_cost(pieces, half),
    )(coefficients, *operands)


def dot_high(left_side, right_side, contract):
    return lax.dot_general(
        left_side, right_side, (contract, ((), ())), precision=HIGHEST, preferred_element_type=jnp.float32
    )


def tree_sum(values):
    while len(values) > 1:
        values = [values[at] + values[at + 1] for at in range(0, len(values), 2)]
    return values[0]


def gram_of(halves):
    def kernel(*refs):
        *in_refs, out_ref = refs
        total = None
        for ref in in_refs:
            term = dot_high(ref[...], ref[...], ((0,), (0,)))
            total = term if total is None else total + term
        out_ref[...] = total

    columns = halves[0].shape[1]
    return pl.pallas_call(
        kernel,
        out_shape=jax.ShapeDtypeStruct((columns, columns), jnp.float32),
        in_specs=[WHOLE] * len(halves),
        out_specs=WHOLE,
        compiler_params=params(),
    )(*halves)


def three_parts(values):
    high = values.astype(jnp.bfloat16)
    return (high, *high_low(values - high.astype(jnp.float32)))


def dot_thin(left_side, right_side):
    a, b = three_parts(left_side), three_parts(right_side)
    pairs = [(a[0], b[0]), (a[0], b[1]), (a[1], b[0]), (a[1], b[1]), (a[0], b[2]), (a[2], b[0])]
    return lax.dot_general(
        jnp.concatenate([pair[0].astype(jnp.float32) for pair in pairs], axis=0).T.astype(jnp.bfloat16),
        jnp.concatenate([pair[1].astype(jnp.float32) for pair in pairs], axis=0).astype(jnp.bfloat16),
        (((1,), (0,)), ((), ())),
        preferred_element_type=jnp.float32,
    )


def inverse_cholesky(terms):
    columns = terms[0].shape[0]
    high = 8

    def kernel(*refs):
        *term_refs, out_ref, gram_ref, inverse_ref = refs
        gram_ref[...] = tree_sum([ref[...] for ref in term_refs])
        row_at = lax.broadcasted_iota(jnp.int32, (columns, columns), 0)
        column_at = lax.broadcasted_iota(jnp.int32, (columns, columns), 1)
        inverse_ref[...] = jnp.where(row_at == column_at, 1.0, 0.0)
        sub_row = lax.broadcasted_iota(jnp.int32, (high, columns), 0)
        for start in range(0, columns, high):
            stop = start + high
            own, inverse = gram_ref[start:stop, :], inverse_ref[start:stop, :]
            spread = [
                jnp.broadcast_to(own[:, start + at : start + at + 1], (high, columns)) for at in range(high)
            ]
            pivots = jnp.ones((high, columns), jnp.float32)
            reciprocals = jnp.ones((high, columns), jnp.float32)
            for at in range(high):
                pivot = jnp.broadcast_to(spread[at][at : at + 1, :], (high, columns))
                reciprocal = 1.0 / pivot
                pivots = jnp.where(sub_row == at, pivot, pivots)
                reciprocals = jnp.where(sub_row == at, reciprocal, reciprocals)
                if at + 1 == high:
                    break
                factor = jnp.where(sub_row > at, spread[at], 0.0) * reciprocal
                for later in range(at + 1, high):
                    spread[later] = spread[later] - factor * spread[later][at : at + 1, :]
                own = own - factor * own[at : at + 1, :]
                inverse = inverse - factor * inverse[at : at + 1, :]
            inverse_ref[start:stop, :] = inverse / jnp.sqrt(pivots)
            if stop < columns:
                update = dot_thin(own * reciprocals, jnp.concatenate([own, inverse], axis=1))
                gram_ref[stop:, :] = gram_ref[stop:, :] - update[stop:, :columns]
                inverse_ref[stop:, :] = inverse_ref[stop:, :] - update[stop:, columns:]
        out_ref[...] = inverse_ref[...].T

    return pl.pallas_call(
        kernel,
        out_shape=jax.ShapeDtypeStruct((columns, columns), jnp.float32),
        in_specs=[WHOLE] * len(terms),
        out_specs=WHOLE,
        scratch_shapes=[pltpu.VMEM((columns, columns), jnp.float32)] * 2,
        compiler_params=params(),
        cost_estimate=pl.CostEstimate(flops=8 * 10**9, bytes_accessed=0, transcendentals=0),
    )(*terms)


def two_parts(values):
    return jnp.concatenate(high_low(values), axis=1)


def dot_parts(left_side, right_side):
    columns = right_side.shape[1]
    right_parts = two_parts(right_side)
    product = jnp.dot(
        two_parts(left_side),
        jnp.concatenate([right_parts, right_parts], axis=0),
        preferred_element_type=jnp.float32,
    )
    return product[:, :columns] + product[:, columns:]


def times_right(halves, right_side, transposed=False):
    def kernel(right_ref, *refs):
        in_refs, (out_ref, *parts_ref) = refs[: len(halves)], refs[len(halves) :]
        at = 0
        for ref in in_refs:
            for tile in row_tiles(ref.shape[0]):
                own = slice(at + tile.start, at + tile.stop)
                value = dot_parts(ref[tile, :], right_ref[...])
                out_ref[own, :] = value
                if transposed:
                    parts_ref[0][:, own] = two_parts(value).T
            at += ref.shape[0]

    rows, columns = sum(half.shape[0] for half in halves), halves[0].shape[1]
    out_shape = [jax.ShapeDtypeStruct((rows, columns), jnp.float32)]
    if transposed:
        out_shape.append(jax.ShapeDtypeStruct((2 * columns, rows), jnp.bfloat16))
    return pl.pallas_call(
        kernel,
        out_shape=out_shape,
        in_specs=[WHOLE] * (1 + len(halves)),
        out_specs=[WHOLE] * len(out_shape),
        compiler_params=params(),
        cost_estimate=pl.CostEstimate(flops=2 * rows * 256 * 256, bytes_accessed=0, transcendentals=0),
    )(right_side, *halves)


def image_and_projected(total, pieces, vectors, inverse_upper, basis_parts):
    n = len(pieces)
    rows, (width, columns) = pieces[0].shape[0], vectors[0].shape

    def kernel(*refs):
        piece_refs, refs = refs[:n], refs[n:]
        vector_refs, refs = refs[:n], refs[n:]
        total_ref, refs = (refs[0], refs[1:]) if total is not None else (None, refs)
        inverse_ref, basis_ref, image_ref, projected_ref, stacked_ref = refs
        for at in range(n):
            stack_vectors(stacked_ref, at, vector_refs[at][...])
        projected = None
        for tile in row_tiles(rows):
            image = product_tile(piece_refs, stacked_ref, tile, columns)
            if total_ref is not None:
                image = image + total_ref[tile, :]
            image_ref[tile, :] = image
            term = jnp.dot(basis_ref[:, tile], two_parts(image), preferred_element_type=jnp.float32)
            projected = term if projected is None else projected + term
        projected = projected[:columns, :] + projected[columns:, :]
        projected = projected[:, :columns] + projected[:, columns:]
        projected_ref[...] = dot_parts(projected, inverse_ref[...])

    operands = [*pieces, *vectors] + ([] if total is None else [total]) + [inverse_upper, basis_parts]
    return pl.pallas_call(
        kernel,
        out_shape=[
            jax.ShapeDtypeStruct((rows, columns), jnp.float32),
            jax.ShapeDtypeStruct((columns, columns), jnp.float32),
        ],
        in_specs=[WHOLE] * len(operands),
        out_specs=[WHOLE] * 2,
        scratch_shapes=[pltpu.VMEM((n, 2 * width, 2 * columns), jnp.bfloat16)],
        compiler_params=params(),
        cost_estimate=product_cost(pieces, rows),
    )(*operands)


def residual_of(mapped, basis_rows, terms):
    def kernel(mapped_ref, basis_ref, *refs):
        *term_refs, projected_ref, residual_ref = refs
        projected = tree_sum([ref[...] for ref in term_refs])
        projected_ref[...] = projected
        for tile in row_tiles(mapped.shape[0]):
            residual_ref[tile, :] = mapped_ref[tile, :] - dot_parts(basis_ref[tile, :], projected)

    return pl.pallas_call(
        kernel,
        out_shape=[
            jax.ShapeDtypeStruct(terms[0].shape, jnp.float32),
            jax.ShapeDtypeStruct(mapped.shape, jnp.float32),
        ],
        in_specs=[WHOLE] * (2 + len(terms)),
        out_specs=[WHOLE] * 2,
        compiler_params=params(),
    )(mapped, basis_rows, *terms)


def exchange(value, offset, n):
    return lax.ppermute(value, "blk", [(at, at ^ offset) for at in range(n)])


def local(n, factor, initial, bounds):
    rows, columns = initial.shape
    half = rows // 2
    halves_at = range(2)
    first, early = first_vectors(factor, initial, n)
    pieces, coefficients = split_factor(factor, bounds, early, n)

    if n == 4:

        def gather_product(halves):
            top, bottom = halves
            x_top, y_bottom = exchange(top, 1, n), exchange(bottom, 2, n)
            x_bottom, y_top = exchange(bottom, 1, n), exchange(top, 2, n)
            total = partial_product(None, pieces[0], [top, bottom])
            xy_top, xy_bottom = exchange(x_top, 2, n), exchange(y_bottom, 1, n)
            total = partial_product(total, [pieces[1][0], pieces[2][1]], [x_top, y_bottom])
            total = partial_product(total, [pieces[1][1], pieces[2][0]], [x_bottom, y_top])
            return total, pieces[3], [xy_top, xy_bottom]

        def all_terms(term):
            pair = term + exchange(term, 1, n)
            return [pair, exchange(pair, 2, n)]
    else:

        def by_offset(value):
            gathered = lax.all_gather(value, "blk")
            me = lax.axis_index("blk")
            return [gathered[jnp.bitwise_xor(me, offset)] for offset in range(n)]

        def gather_product(halves):
            vectors = [block[at * half : (at + 1) * half] for block in by_offset(jnp.concatenate(halves)) for at in halves_at]
            return None, [piece for pair in pieces for piece in pair], vectors

        all_terms = by_offset

    previous, current = None, first
    for order_step in range(DEGREE):
        product = gather_product(current)
        following = [recurrence_step(coefficients, *product, current, previous, at) for at in halves_at]
        previous, current = current, following

    inverse_upper = inverse_cholesky(all_terms(gram_of(current)))
    basis_rows, basis_parts = times_right(current, inverse_upper, transposed=True)
    image, projected_term = image_and_projected(*gather_product(current), inverse_upper, basis_parts)
    projected_terms = all_terms(projected_term)
    (mapped,) = times_right([image], inverse_upper)
    projected, residual = residual_of(mapped, basis_rows, projected_terms)
    return (basis_rows, projected, residual)


def solution(mesh):
    in_specs = (P(("bulk", "blk"), None), P(("bulk", "blk"), None), P("bulk"))
    out_specs = (P(("bulk", "blk"), None), P("bulk", None), P(("bulk", "blk"), None))
    return jax.shard_map(
        functools.partial(local, mesh.shape["blk"]),
        mesh=mesh,
        in_specs=in_specs,
        out_specs=out_specs,
        check_vma=False,
    )
```

```python
import functools

import jax
import jax.numpy as jnp
from jax import lax
from jax.experimental import pallas as pl
from jax.experimental.pallas import tpu as pltpu
from jax.sharding import PartitionSpec as P

DEGREE = 8
HIGHEST = lax.Precision.HIGHEST
WHOLE = pl.BlockSpec(memory_space=pltpu.VMEM)
ANYWHERE = pl.BlockSpec(memory_space=pl.ANY)
HBM = pl.BlockSpec(memory_space=pltpu.HBM)
SCALARS = pl.BlockSpec(memory_space=pltpu.SMEM)
VMEM_LIMIT = 16 * 2**20


def params():
    return pltpu.CompilerParams(vmem_limit_bytes=VMEM_LIMIT)


def high_low(values):
    high = values.astype(jnp.bfloat16)
    low = (values - high.astype(jnp.float32)).astype(jnp.bfloat16)
    return high, low


def split_factor(factor, n, offsets):
    rows, order = factor.shape
    width, count = order // (2 * n), 2 * len(offsets)

    def kernel(factor_ref, *refs):
        out_refs, (slots, arrived) = refs[:count], refs[count:]
        me = lax.axis_index("blk")

        def fetch(at):
            owner = jnp.bitwise_xor(me, offsets[at // 2])
            start = pl.multiple_of((2 * owner + at % 2) * width, width)
            return pltpu.make_async_copy(
                factor_ref.at[:, pl.ds(start, width)], slots.at[at % 3], arrived.at[at % 3]
            )

        fetch(0).start()
        fetch(1).start()
        for at in range(count):
            if at + 2 < count:
                fetch(at + 2).start()
            fetch(at).wait()

            @pl.loop(0, rows // 64)
            def _(tile):
                own = pl.ds(pl.multiple_of(tile * 64, 64), 64)
                high, low = high_low(slots[at % 3, own, :])
                out_refs[at][own, :width] = high
                out_refs[at][own, width:] = low

    pieces = pl.pallas_call(
        kernel,
        out_shape=[jax.ShapeDtypeStruct((rows, 2 * width), jnp.bfloat16)] * count,
        in_specs=[HBM],
        out_specs=[WHOLE] * count,
        scratch_shapes=[pltpu.VMEM((3, rows, width), jnp.float32), pltpu.SemaphoreType.DMA((3,))],
        compiler_params=pltpu.CompilerParams(vmem_limit_bytes=40 * 2**20),
        cost_estimate=pl.CostEstimate(flops=0, bytes_accessed=8 * count * rows * width, transcendentals=0),
    )(factor)
    return [pieces[2 * at : 2 * at + 2] for at in range(len(offsets))]


def left_lanes(shape):
    return lax.broadcasted_iota(jnp.int32, shape, 1) < shape[1] // 2


def swap_lanes(values):
    return pltpu.roll(values, values.shape[1] // 2, 1)


def side_by_side(first, second):
    left = left_lanes(first.shape)
    swapped_first, swapped_second = swap_lanes(first), swap_lanes(second)
    return jnp.where(left, first, swapped_second), jnp.where(left, swapped_first, second)


def packed_vectors(initial, at, after=()):
    rows, columns = initial.shape
    half = rows // 2

    def kernel(initial_ref, *refs):
        out_ref = refs[-1]
        for tile in row_tiles(half):
            below = slice(half + tile.start, half + tile.stop)
            out_ref[tile, :] = side_by_side(initial_ref[tile, :], initial_ref[below, :])[at]

    return pl.pallas_call(
        kernel,
        out_shape=jax.ShapeDtypeStruct((half, columns), jnp.float32),
        in_specs=[WHOLE] + [ANYWHERE] * len(after),
        out_specs=WHOLE,
        compiler_params=params(),
    )(initial, *after)


def recurrence_coefficients(bounds, columns):
    def kernel(bounds_ref, out_ref):
        centre = (bounds_ref[0] + bounds_ref[1]) / 2.0
        radius = (bounds_ref[1] - bounds_ref[0]) / 2.0
        out_ref[0:1, :] = jnp.full((1, columns), centre, jnp.float32)
        out_ref[1:2, :] = 1.0 / jnp.full((1, columns), radius, jnp.float32)

    return pl.pallas_call(
        kernel,
        out_shape=jax.ShapeDtypeStruct((2, columns), jnp.float32),
        in_specs=[SCALARS],
        out_specs=WHOLE,
        compiler_params=params(),
    )(bounds)


def stack_vectors(stacked_ref, at, vectors):
    width, columns = vectors.shape
    high, low = high_low(vectors)
    for start in (0, width):
        stacked_ref[at, start : start + width, :columns] = high
        stacked_ref[at, start : start + width, columns:] = low


def product_tile(pieces, stacked_ref, rows, columns):
    sides = []
    for side in range(2):
        total = None
        for at in range(len(pieces) // 2):
            term = jnp.dot(pieces[2 * at + side][rows, :], stacked_ref[at], preferred_element_type=jnp.float32)
            total = term if total is None else total + term
        sides.append(total[:, :columns] + total[:, columns:])
    return jnp.where(left_lanes(sides[0].shape), *sides)


def add_parts(first, second):
    left = left_lanes(first.shape)
    return jnp.where(left, first, second) + swap_lanes(jnp.where(left, second, first))


def row_tiles(rows):
    tile = min(rows, 256)
    return [slice(start, start + tile) for start in range(0, rows, tile)]


def product_cost(pieces, rows):
    doubled = pieces[0].shape[1]
    return pl.CostEstimate(
        flops=rows * doubled * 32 * len(pieces),
        bytes_accessed=rows * doubled * len(pieces) // 8,
        transcendentals=0,
    )


def partial_product(total, pieces, vectors, after=()):
    n, blocks = len(pieces), len(vectors)
    rows, (width, columns) = pieces[0].shape[0], vectors[0].shape

    def kernel(*refs):
        piece_refs, vector_refs = refs[:n], refs[n : n + blocks]
        total_ref = refs[n + blocks] if total is not None else None
        out_ref, stacked_ref = refs[-2:]
        for at in range(blocks):
            stack_vectors(stacked_ref, at, vector_refs[at][...])
        for tile in row_tiles(rows):
            value = product_tile(piece_refs, stacked_ref, tile, columns)
            out_ref[tile, :] = value if total_ref is None else total_ref[tile, :] + value

    operands = [*pieces, *vectors] + ([] if total is None else [total])
    return pl.pallas_call(
        kernel,
        out_shape=jax.ShapeDtypeStruct((rows, columns), jnp.float32),
        in_specs=[WHOLE] * len(operands) + [ANYWHERE] * len(after),
        out_specs=WHOLE,
        scratch_shapes=[pltpu.VMEM((blocks, 2 * width, 2 * columns), jnp.bfloat16)],
        compiler_params=params(),
        cost_estimate=product_cost(pieces, rows),
    )(*operands, *after)


def held_until(value, after):
    def kernel(value_ref, *refs):
        refs[-1][...] = value_ref[...]

    return pl.pallas_call(
        kernel,
        out_shape=jax.ShapeDtypeStruct(value.shape, value.dtype),
        in_specs=[WHOLE] + [ANYWHERE] * len(after),
        out_specs=WHOLE,
        compiler_params=params(),
        cost_estimate=pl.CostEstimate(flops=0, bytes_accessed=0, transcendentals=0),
    )(value, *after)


def recurrence_step(coefficients, total, pieces, vectors, current, previous, after=()):
    n, blocks = len(pieces), len(vectors)
    rows, (width, columns) = pieces[0].shape[0], vectors[0].shape
    half = rows // 2

    def kernel(coefficient_ref, *refs):
        piece_refs, refs = refs[:n], refs[n:]
        vector_refs, refs = refs[:blocks], refs[blocks:]
        total_ref, refs = (refs[0], refs[1:]) if total is not None else (None, refs)
        current_ref, refs = refs[0], refs[1:]
        previous_ref, refs = (refs[0], refs[1:]) if previous is not None else (None, refs)
        out_ref, stacked_ref = refs[-2:]
        for at in range(blocks):
            stack_vectors(stacked_ref, at, vector_refs[at][...])
        centre, inverse_radius = coefficient_ref[0:1, :], coefficient_ref[1:2, :]

        def product(tile):
            value = product_tile(piece_refs, stacked_ref, tile, columns)
            return value if total_ref is None else value + total_ref[tile, :]

        for tile in row_tiles(half):
            value = add_parts(product(tile), product(slice(half + tile.start, half + tile.stop)))
            value = (value - centre * current_ref[tile, :]) * inverse_radius
            if previous_ref is not None:
                value = 2.0 * value - previous_ref[tile, :]
            out_ref[tile, :] = value

    operands = [*pieces, *vectors] + ([] if total is None else [total])
    operands += [current] + ([] if previous is None else [previous])
    return pl.pallas_call(
        kernel,
        out_shape=jax.ShapeDtypeStruct((half, columns), jnp.float32),
        in_specs=[WHOLE] * (1 + len(operands)) + [ANYWHERE] * len(after),
        out_specs=WHOLE,
        scratch_shapes=[pltpu.VMEM((blocks, 2 * width, 2 * columns), jnp.bfloat16)],
        compiler_params=params(),
        cost_estimate=product_cost(pieces, rows),
    )(coefficients, *operands, *after)


def dot_high(left_side, right_side, contract):
    return lax.dot_general(
        left_side, right_side, (contract, ((), ())), precision=HIGHEST, preferred_element_type=jnp.float32
    )


def tree_sum(values):
    while len(values) > 1:
        values = [values[at] + values[at + 1] for at in range(0, len(values), 2)]
    return values[0]


def filtered_and_gram(chunks):
    half, columns = chunks[0].shape

    def kernel(first_ref, second_ref, filtered_ref, gram_ref):
        total = None
        for tile in row_tiles(half):
            for start, rows in zip((0, half), side_by_side(first_ref[tile, :], second_ref[tile, :])):
                filtered_ref[start + tile.start : start + tile.stop, :] = rows
                term = dot_high(rows, rows, ((0,), (0,)))
                total = term if total is None else total + term
        gram_ref[...] = total

    return pl.pallas_call(
        kernel,
        out_shape=[
            jax.ShapeDtypeStruct((2 * half, columns), jnp.float32),
            jax.ShapeDtypeStruct((columns, columns), jnp.float32),
        ],
        in_specs=[WHOLE] * 2,
        out_specs=[WHOLE] * 2,
        compiler_params=params(),
        cost_estimate=pl.CostEstimate(flops=10**9 // 2, bytes_accessed=0, transcendentals=0),
    )(*chunks)


def three_parts(values):
    high = values.astype(jnp.bfloat16)
    return (high, *high_low(values - high.astype(jnp.float32)))


def dot_thin(left_side, right_side):
    a, b = three_parts(left_side), three_parts(right_side)
    pairs = [(a[0], b[0]), (a[0], b[1]), (a[1], b[0]), (a[1], b[1]), (a[0], b[2]), (a[2], b[0])]
    return lax.dot_general(
        jnp.concatenate([pair[0].astype(jnp.float32) for pair in pairs], axis=0).T.astype(jnp.bfloat16),
        jnp.concatenate([pair[1].astype(jnp.float32) for pair in pairs], axis=0).astype(jnp.bfloat16),
        (((1,), (0,)), ((), ())),
        preferred_element_type=jnp.float32,
    )


def inverse_cholesky(terms):
    columns = terms[0].shape[0]
    high = 8

    def kernel(*refs):
        *term_refs, out_ref, gram_ref, inverse_ref = refs
        gram_ref[...] = tree_sum([ref[...] for ref in term_refs])
        row_at = lax.broadcasted_iota(jnp.int32, (columns, columns), 0)
        column_at = lax.broadcasted_iota(jnp.int32, (columns, columns), 1)
        inverse_ref[...] = jnp.where(row_at == column_at, 1.0, 0.0)
        sub_row = lax.broadcasted_iota(jnp.int32, (high, columns), 0)
        for start in range(0, columns, high):
            stop = start + high
            own, inverse = gram_ref[start:stop, :], inverse_ref[start:stop, :]
            spread = [
                jnp.broadcast_to(own[:, start + at : start + at + 1], (high, columns)) for at in range(high)
            ]
            pivots = jnp.ones((high, columns), jnp.float32)
            reciprocals = jnp.ones((high, columns), jnp.float32)
            for at in range(high):
                pivot = jnp.broadcast_to(spread[at][at : at + 1, :], (high, columns))
                reciprocal = 1.0 / pivot
                pivots = jnp.where(sub_row == at, pivot, pivots)
                reciprocals = jnp.where(sub_row == at, reciprocal, reciprocals)
                if at + 1 == high:
                    break
                factor = jnp.where(sub_row > at, spread[at], 0.0) * reciprocal
                for later in range(at + 1, high):
                    spread[later] = spread[later] - factor * spread[later][at : at + 1, :]
                own = own - factor * own[at : at + 1, :]
                inverse = inverse - factor * inverse[at : at + 1, :]
            inverse_ref[start:stop, :] = inverse / jnp.sqrt(pivots)
            if stop < columns:
                update = dot_thin(own * reciprocals, jnp.concatenate([own, inverse], axis=1))
                gram_ref[stop:, :] = gram_ref[stop:, :] - update[stop:, :columns]
                inverse_ref[stop:, :] = inverse_ref[stop:, :] - update[stop:, columns:]
        out_ref[...] = inverse_ref[...].T

    return pl.pallas_call(
        kernel,
        out_shape=jax.ShapeDtypeStruct((columns, columns), jnp.float32),
        in_specs=[WHOLE] * len(terms),
        out_specs=WHOLE,
        scratch_shapes=[pltpu.VMEM((columns, columns), jnp.float32)] * 2,
        compiler_params=params(),
        cost_estimate=pl.CostEstimate(flops=8 * 10**9, bytes_accessed=0, transcendentals=0),
    )(*terms)


def two_parts(values):
    return jnp.concatenate(high_low(values), axis=1)


def dot_parts(left_side, right_side):
    columns = right_side.shape[1]
    right_parts = two_parts(right_side)
    product = jnp.dot(
        two_parts(left_side),
        jnp.concatenate([right_parts, right_parts], axis=0),
        preferred_element_type=jnp.float32,
    )
    return product[:, :columns] + product[:, columns:]


def times_right(block, right_side, transposed=False):
    rows, columns = block.shape

    def kernel(right_ref, block_ref, out_ref, *parts_ref):
        for tile in row_tiles(rows):
            value = dot_parts(block_ref[tile, :], right_ref[...])
            out_ref[tile, :] = value
            if transposed:
                parts_ref[0][:, tile] = two_parts(value).T

    out_shape = [jax.ShapeDtypeStruct((rows, columns), jnp.float32)]
    if transposed:
        out_shape.append(jax.ShapeDtypeStruct((2 * columns, rows), jnp.bfloat16))
    return pl.pallas_call(
        kernel,
        out_shape=out_shape,
        in_specs=[WHOLE] * 2,
        out_specs=[WHOLE] * len(out_shape),
        compiler_params=params(),
        cost_estimate=pl.CostEstimate(flops=2 * rows * 256 * 256, bytes_accessed=0, transcendentals=0),
    )(right_side, block)


def image_and_projected(first_parts, total, pieces, vectors, inverse_upper, basis_parts):
    n, blocks = len(pieces), len(vectors)
    rows, (width, columns) = pieces[0].shape[0], vectors[0].shape

    def kernel(first_ref, *refs):
        piece_refs, refs = refs[:n], refs[n:]
        vector_refs, refs = refs[:blocks], refs[blocks:]
        total_ref, refs = (refs[0], refs[1:]) if total is not None else (None, refs)
        inverse_ref, basis_ref, image_ref, projected_ref, stacked_ref = refs
        for at in range(blocks):
            stack_vectors(stacked_ref, at, vector_refs[at][...])
        projected = None
        for tile in row_tiles(rows):
            value = product_tile(piece_refs, stacked_ref, tile, columns)
            if total_ref is not None:
                value = value + total_ref[tile, :]
            image = add_parts(first_ref[tile, :], value)
            image_ref[tile, :] = image
            term = jnp.dot(basis_ref[:, tile], two_parts(image), preferred_element_type=jnp.float32)
            projected = term if projected is None else projected + term
        projected = projected[:columns, :] + projected[columns:, :]
        projected = projected[:, :columns] + projected[:, columns:]
        projected_ref[...] = dot_parts(projected, inverse_ref[...])

    operands = [*pieces, *vectors] + ([] if total is None else [total]) + [inverse_upper, basis_parts]
    return pl.pallas_call(
        kernel,
        out_shape=[
            jax.ShapeDtypeStruct((rows, columns), jnp.float32),
            jax.ShapeDtypeStruct((columns, columns), jnp.float32),
        ],
        in_specs=[WHOLE] * (1 + len(operands)),
        out_specs=[WHOLE] * 2,
        scratch_shapes=[pltpu.VMEM((blocks, 2 * width, 2 * columns), jnp.bfloat16)],
        compiler_params=params(),
        cost_estimate=product_cost(pieces, rows),
    )(first_parts, *operands)


def residual_of(mapped, basis_rows, terms):
    def kernel(mapped_ref, basis_ref, *refs):
        *term_refs, projected_ref, residual_ref = refs
        projected = tree_sum([ref[...] for ref in term_refs])
        projected_ref[...] = projected
        for tile in row_tiles(mapped.shape[0]):
            residual_ref[tile, :] = mapped_ref[tile, :] - dot_parts(basis_ref[tile, :], projected)

    return pl.pallas_call(
        kernel,
        out_shape=[
            jax.ShapeDtypeStruct(terms[0].shape, jnp.float32),
            jax.ShapeDtypeStruct(mapped.shape, jnp.float32),
        ],
        in_specs=[WHOLE] * (2 + len(terms)),
        out_specs=[WHOLE] * 2,
        compiler_params=params(),
    )(mapped, basis_rows, *terms)


def exchange(value, offset, n):
    return lax.ppermute(value, "blk", [(at, at ^ offset) for at in range(n)])


def local(n, factor, initial, bounds):
    coefficients = recurrence_coefficients(bounds, initial.shape[1])
    first = packed_vectors(initial, 0)

    if n == 4:
        own, along_x = split_factor(factor, n, (0, 1))
        second = packed_vectors(initial, 1, after=(own[0],))
        along_y, across = split_factor(factor, n, (2, 3))

        sent, forwarded, held = {}, {}, {0: (), 1: ()}

        def send(at, chunk):
            by_x, by_y = exchange(chunk, 1, n), exchange(chunk, 2, n)
            sent[at] = by_x, by_y, partial_product(None, own, [chunk])

        def forward(at, after):
            block = sent[at][at]
            if after:
                block = held_until(block, after)
                held[at] = (block,)
            forwarded[at] = exchange(block, 2 - at, n)

        def last_blocks(at):
            by_x, by_y, total = sent[at]
            other = 1 - at
            total = partial_product(total, [*along_x, *along_y], [by_x, by_y], after=(sent[other][2],))
            if other not in forwarded:
                forward(other, (total,))
            return total, across, [forwarded.pop(at)]

        def all_terms(term):
            return [term] + [exchange(term, offset, n) for offset in (1, 2, 3)]
    else:
        pieces = [piece for pair in split_factor(factor, n, range(n)) for piece in pair]
        second = packed_vectors(initial, 1)
        sent, held = {}, {0: (), 1: ()}

        def all_terms(value):
            gathered = lax.all_gather(value, "blk")
            me = lax.axis_index("blk")
            return [gathered[jnp.bitwise_xor(me, offset)] for offset in range(n)]

        def send(at, chunk):
            sent[at] = all_terms(chunk)

        def last_blocks(at):
            return None, pieces, sent[at]

    previous, current = [None, None], [first, second]
    for at in range(2):
        send(at, current[at])
    if n == 4:
        forward(0, ())
    for order_step in range(DEGREE):
        for at in range(2):
            blocks = last_blocks(at)
            following = recurrence_step(coefficients, *blocks, current[at], previous[at], after=held[1 - at])
            previous[at], current[at] = current[at], following
            send(at, following)

    filtered, gram_term = filtered_and_gram(current)
    inverse_upper = inverse_cholesky(all_terms(gram_term))
    basis_rows, basis_parts = times_right(filtered, inverse_upper, transposed=True)
    first_parts = partial_product(*last_blocks(0))
    image, projected_term = image_and_projected(first_parts, *last_blocks(1), inverse_upper, basis_parts)
    projected_terms = all_terms(projected_term)
    (mapped,) = times_right(image, inverse_upper)
    projected, residual = residual_of(mapped, basis_rows, projected_terms)
    return (basis_rows, projected, residual)


def solution(mesh):
    in_specs = (P(("bulk", "blk"), None), P(("bulk", "blk"), None), P("bulk"))
    out_specs = (P(("bulk", "blk"), None), P("bulk", None), P(("bulk", "blk"), None))
    return jax.shard_map(
        functools.partial(local, mesh.shape["blk"]),
        mesh=mesh,
        in_specs=in_specs,
        out_specs=out_specs,
        check_vma=False,
    )
```

```python
import functools

import jax
import jax.numpy as jnp
from jax import lax
from jax.experimental import pallas as pl
from jax.experimental.pallas import tpu as pltpu
from jax.sharding import PartitionSpec as P

DEGREE = 8
HIGHEST = lax.Precision.HIGHEST
WHOLE = pl.BlockSpec(memory_space=pltpu.VMEM)
ANYWHERE = pl.BlockSpec(memory_space=pl.ANY)
HBM = pl.BlockSpec(memory_space=pltpu.HBM)
SCALARS = pl.BlockSpec(memory_space=pltpu.SMEM)
VMEM_LIMIT = 16 * 2**20


def params():
    return pltpu.CompilerParams(vmem_limit_bytes=VMEM_LIMIT)


def high_low(values):
    high = values.astype(jnp.bfloat16)
    low = (values - high.astype(jnp.float32)).astype(jnp.bfloat16)
    return high, low


def split_factor(factor, n, offsets, after=()):
    rows, order = factor.shape
    width, count = order // (2 * n), 2 * len(offsets)

    def kernel(factor_ref, *refs):
        out_refs, (slots, arrived) = refs[len(after) : len(after) + count], refs[-2:]
        me = lax.axis_index("blk")

        def fetch(at):
            owner = jnp.bitwise_xor(me, offsets[at // 2])
            start = pl.multiple_of((2 * owner + at % 2) * width, width)
            return pltpu.make_async_copy(
                factor_ref.at[:, pl.ds(start, width)], slots.at[at % 3], arrived.at[at % 3]
            )

        fetch(0).start()
        fetch(1).start()
        for at in range(count):
            if at + 2 < count:
                fetch(at + 2).start()
            fetch(at).wait()

            @pl.loop(0, rows // 64)
            def _(tile):
                own = pl.ds(pl.multiple_of(tile * 64, 64), 64)
                high, low = high_low(slots[at % 3, own, :])
                out_refs[at][own, :width] = high
                out_refs[at][own, width:] = low

    pieces = pl.pallas_call(
        kernel,
        out_shape=[jax.ShapeDtypeStruct((rows, 2 * width), jnp.bfloat16)] * count,
        in_specs=[HBM] + [ANYWHERE] * len(after),
        out_specs=[WHOLE] * count,
        scratch_shapes=[pltpu.VMEM((3, rows, width), jnp.float32), pltpu.SemaphoreType.DMA((3,))],
        compiler_params=pltpu.CompilerParams(vmem_limit_bytes=40 * 2**20),
        cost_estimate=pl.CostEstimate(flops=0, bytes_accessed=8 * count * rows * width, transcendentals=0),
    )(factor, *after)
    return [pieces[2 * at : 2 * at + 2] for at in range(len(offsets))]


def recurrence_coefficients(bounds, columns):
    def kernel(bounds_ref, out_ref):
        centre = (bounds_ref[0] + bounds_ref[1]) / 2.0
        radius = (bounds_ref[1] - bounds_ref[0]) / 2.0
        out_ref[0:1, :] = jnp.full((1, columns), centre, jnp.float32)
        out_ref[1:2, :] = 1.0 / jnp.full((1, columns), radius, jnp.float32)

    return pl.pallas_call(
        kernel,
        out_shape=jax.ShapeDtypeStruct((2, columns), jnp.float32),
        in_specs=[SCALARS],
        out_specs=WHOLE,
        compiler_params=params(),
    )(bounds)


def stack_vectors(stacked_ref, at, vectors):
    width, columns = vectors.shape
    high, low = high_low(vectors)
    for start in (0, width):
        stacked_ref[at, start : start + width, :columns] = high
        stacked_ref[at, start : start + width, columns:] = low


def product_tile(pieces, stacked_ref, rows, columns):
    total = None
    for at, piece in enumerate(pieces):
        term = jnp.dot(piece[rows, :], stacked_ref[at], preferred_element_type=jnp.float32)
        total = term if total is None else total + term
    return total[:, :columns] + total[:, columns:]


def row_tiles(rows):
    tile = min(rows, 256)
    return [slice(start, start + tile) for start in range(0, rows, tile)]


def product_cost(pieces, rows):
    doubled = pieces[0].shape[1]
    return pl.CostEstimate(
        flops=2 * rows * doubled * 256 * len(pieces),
        bytes_accessed=2 * rows * doubled * len(pieces),
        transcendentals=0,
    )


def partial_product(total, pieces, vectors):
    n = len(pieces)
    rows, (width, columns) = pieces[0].shape[0], vectors[0].shape

    def kernel(*refs):
        piece_refs, vector_refs = refs[:n], refs[n : 2 * n]
        total_ref = refs[2 * n] if total is not None else None
        out_ref, stacked_ref = refs[-2:]
        for at in range(n):
            stack_vectors(stacked_ref, at, vector_refs[at][...])
        for tile in row_tiles(rows):
            value = product_tile(piece_refs, stacked_ref, tile, columns)
            out_ref[tile, :] = value if total_ref is None else total_ref[tile, :] + value

    operands = [*pieces, *vectors] + ([] if total is None else [total])
    return pl.pallas_call(
        kernel,
        out_shape=jax.ShapeDtypeStruct((rows, columns), jnp.float32),
        in_specs=[WHOLE] * len(operands),
        out_specs=WHOLE,
        scratch_shapes=[pltpu.VMEM((n, 2 * width, 2 * columns), jnp.bfloat16)],
        compiler_params=params(),
        cost_estimate=product_cost(pieces, rows),
    )(*operands)


def recurrence_step(coefficients, total, pieces, vectors, current, previous, at):
    n = len(pieces)
    half, (width, columns) = current[at].shape[0], vectors[0].shape

    def kernel(coefficient_ref, *refs):
        piece_refs, refs = refs[:n], refs[n:]
        vector_refs, refs = refs[:n], refs[n:]
        total_ref, refs = (refs[0], refs[1:]) if total is not None else (None, refs)
        current_ref, refs = refs[0], refs[1:]
        previous_ref, refs = (refs[0], refs[1:]) if previous else (None, refs)
        out_ref, stacked_ref = refs
        for term in range(n):
            stack_vectors(stacked_ref, term, vector_refs[term][...])
        centre, inverse_radius = coefficient_ref[0:1, :columns], coefficient_ref[1:2, :columns]
        for own in row_tiles(half):
            tile = slice(at * half + own.start, at * half + own.stop)
            value = product_tile(piece_refs, stacked_ref, tile, columns)
            if total_ref is not None:
                value = value + total_ref[tile, :]
            value = (value - centre * current_ref[own, :]) * inverse_radius
            if previous_ref is not None:
                value = 2.0 * value - previous_ref[own, :]
            out_ref[own, :] = value

    operands = [*pieces, *vectors] + ([] if total is None else [total])
    operands += [current[at]] + ([previous[at]] if previous else [])
    return pl.pallas_call(
        kernel,
        out_shape=jax.ShapeDtypeStruct((half, columns), jnp.float32),
        in_specs=[WHOLE] * (1 + len(operands)),
        out_specs=WHOLE,
        scratch_shapes=[pltpu.VMEM((n, 2 * width, 2 * columns), jnp.bfloat16)],
        compiler_params=params(),
        cost_estimate=product_cost(pieces, half),
    )(coefficients, *operands)


def dot_high(left_side, right_side, contract):
    return lax.dot_general(
        left_side, right_side, (contract, ((), ())), precision=HIGHEST, preferred_element_type=jnp.float32
    )


def tree_sum(values):
    while len(values) > 1:
        values = [values[at] + values[at + 1] for at in range(0, len(values), 2)]
    return values[0]


def gram_of(halves):
    def kernel(*refs):
        *in_refs, out_ref = refs
        total = None
        for ref in in_refs:
            term = dot_high(ref[...], ref[...], ((0,), (0,)))
            total = term if total is None else total + term
        out_ref[...] = total

    columns = halves[0].shape[1]
    return pl.pallas_call(
        kernel,
        out_shape=jax.ShapeDtypeStruct((columns, columns), jnp.float32),
        in_specs=[WHOLE] * len(halves),
        out_specs=WHOLE,
        compiler_params=params(),
    )(*halves)


def three_parts(values):
    high = values.astype(jnp.bfloat16)
    return (high, *high_low(values - high.astype(jnp.float32)))


def dot_thin(left_side, right_side):
    a, b = three_parts(left_side), three_parts(right_side)
    pairs = [(a[0], b[0]), (a[0], b[1]), (a[1], b[0]), (a[1], b[1]), (a[0], b[2]), (a[2], b[0])]
    return lax.dot_general(
        jnp.concatenate([pair[0].astype(jnp.float32) for pair in pairs], axis=0).T.astype(jnp.bfloat16),
        jnp.concatenate([pair[1].astype(jnp.float32) for pair in pairs], axis=0).astype(jnp.bfloat16),
        (((1,), (0,)), ((), ())),
        preferred_element_type=jnp.float32,
    )


def inverse_cholesky(terms):
    columns = terms[0].shape[0]
    high = 8

    def kernel(*refs):
        *term_refs, out_ref, gram_ref, inverse_ref = refs
        gram_ref[...] = tree_sum([ref[...] for ref in term_refs])
        row_at = lax.broadcasted_iota(jnp.int32, (columns, columns), 0)
        column_at = lax.broadcasted_iota(jnp.int32, (columns, columns), 1)
        inverse_ref[...] = jnp.where(row_at == column_at, 1.0, 0.0)
        sub_row = lax.broadcasted_iota(jnp.int32, (high, columns), 0)
        for start in range(0, columns, high):
            stop = start + high
            own, inverse = gram_ref[start:stop, :], inverse_ref[start:stop, :]
            spread = [
                jnp.broadcast_to(own[:, start + at : start + at + 1], (high, columns)) for at in range(high)
            ]
            pivots = jnp.ones((high, columns), jnp.float32)
            reciprocals = jnp.ones((high, columns), jnp.float32)
            for at in range(high):
                pivot = jnp.broadcast_to(spread[at][at : at + 1, :], (high, columns))
                reciprocal = 1.0 / pivot
                pivots = jnp.where(sub_row == at, pivot, pivots)
                reciprocals = jnp.where(sub_row == at, reciprocal, reciprocals)
                if at + 1 == high:
                    break
                factor = jnp.where(sub_row > at, spread[at], 0.0) * reciprocal
                for later in range(at + 1, high):
                    spread[later] = spread[later] - factor * spread[later][at : at + 1, :]
                own = own - factor * own[at : at + 1, :]
                inverse = inverse - factor * inverse[at : at + 1, :]
            inverse_ref[start:stop, :] = inverse / jnp.sqrt(pivots)
            if stop < columns:
                update = dot_thin(own * reciprocals, jnp.concatenate([own, inverse], axis=1))
                gram_ref[stop:, :] = gram_ref[stop:, :] - update[stop:, :columns]
                inverse_ref[stop:, :] = inverse_ref[stop:, :] - update[stop:, columns:]
        out_ref[...] = inverse_ref[...].T

    return pl.pallas_call(
        kernel,
        out_shape=jax.ShapeDtypeStruct((columns, columns), jnp.float32),
        in_specs=[WHOLE] * len(terms),
        out_specs=WHOLE,
        scratch_shapes=[pltpu.VMEM((columns, columns), jnp.float32)] * 2,
        compiler_params=params(),
        cost_estimate=pl.CostEstimate(flops=25 * 10**9, bytes_accessed=0, transcendentals=0),
    )(*terms)


def two_parts(values):
    return jnp.concatenate(high_low(values), axis=1)


def dot_parts(left_side, right_side):
    columns = right_side.shape[1]
    right_parts = two_parts(right_side)
    product = jnp.dot(
        two_parts(left_side),
        jnp.concatenate([right_parts, right_parts], axis=0),
        preferred_element_type=jnp.float32,
    )
    return product[:, :columns] + product[:, columns:]


def times_right(halves, right_side, transposed=False):
    def kernel(right_ref, *refs):
        in_refs, (out_ref, *parts_ref) = refs[: len(halves)], refs[len(halves) :]
        at = 0
        for ref in in_refs:
            for tile in row_tiles(ref.shape[0]):
                own = slice(at + tile.start, at + tile.stop)
                value = dot_parts(ref[tile, :], right_ref[...])
                out_ref[own, :] = value
                if transposed:
                    parts_ref[0][:, own] = two_parts(value).T
            at += ref.shape[0]

    rows, columns = sum(half.shape[0] for half in halves), halves[0].shape[1]
    out_shape = [jax.ShapeDtypeStruct((rows, columns), jnp.float32)]
    if transposed:
        out_shape.append(jax.ShapeDtypeStruct((2 * columns, rows), jnp.bfloat16))
    return pl.pallas_call(
        kernel,
        out_shape=out_shape,
        in_specs=[WHOLE] * (1 + len(halves)),
        out_specs=[WHOLE] * len(out_shape),
        compiler_params=params(),
        cost_estimate=pl.CostEstimate(flops=2 * rows * 256 * 256, bytes_accessed=0, transcendentals=0),
    )(right_side, *halves)


def image_and_projected(total, pieces, vectors, inverse_upper, basis_parts):
    n = len(pieces)
    rows, (width, columns) = pieces[0].shape[0], vectors[0].shape

    def kernel(*refs):
        piece_refs, refs = refs[:n], refs[n:]
        vector_refs, refs = refs[:n], refs[n:]
        total_ref, refs = (refs[0], refs[1:]) if total is not None else (None, refs)
        inverse_ref, basis_ref, image_ref, projected_ref, stacked_ref = refs
        for at in range(n):
            stack_vectors(stacked_ref, at, vector_refs[at][...])
        projected = None
        for tile in row_tiles(rows):
            image = product_tile(piece_refs, stacked_ref, tile, columns)
            if total_ref is not None:
                image = image + total_ref[tile, :]
            image_ref[tile, :] = image
            term = jnp.dot(basis_ref[:, tile], two_parts(image), preferred_element_type=jnp.float32)
            projected = term if projected is None else projected + term
        projected = projected[:columns, :] + projected[columns:, :]
        projected = projected[:, :columns] + projected[:, columns:]
        projected_ref[...] = dot_parts(projected, inverse_ref[...])

    operands = [*pieces, *vectors] + ([] if total is None else [total]) + [inverse_upper, basis_parts]
    return pl.pallas_call(
        kernel,
        out_shape=[
            jax.ShapeDtypeStruct((rows, columns), jnp.float32),
            jax.ShapeDtypeStruct((columns, columns), jnp.float32),
        ],
        in_specs=[WHOLE] * len(operands),
        out_specs=[WHOLE] * 2,
        scratch_shapes=[pltpu.VMEM((n, 2 * width, 2 * columns), jnp.bfloat16)],
        compiler_params=params(),
        cost_estimate=product_cost(pieces, rows),
    )(*operands)


def residual_of(mapped, basis_rows, terms):
    def kernel(mapped_ref, basis_ref, *refs):
        *term_refs, projected_ref, residual_ref = refs
        projected = tree_sum([ref[...] for ref in term_refs])
        projected_ref[...] = projected
        for tile in row_tiles(mapped.shape[0]):
            residual_ref[tile, :] = mapped_ref[tile, :] - dot_parts(basis_ref[tile, :], projected)

    return pl.pallas_call(
        kernel,
        out_shape=[
            jax.ShapeDtypeStruct(terms[0].shape, jnp.float32),
            jax.ShapeDtypeStruct(mapped.shape, jnp.float32),
        ],
        in_specs=[WHOLE] * (2 + len(terms)),
        out_specs=[WHOLE] * 2,
        compiler_params=params(),
    )(mapped, basis_rows, *terms)


def exchange(value, offset, n):
    return lax.ppermute(value, "blk", [(at, at ^ offset) for at in range(n)])


def local(n, factor, initial, bounds):
    rows, columns = initial.shape
    half = rows // 2
    halves_at = range(2)
    coefficients = recurrence_coefficients(bounds, columns)

    if n == 4:
        own, along_x = split_factor(factor, n, (0, 1))
        rest = []

        def gather_product(halves):
            top, bottom = halves
            x_top = exchange(top, 1, n)
            y_bottom, x_bottom, y_top = exchange(bottom, 2, n), exchange(bottom, 1, n), exchange(top, 2, n)
            xy_top, xy_bottom = exchange(x_top, 2, n), exchange(y_bottom, 1, n)
            if not rest:
                rest.extend(split_factor(factor, n, (2, 3), after=(x_top, y_bottom)))
            along_y, across = rest
            total = partial_product(None, own, halves)
            total = partial_product(total, [along_x[0], along_y[1]], [x_top, y_bottom])
            total = partial_product(total, [along_x[1], along_y[0]], [x_bottom, y_top])
            return total, across, [xy_top, xy_bottom]

        def all_terms(term):
            return [term] + [exchange(term, offset, n) for offset in (1, 2, 3)]
    else:
        pieces = [piece for pair in split_factor(factor, n, range(n)) for piece in pair]

        def all_terms(value):
            gathered = lax.all_gather(value, "blk")
            me = lax.axis_index("blk")
            return [gathered[jnp.bitwise_xor(me, offset)] for offset in range(n)]

        def gather_product(halves):
            blocks = all_terms(jnp.concatenate(halves))
            return None, pieces, [block[at * half : (at + 1) * half] for block in blocks for at in halves_at]

    previous, current = None, [initial[:half], initial[half:]]
    for order_step in range(DEGREE):
        product = gather_product(current)
        following = [recurrence_step(coefficients, *product, current, previous, at) for at in halves_at]
        previous, current = current, following

    inverse_upper = inverse_cholesky(all_terms(gram_of(current)))
    basis_rows, basis_parts = times_right(current, inverse_upper, transposed=True)
    image, projected_term = image_and_projected(*gather_product(current), inverse_upper, basis_parts)
    projected_terms = all_terms(projected_term)
    (mapped,) = times_right([image], inverse_upper)
    projected, residual = residual_of(mapped, basis_rows, projected_terms)
    return (basis_rows, projected, residual)


def solution(mesh):
    in_specs = (P(("bulk", "blk"), None), P(("bulk", "blk"), None), P("bulk"))
    out_specs = (P(("bulk", "blk"), None), P("bulk", None), P(("bulk", "blk"), None))
    return jax.shard_map(
        functools.partial(local, mesh.shape["blk"]),
        mesh=mesh,
        in_specs=in_specs,
        out_specs=out_specs,
        check_vma=False,
    )
```

```python
import functools

import jax
import jax.numpy as jnp
from jax import lax
from jax.experimental import pallas as pl
from jax.experimental.pallas import tpu as pltpu
from jax.sharding import PartitionSpec as P

DEGREE = 8
HIGHEST = lax.Precision.HIGHEST
WHOLE = pl.BlockSpec(memory_space=pltpu.VMEM)
ANYWHERE = pl.BlockSpec(memory_space=pl.ANY)
HBM = pl.BlockSpec(memory_space=pltpu.HBM)
SCALARS = pl.BlockSpec(memory_space=pltpu.SMEM)
VMEM_LIMIT = 16 * 2**20


def params():
    return pltpu.CompilerParams(vmem_limit_bytes=VMEM_LIMIT)


def high_low(values):
    high = values.astype(jnp.bfloat16)
    low = (values - high.astype(jnp.float32)).astype(jnp.bfloat16)
    return high, low


def splitter(factor_ref, slots, arrived, count, emit):
    rows, width = slots.shape[1:]
    me = lax.axis_index("blk")

    def fetch(at):
        owner = jnp.bitwise_xor(me, at // 2)
        start = pl.multiple_of((2 * owner + at % 2) * width, width)
        return pltpu.make_async_copy(factor_ref.at[:, pl.ds(start, width)], slots.at[at % 3], arrived.at[at % 3])

    fetch(0).start()
    fetch(1).start()
    for at in range(count):
        if at + 2 < count:
            fetch(at + 2).start()
        fetch(at).wait()

        @pl.loop(0, rows // 64)
        def _(tile):
            own = pl.ds(pl.multiple_of(tile * 64, 64), 64)
            emit(at, own, *high_low(slots[at % 3, own, :]))

        yield at


def starts_late():
    return lax.rem(lax.axis_index("bulk"), 2) == 0


def first_vectors(factor, initial, n):
    (rows, order), columns = factor.shape, initial.shape[1]
    width, count, half = order // (2 * n), 2 * n, rows // 2

    def kernel(initial_ref, factor_ref, top_ref, bottom_ref, piece_ref, slots, arrived, split, sent, loaded):
        loads = [
            pltpu.make_async_copy(initial_ref.at[pl.ds(at * half, half), :], ref, loaded.at[at])
            for at, ref in enumerate((top_ref, bottom_ref))
        ]
        for load in loads:
            load.start()

        @pl.when(starts_late())
        def _():
            def store(at):
                return pltpu.make_async_copy(split.at[at % 2], piece_ref.at[at], sent.at[at % 2])

            def emit(at, own, high, low):
                split[at % 2, own, :width] = high
                split[at % 2, own, width:] = low

            for at in splitter(factor_ref, slots, arrived, count, emit):
                store(at).start()
                if at >= 1:
                    store(at - 1).wait()
            store(count - 1).wait()

        for load in loads:
            load.wait()

    top, bottom, pieces = pl.pallas_call(
        kernel,
        out_shape=[jax.ShapeDtypeStruct((half, columns), jnp.float32)] * 2
        + [jax.ShapeDtypeStruct((count, rows, 2 * width), jnp.bfloat16)],
        in_specs=[HBM] * 2,
        out_specs=[WHOLE] * 2 + [HBM],
        scratch_shapes=[
            pltpu.VMEM((3, rows, width), jnp.float32),
            pltpu.SemaphoreType.DMA((3,)),
            pltpu.VMEM((2, rows, 2 * width), jnp.bfloat16),
            pltpu.SemaphoreType.DMA((2,)),
            pltpu.SemaphoreType.DMA((2,)),
        ],
        compiler_params=pltpu.CompilerParams(vmem_limit_bytes=56 * 2**20),
    )(initial, factor)
    return [top, bottom], pieces


def split_factor(factor, early, n):
    rows, order = factor.shape
    width, count = order // (2 * n), 2 * n

    def kernel(factor_ref, early_ref, *refs):
        out_refs, (slots, arrived, loaded) = refs[:count], refs[count:]

        @pl.when(starts_late())
        def _():
            loads = [
                pltpu.make_async_copy(early_ref.at[at], out_refs[at], loaded.at[at]) for at in range(count)
            ]
            for load in loads:
                load.start()
            for load in loads:
                load.wait()

        @pl.when(jnp.logical_not(starts_late()))
        def _():
            def emit(at, own, high, low):
                out_refs[at][own, :width] = high
                out_refs[at][own, width:] = low

            for _ in splitter(factor_ref, slots, arrived, count, emit):
                pass

    pieces = pl.pallas_call(
        kernel,
        out_shape=[jax.ShapeDtypeStruct((rows, 2 * width), jnp.bfloat16)] * count,
        in_specs=[HBM] * 2,
        out_specs=[WHOLE] * count,
        scratch_shapes=[
            pltpu.VMEM((3, rows, width), jnp.float32),
            pltpu.SemaphoreType.DMA((3,)),
            pltpu.SemaphoreType.DMA((count,)),
        ],
        compiler_params=pltpu.CompilerParams(vmem_limit_bytes=28 * 2**20),
        cost_estimate=pl.CostEstimate(flops=0, bytes_accessed=4 * rows * order, transcendentals=0),
    )(factor, early)
    return [pieces[2 * offset : 2 * offset + 2] for offset in range(n)]


def recurrence_coefficients(bounds, columns):
    def kernel(bounds_ref, out_ref):
        centre = (bounds_ref[0] + bounds_ref[1]) / 2.0
        radius = (bounds_ref[1] - bounds_ref[0]) / 2.0
        out_ref[0:1, :] = jnp.full((1, columns), centre, jnp.float32)
        out_ref[1:2, :] = 1.0 / jnp.full((1, columns), radius, jnp.float32)

    return pl.pallas_call(
        kernel,
        out_shape=jax.ShapeDtypeStruct((2, columns), jnp.float32),
        in_specs=[SCALARS],
        out_specs=WHOLE,
        compiler_params=params(),
    )(bounds)


def stack_vectors(stacked_ref, at, vectors):
    width, columns = vectors.shape
    high, low = high_low(vectors)
    for start in (0, width):
        stacked_ref[at, start : start + width, :columns] = high
        stacked_ref[at, start : start + width, columns:] = low


def product_tile(pieces, stacked_ref, rows, columns):
    total = None
    for at, piece in enumerate(pieces):
        term = jnp.dot(piece[rows, :], stacked_ref[at], preferred_element_type=jnp.float32)
        total = term if total is None else total + term
    return total[:, :columns] + total[:, columns:]


def row_tiles(rows):
    tile = min(rows, 256)
    return [slice(start, start + tile) for start in range(0, rows, tile)]


def product_cost(pieces, rows):
    doubled = pieces[0].shape[1]
    return pl.CostEstimate(
        flops=2 * rows * doubled * 256 * len(pieces),
        bytes_accessed=2 * rows * doubled * len(pieces),
        transcendentals=0,
    )


def partial_product(total, pieces, vectors, put_off=False):
    n = len(pieces)
    rows, (width, columns) = pieces[0].shape[0], vectors[0].shape

    def kernel(*refs):
        piece_refs, vector_refs = refs[:n], refs[n : 2 * n]
        total_ref = refs[2 * n] if total is not None else None
        out_ref, stacked_ref = refs[-2:]

        def add():
            for at in range(n):
                stack_vectors(stacked_ref, at, vector_refs[at][...])
            for tile in row_tiles(rows):
                value = product_tile(piece_refs, stacked_ref, tile, columns)
                out_ref[tile, :] = value if total_ref is None else total_ref[tile, :] + value

        if put_off:
            pl.when(starts_late())(add)

            @pl.when(jnp.logical_not(starts_late()))
            def _():
                out_ref[...] = total_ref[...]
        else:
            add()

    operands = [*pieces, *vectors] + ([] if total is None else [total])
    return pl.pallas_call(
        kernel,
        out_shape=jax.ShapeDtypeStruct((rows, columns), jnp.float32),
        in_specs=[WHOLE] * len(operands),
        out_specs=WHOLE,
        scratch_shapes=[pltpu.VMEM((n, 2 * width, 2 * columns), jnp.bfloat16)],
        compiler_params=params(),
        cost_estimate=product_cost(pieces, rows),
    )(*operands)


def recurrence_step(coefficients, total, pieces, vectors, rest, current, previous, at):
    rest_pieces, rest_vectors = rest
    counts = (len(pieces), len(vectors), len(rest_pieces), len(rest_vectors))
    n = len(pieces)
    half, (width, columns) = current[at].shape[0], vectors[0].shape

    def kernel(coefficient_ref, *refs):
        groups = []
        for count in counts:
            groups.append(refs[:count])
            refs = refs[count:]
        piece_refs, vector_refs, rest_piece_refs, rest_vector_refs = groups
        total_ref, refs = (refs[0], refs[1:]) if total is not None else (None, refs)
        current_ref, refs = refs[0], refs[1:]
        previous_ref, refs = (refs[0], refs[1:]) if previous else (None, refs)
        out_ref, stacked_ref, sum_ref = refs
        tiles = [(own, slice(at * half + own.start, at * half + own.stop)) for own in row_tiles(half)]
        if rest_pieces:

            @pl.when(jnp.logical_not(starts_late()))
            def _():
                for term in range(len(rest_vectors)):
                    stack_vectors(stacked_ref, term, rest_vector_refs[term][...])
                for own, tile in tiles:
                    sum_ref[own, :] = total_ref[tile, :] + product_tile(rest_piece_refs, stacked_ref, tile, columns)

            @pl.when(starts_late())
            def _():
                for own, tile in tiles:
                    sum_ref[own, :] = total_ref[tile, :]

        for term in range(n):
            stack_vectors(stacked_ref, term, vector_refs[term][...])
        centre, inverse_radius = coefficient_ref[0:1, :columns], coefficient_ref[1:2, :columns]
        for own, tile in tiles:
            value = product_tile(piece_refs, stacked_ref, tile, columns)
            if rest_pieces:
                value = value + sum_ref[own, :]
            elif total_ref is not None:
                value = value + total_ref[tile, :]
            value = (value - centre * current_ref[own, :]) * inverse_radius
            if previous_ref is not None:
                value = 2.0 * value - previous_ref[own, :]
            out_ref[own, :] = value

    operands = [*pieces, *vectors, *rest_pieces, *rest_vectors] + ([] if total is None else [total])
    operands += [current[at]] + ([previous[at]] if previous else [])
    return pl.pallas_call(
        kernel,
        out_shape=jax.ShapeDtypeStruct((half, columns), jnp.float32),
        in_specs=[WHOLE] * (1 + len(operands)),
        out_specs=WHOLE,
        scratch_shapes=[
            pltpu.VMEM((n, 2 * width, 2 * columns), jnp.bfloat16),
            pltpu.VMEM((half, columns), jnp.float32),
        ],
        compiler_params=params(),
        cost_estimate=product_cost(pieces, half),
    )(coefficients, *operands)


def dot_high(left_side, right_side, contract):
    return lax.dot_general(
        left_side, right_side, (contract, ((), ())), precision=HIGHEST, preferred_element_type=jnp.float32
    )


def tree_sum(values):
    while len(values) > 1:
        values = [values[at] + values[at + 1] for at in range(0, len(values), 2)]
    return values[0]


def gram_of(halves, n):
    def kernel(*refs):
        *in_refs, out_ref = refs
        total = None
        for ref in in_refs:
            term = dot_high(ref[...], ref[...], ((0,), (0,)))
            total = term if total is None else total + term
        for at in range(n):
            out_ref[at] = total

    columns = halves[0].shape[1]
    return pl.pallas_call(
        kernel,
        out_shape=jax.ShapeDtypeStruct((n, columns, columns), jnp.float32),
        in_specs=[WHOLE] * len(halves),
        out_specs=WHOLE,
        compiler_params=params(),
    )(*halves)


def three_parts(values):
    high = values.astype(jnp.bfloat16)
    return (high, *high_low(values - high.astype(jnp.float32)))


def dot_thin(left_side, right_side):
    a, b = three_parts(left_side), three_parts(right_side)
    pairs = [(a[0], b[0]), (a[0], b[1]), (a[1], b[0]), (a[1], b[1]), (a[0], b[2]), (a[2], b[0])]
    return lax.dot_general(
        jnp.concatenate([pair[0].astype(jnp.float32) for pair in pairs], axis=0).T.astype(jnp.bfloat16),
        jnp.concatenate([pair[1].astype(jnp.float32) for pair in pairs], axis=0).astype(jnp.bfloat16),
        (((1,), (0,)), ((), ())),
        preferred_element_type=jnp.float32,
    )


def inverse_cholesky(terms, after=()):
    columns = terms.shape[-1]
    high = 8

    def kernel(*refs):
        terms_ref, (out_ref, gram_ref, inverse_ref) = refs[0], refs[-3:]
        gram_ref[...] = tree_sum([terms_ref[at] for at in range(terms_ref.shape[0])])
        row_at = lax.broadcasted_iota(jnp.int32, (columns, columns), 0)
        column_at = lax.broadcasted_iota(jnp.int32, (columns, columns), 1)
        inverse_ref[...] = jnp.where(row_at == column_at, 1.0, 0.0)
        sub_row = lax.broadcasted_iota(jnp.int32, (high, columns), 0)
        for start in range(0, columns, high):
            stop = start + high
            own, inverse = gram_ref[start:stop, :], inverse_ref[start:stop, :]
            spread = [
                jnp.broadcast_to(own[:, start + at : start + at + 1], (high, columns)) for at in range(high)
            ]
            pivots = jnp.ones((high, columns), jnp.float32)
            reciprocals = jnp.ones((high, columns), jnp.float32)
            for at in range(high):
                pivot = jnp.broadcast_to(spread[at][at : at + 1, :], (high, columns))
                reciprocal = 1.0 / pivot
                pivots = jnp.where(sub_row == at, pivot, pivots)
                reciprocals = jnp.where(sub_row == at, reciprocal, reciprocals)
                if at + 1 == high:
                    break
                factor = jnp.where(sub_row > at, spread[at], 0.0) * reciprocal
                for later in range(at + 1, high):
                    spread[later] = spread[later] - factor * spread[later][at : at + 1, :]
                own = own - factor * own[at : at + 1, :]
                inverse = inverse - factor * inverse[at : at + 1, :]
            inverse_ref[start:stop, :] = inverse / jnp.sqrt(pivots)
            if stop < columns:
                update = dot_thin(own * reciprocals, jnp.concatenate([own, inverse], axis=1))
                gram_ref[stop:, :] = gram_ref[stop:, :] - update[stop:, :columns]
                inverse_ref[stop:, :] = inverse_ref[stop:, :] - update[stop:, columns:]
        out_ref[...] = inverse_ref[...].T

    return pl.pallas_call(
        kernel,
        out_shape=jax.ShapeDtypeStruct((columns, columns), jnp.float32),
        in_specs=[WHOLE] + [ANYWHERE] * len(after),
        out_specs=WHOLE,
        scratch_shapes=[pltpu.VMEM((columns, columns), jnp.float32)] * 2,
        compiler_params=params(),
        cost_estimate=pl.CostEstimate(flops=25 * 10**9, bytes_accessed=0, transcendentals=0),
    )(terms, *after)


def two_parts(values):
    return jnp.concatenate(high_low(values), axis=1)


def dot_parts(left_side, right_side):
    columns = right_side.shape[1]
    right_parts = two_parts(right_side)
    product = jnp.dot(
        two_parts(left_side),
        jnp.concatenate([right_parts, right_parts], axis=0),
        preferred_element_type=jnp.float32,
    )
    return product[:, :columns] + product[:, columns:]


def times_right(halves, right_side, transposed=False):
    def kernel(right_ref, *refs):
        in_refs, (out_ref, *parts_ref) = refs[: len(halves)], refs[len(halves) :]
        at = 0
        for ref in in_refs:
            for tile in row_tiles(ref.shape[0]):
                own = slice(at + tile.start, at + tile.stop)
                value = dot_parts(ref[tile, :], right_ref[...])
                out_ref[own, :] = value
                if transposed:
                    parts_ref[0][:, own] = two_parts(value).T
            at += ref.shape[0]

    rows, columns = sum(half.shape[0] for half in halves), halves[0].shape[1]
    out_shape = [jax.ShapeDtypeStruct((rows, columns), jnp.float32)]
    if transposed:
        out_shape.append(jax.ShapeDtypeStruct((2 * columns, rows), jnp.bfloat16))
    return pl.pallas_call(
        kernel,
        out_shape=out_shape,
        in_specs=[WHOLE] * (1 + len(halves)),
        out_specs=[WHOLE] * len(out_shape),
        compiler_params=params(),
        cost_estimate=pl.CostEstimate(flops=2 * rows * 256 * 256, bytes_accessed=0, transcendentals=0),
    )(right_side, *halves)


def image_and_projected(total, pieces, vectors, inverse_upper, basis_parts, copies):
    n = len(pieces)
    rows, (width, columns) = pieces[0].shape[0], vectors[0].shape

    def kernel(*refs):
        piece_refs, refs = refs[:n], refs[n:]
        vector_refs, refs = refs[:n], refs[n:]
        total_ref, refs = (refs[0], refs[1:]) if total is not None else (None, refs)
        inverse_ref, basis_ref, image_ref, projected_ref, stacked_ref = refs
        for at in range(n):
            stack_vectors(stacked_ref, at, vector_refs[at][...])
        projected = None
        for tile in row_tiles(rows):
            image = product_tile(piece_refs, stacked_ref, tile, columns)
            if total_ref is not None:
                image = image + total_ref[tile, :]
            image_ref[tile, :] = image
            term = jnp.dot(basis_ref[:, tile], two_parts(image), preferred_element_type=jnp.float32)
            projected = term if projected is None else projected + term
        projected = projected[:columns, :] + projected[columns:, :]
        projected = projected[:, :columns] + projected[:, columns:]
        projected = dot_parts(projected, inverse_ref[...])
        for at in range(copies):
            projected_ref[at] = projected

    operands = [*pieces, *vectors] + ([] if total is None else [total]) + [inverse_upper, basis_parts]
    return pl.pallas_call(
        kernel,
        out_shape=[
            jax.ShapeDtypeStruct((rows, columns), jnp.float32),
            jax.ShapeDtypeStruct((copies, columns, columns), jnp.float32),
        ],
        in_specs=[WHOLE] * len(operands),
        out_specs=[WHOLE] * 2,
        scratch_shapes=[pltpu.VMEM((n, 2 * width, 2 * columns), jnp.bfloat16)],
        compiler_params=params(),
        cost_estimate=product_cost(pieces, rows),
    )(*operands)


def residual_of(mapped, basis_rows, terms):
    def kernel(mapped_ref, basis_ref, terms_ref, projected_ref, residual_ref):
        projected = tree_sum([terms_ref[at] for at in range(terms_ref.shape[0])])
        projected_ref[...] = projected
        for tile in row_tiles(mapped.shape[0]):
            residual_ref[tile, :] = mapped_ref[tile, :] - dot_parts(basis_ref[tile, :], projected)

    return pl.pallas_call(
        kernel,
        out_shape=[
            jax.ShapeDtypeStruct(terms.shape[1:], jnp.float32),
            jax.ShapeDtypeStruct(mapped.shape, jnp.float32),
        ],
        in_specs=[WHOLE] * 3,
        out_specs=[WHOLE] * 2,
        compiler_params=params(),
    )(mapped, basis_rows, terms)


def exchange(value, offset, n):
    return lax.ppermute(value, "blk", [(at, at ^ offset) for at in range(n)])


def local(n, factor, initial, bounds):
    rows, columns = initial.shape
    half = rows // 2
    halves_at = range(2)
    coefficients = recurrence_coefficients(bounds, columns)
    first, early = first_vectors(factor, initial, n)
    pieces = split_factor(factor, early, n)

    if n == 4:
        own, along_x, along_y, across = pieces

        def gather_product(halves, put_off):
            top, bottom = halves
            x_top, y_bottom = exchange(top, 1, n), exchange(bottom, 2, n)
            x_bottom, y_top = exchange(bottom, 1, n), exchange(top, 2, n)
            xy_top, xy_bottom = exchange(x_top, 2, n), exchange(y_bottom, 1, n)
            total = partial_product(None, own, halves)
            total = partial_product(total, [along_x[0], along_y[1]], [x_top, y_bottom])
            middle = [along_x[1], along_y[0]], [x_bottom, y_top]
            total = partial_product(total, *middle, put_off=put_off)
            return (total, across, [xy_top, xy_bottom]), middle if put_off else ((), ()), (x_top, y_bottom)

        def all_terms(copies):
            return lax.all_to_all(copies, "blk", 0, 0)
    else:

        def gather_product(halves, put_off):
            gathered, me = lax.all_gather(jnp.concatenate(halves), "blk"), lax.axis_index("blk")
            blocks = [gathered[jnp.bitwise_xor(me, offset)] for offset in range(n)]
            vectors = [block[at * half : (at + 1) * half] for block in blocks for at in halves_at]
            return (None, [piece for pair in pieces for piece in pair], vectors), ((), ()), ()

        def all_terms(copies):
            return lax.all_gather(copies[0], "blk")

    previous, current = None, first
    for order_step in range(DEGREE):
        product, rest, _ = gather_product(current, True)
        following = [recurrence_step(coefficients, *product, rest, current, previous, at) for at in halves_at]
        previous, current = current, following

    gram_terms = all_terms(gram_of(current, n))
    product, _, arrived = gather_product(current, False)
    inverse_upper = inverse_cholesky(gram_terms, after=arrived)
    basis_rows, basis_parts = times_right(current, inverse_upper, transposed=True)
    image, projected_term = image_and_projected(*product, inverse_upper, basis_parts, n)
    projected_terms = all_terms(projected_term)
    (mapped,) = times_right([image], inverse_upper)
    projected, residual = residual_of(mapped, basis_rows, projected_terms)
    return (basis_rows, projected, residual)


def solution(mesh):
    in_specs = (P(("bulk", "blk"), None), P(("bulk", "blk"), None), P("bulk"))
    out_specs = (P(("bulk", "blk"), None), P("bulk", None), P(("bulk", "blk"), None))
    return jax.shard_map(
        functools.partial(local, mesh.shape["blk"]),
        mesh=mesh,
        in_specs=in_specs,
        out_specs=out_specs,
        check_vma=False,
    )
```

```python
import functools

import jax
import jax.numpy as jnp
from jax import lax
from jax.experimental import pallas as pl
from jax.experimental.pallas import tpu as pltpu
from jax.sharding import PartitionSpec as P

DEGREE = 8
HIGHEST = lax.Precision.HIGHEST
WHOLE = pl.BlockSpec(memory_space=pltpu.VMEM)
ANYWHERE = pl.BlockSpec(memory_space=pl.ANY)
HBM = pl.BlockSpec(memory_space=pltpu.HBM)
SCALARS = pl.BlockSpec(memory_space=pltpu.SMEM)
VMEM_LIMIT = 16 * 2**20


def params():
    return pltpu.CompilerParams(vmem_limit_bytes=VMEM_LIMIT)


def high_low(values):
    high = values.astype(jnp.bfloat16)
    low = (values - high.astype(jnp.float32)).astype(jnp.bfloat16)
    return high, low


def split_factor(factor, n, offsets, after=()):
    rows, order = factor.shape
    width, count = order // (2 * n), 2 * len(offsets)

    def kernel(factor_ref, *refs):
        out_refs, (slots, arrived) = refs[len(after) : len(after) + count], refs[-2:]
        me = lax.axis_index("blk")

        def fetch(at):
            owner = jnp.bitwise_xor(me, offsets[at // 2])
            start = pl.multiple_of((2 * owner + at % 2) * width, width)
            return pltpu.make_async_copy(
                factor_ref.at[:, pl.ds(start, width)], slots.at[at % 3], arrived.at[at % 3]
            )

        fetch(0).start()
        fetch(1).start()
        for at in range(count):
            if at + 2 < count:
                fetch(at + 2).start()
            fetch(at).wait()

            @pl.loop(0, rows // 64)
            def _(tile):
                own = pl.ds(pl.multiple_of(tile * 64, 64), 64)
                high, low = high_low(slots[at % 3, own, :])
                out_refs[at][own, :width] = high
                out_refs[at][own, width:] = low

    pieces = pl.pallas_call(
        kernel,
        out_shape=[jax.ShapeDtypeStruct((rows, 2 * width), jnp.bfloat16)] * count,
        in_specs=[HBM] + [ANYWHERE] * len(after),
        out_specs=[WHOLE] * count,
        scratch_shapes=[pltpu.VMEM((3, rows, width), jnp.float32), pltpu.SemaphoreType.DMA((3,))],
        compiler_params=pltpu.CompilerParams(vmem_limit_bytes=40 * 2**20),
        cost_estimate=pl.CostEstimate(flops=0, bytes_accessed=8 * count * rows * width, transcendentals=0),
    )(factor, *after)
    return [pieces[2 * at : 2 * at + 2] for at in range(len(offsets))]


def recurrence_coefficients(bounds, columns):
    def kernel(bounds_ref, out_ref):
        centre = (bounds_ref[0] + bounds_ref[1]) / 2.0
        radius = (bounds_ref[1] - bounds_ref[0]) / 2.0
        out_ref[0:1, :] = jnp.full((1, columns), centre, jnp.float32)
        out_ref[1:2, :] = 1.0 / jnp.full((1, columns), radius, jnp.float32)

    return pl.pallas_call(
        kernel,
        out_shape=jax.ShapeDtypeStruct((2, columns), jnp.float32),
        in_specs=[SCALARS],
        out_specs=WHOLE,
        compiler_params=params(),
    )(bounds)


def stack_vectors(stacked_ref, at, vectors):
    width, columns = vectors.shape
    high, low = high_low(vectors)
    for start in (0, width):
        stacked_ref[at, start : start + width, :columns] = high
        stacked_ref[at, start : start + width, columns:] = low


def stack_all(stacked_ref, vector_refs):
    width, at = stacked_ref.shape[1] // 2, 0
    for ref in vector_refs:
        for start in range(0, ref.shape[0], width):
            stack_vectors(stacked_ref, at, ref[start : start + width, :])
            at += 1


def product_tile(pieces, stacked_ref, rows, columns):
    total = None
    for at, piece in enumerate(pieces):
        term = jnp.dot(piece[rows, :], stacked_ref[at], preferred_element_type=jnp.float32)
        total = term if total is None else total + term
    return total[:, :columns] + total[:, columns:]


def row_tiles(rows):
    tile = min(rows, 256)
    return [slice(start, start + tile) for start in range(0, rows, tile)]


def product_cost(pieces, rows):
    doubled = pieces[0].shape[1]
    return pl.CostEstimate(
        flops=2 * rows * doubled * 256 * len(pieces),
        bytes_accessed=2 * rows * doubled * len(pieces),
        transcendentals=0,
    )


def partial_product(total, pieces, vectors):
    n, m = len(pieces), len(vectors)
    (rows, doubled), columns = pieces[0].shape, vectors[0].shape[1]

    def kernel(*refs):
        piece_refs, vector_refs = refs[:n], refs[n : n + m]
        total_ref = refs[n + m] if total is not None else None
        out_ref, stacked_ref = refs[-2:]
        stack_all(stacked_ref, vector_refs)
        for tile in row_tiles(rows):
            value = product_tile(piece_refs, stacked_ref, tile, columns)
            out_ref[tile, :] = value if total_ref is None else total_ref[tile, :] + value

    operands = [*pieces, *vectors] + ([] if total is None else [total])
    return pl.pallas_call(
        kernel,
        out_shape=jax.ShapeDtypeStruct((rows, columns), jnp.float32),
        in_specs=[WHOLE] * len(operands),
        out_specs=WHOLE,
        scratch_shapes=[pltpu.VMEM((n, doubled, 2 * columns), jnp.bfloat16)],
        compiler_params=params(),
        cost_estimate=product_cost(pieces, rows),
    )(*operands)


def recurrence_step(coefficients, total, pieces, vectors, current, previous, whole):
    n, m = len(pieces), len(vectors)
    half, columns = current[0].shape
    doubled = pieces[0].shape[1]

    def kernel(coefficient_ref, *refs):
        piece_refs, refs = refs[:n], refs[n:]
        vector_refs, refs = refs[:m], refs[m:]
        total_ref, refs = (refs[0], refs[1:]) if total is not None else (None, refs)
        current_refs, refs = refs[:2], refs[2:]
        previous_refs, refs = (refs[:2], refs[2:]) if previous else (None, refs)
        *out_refs, stacked_ref = refs
        stack_all(stacked_ref, vector_refs)
        centre, inverse_radius = coefficient_ref[0:1, :columns], coefficient_ref[1:2, :columns]
        for at in (1, 0):
            for own in row_tiles(half):
                tile = slice(at * half + own.start, at * half + own.stop)
                value = product_tile(piece_refs, stacked_ref, tile, columns)
                if total_ref is not None:
                    value = value + total_ref[tile, :]
                value = (value - centre * current_refs[at][own, :]) * inverse_radius
                if previous_refs is not None:
                    value = 2.0 * value - previous_refs[at][own, :]
                if whole:
                    out_refs[0][tile, :] = value
                else:
                    out_refs[at][own, :] = value

    operands = [*pieces, *vectors] + ([] if total is None else [total])
    operands += [*current, *(previous or ())]
    out_shape = [jax.ShapeDtypeStruct((2 * half if whole else half, columns), jnp.float32)] * (1 if whole else 2)
    return pl.pallas_call(
        kernel,
        out_shape=out_shape,
        in_specs=[WHOLE] * (1 + len(operands)),
        out_specs=[WHOLE] * len(out_shape),
        scratch_shapes=[pltpu.VMEM((n, doubled, 2 * columns), jnp.bfloat16)],
        compiler_params=params(),
        cost_estimate=product_cost(pieces, 2 * half),
    )(coefficients, *operands)


def rows_of(block, start, stop):
    def kernel(block_ref, out_ref):
        out_ref[...] = block_ref[start:stop, :]

    return pl.pallas_call(
        kernel,
        out_shape=jax.ShapeDtypeStruct((stop - start, block.shape[1]), block.dtype),
        in_specs=[WHOLE],
        out_specs=WHOLE,
        compiler_params=params(),
        cost_estimate=pl.CostEstimate(flops=0, bytes_accessed=0, transcendentals=0),
    )(block)


def dot_high(left_side, right_side, contract):
    return lax.dot_general(
        left_side, right_side, (contract, ((), ())), precision=HIGHEST, preferred_element_type=jnp.float32
    )


def tree_sum(values):
    while len(values) > 1:
        values = [values[at] + values[at + 1] for at in range(0, len(values), 2)]
    return values[0]


def gram_of(halves):
    def kernel(*refs):
        *in_refs, out_ref = refs
        total = None
        for ref in in_refs:
            term = dot_high(ref[...], ref[...], ((0,), (0,)))
            total = term if total is None else total + term
        out_ref[...] = total

    columns = halves[0].shape[1]
    return pl.pallas_call(
        kernel,
        out_shape=jax.ShapeDtypeStruct((columns, columns), jnp.float32),
        in_specs=[WHOLE] * len(halves),
        out_specs=WHOLE,
        compiler_params=params(),
    )(*halves)


def three_parts(values):
    high = values.astype(jnp.bfloat16)
    return (high, *high_low(values - high.astype(jnp.float32)))


def dot_thin(left_side, right_side):
    a, b = three_parts(left_side), three_parts(right_side)
    pairs = [(a[0], b[0]), (a[0], b[1]), (a[1], b[0]), (a[1], b[1]), (a[0], b[2]), (a[2], b[0])]
    return lax.dot_general(
        jnp.concatenate([pair[0].astype(jnp.float32) for pair in pairs], axis=0).T.astype(jnp.bfloat16),
        jnp.concatenate([pair[1].astype(jnp.float32) for pair in pairs], axis=0).astype(jnp.bfloat16),
        (((1,), (0,)), ((), ())),
        preferred_element_type=jnp.float32,
    )


def inverse_cholesky(terms):
    columns = terms[0].shape[0]
    high = 16

    def kernel(*refs):
        *term_refs, out_ref, gram_ref, inverse_ref = refs
        gram_ref[...] = tree_sum([ref[...] for ref in term_refs])
        row_at = lax.broadcasted_iota(jnp.int32, (columns, columns), 0)
        column_at = lax.broadcasted_iota(jnp.int32, (columns, columns), 1)
        inverse_ref[...] = jnp.where(row_at == column_at, 1.0, 0.0)
        sub_row = lax.broadcasted_iota(jnp.int32, (high, columns), 0)
        for start in range(0, columns, high):
            stop = start + high
            own, inverse = gram_ref[start:stop, :], inverse_ref[start:stop, :]
            spread = [
                jnp.broadcast_to(own[:, start + at : start + at + 1], (high, columns)) for at in range(high)
            ]
            pivots = jnp.ones((high, columns), jnp.float32)
            reciprocals = jnp.ones((high, columns), jnp.float32)
            for at in range(high):
                pivot = jnp.broadcast_to(spread[at][at : at + 1, :], (high, columns))
                reciprocal = 1.0 / pivot
                pivots = jnp.where(sub_row == at, pivot, pivots)
                reciprocals = jnp.where(sub_row == at, reciprocal, reciprocals)
                if at + 1 == high:
                    break
                factor = jnp.where(sub_row > at, spread[at], 0.0) * reciprocal
                for later in range(at + 1, high):
                    spread[later] = spread[later] - factor * spread[later][at : at + 1, :]
                own = own - factor * own[at : at + 1, :]
                inverse = inverse - factor * inverse[at : at + 1, :]
            inverse_ref[start:stop, :] = inverse / jnp.sqrt(pivots)
            if stop < columns:
                update = dot_thin(own * reciprocals, jnp.concatenate([own, inverse], axis=1))
                gram_ref[stop:, :] = gram_ref[stop:, :] - update[stop:, :columns]
                inverse_ref[stop:, :] = inverse_ref[stop:, :] - update[stop:, columns:]
        out_ref[...] = inverse_ref[...].T

    return pl.pallas_call(
        kernel,
        out_shape=jax.ShapeDtypeStruct((columns, columns), jnp.float32),
        in_specs=[WHOLE] * len(terms),
        out_specs=WHOLE,
        scratch_shapes=[pltpu.VMEM((columns, columns), jnp.float32)] * 2,
        compiler_params=params(),
        cost_estimate=pl.CostEstimate(flops=25 * 10**9, bytes_accessed=0, transcendentals=0),
    )(*terms)


def two_parts(values):
    return jnp.concatenate(high_low(values), axis=1)


def dot_parts(left_side, right_side):
    columns = right_side.shape[1]
    right_parts = two_parts(right_side)
    product = jnp.dot(
        two_parts(left_side),
        jnp.concatenate([right_parts, right_parts], axis=0),
        preferred_element_type=jnp.float32,
    )
    return product[:, :columns] + product[:, columns:]


def times_right(halves, right_side, transposed=False):
    def kernel(right_ref, *refs):
        in_refs, (out_ref, *parts_ref) = refs[: len(halves)], refs[len(halves) :]
        at = 0
        for ref in in_refs:
            for tile in row_tiles(ref.shape[0]):
                own = slice(at + tile.start, at + tile.stop)
                value = dot_parts(ref[tile, :], right_ref[...])
                out_ref[own, :] = value
                if transposed:
                    parts_ref[0][:, own] = two_parts(value).T
            at += ref.shape[0]

    rows, columns = sum(half.shape[0] for half in halves), halves[0].shape[1]
    out_shape = [jax.ShapeDtypeStruct((rows, columns), jnp.float32)]
    if transposed:
        out_shape.append(jax.ShapeDtypeStruct((2 * columns, rows), jnp.bfloat16))
    return pl.pallas_call(
        kernel,
        out_shape=out_shape,
        in_specs=[WHOLE] * (1 + len(halves)),
        out_specs=[WHOLE] * len(out_shape),
        compiler_params=params(),
        cost_estimate=pl.CostEstimate(flops=2 * rows * 256 * 256, bytes_accessed=0, transcendentals=0),
    )(right_side, *halves)


def image_and_projected(total, pieces, vectors, inverse_upper, basis_parts):
    n, m = len(pieces), len(vectors)
    (rows, doubled), columns = pieces[0].shape, vectors[0].shape[1]

    def kernel(*refs):
        piece_refs, refs = refs[:n], refs[n:]
        vector_refs, refs = refs[:m], refs[m:]
        total_ref, refs = (refs[0], refs[1:]) if total is not None else (None, refs)
        inverse_ref, basis_ref, image_ref, projected_ref, stacked_ref = refs
        stack_all(stacked_ref, vector_refs)
        projected = None
        for tile in row_tiles(rows):
            image = product_tile(piece_refs, stacked_ref, tile, columns)
            if total_ref is not None:
                image = image + total_ref[tile, :]
            image_ref[tile, :] = image
            term = jnp.dot(basis_ref[:, tile], two_parts(image), preferred_element_type=jnp.float32)
            projected = term if projected is None else projected + term
        projected = projected[:columns, :] + projected[columns:, :]
        projected = projected[:, :columns] + projected[:, columns:]
        projected_ref[...] = dot_parts(projected, inverse_ref[...])

    operands = [*pieces, *vectors] + ([] if total is None else [total]) + [inverse_upper, basis_parts]
    return pl.pallas_call(
        kernel,
        out_shape=[
            jax.ShapeDtypeStruct((rows, columns), jnp.float32),
            jax.ShapeDtypeStruct((columns, columns), jnp.float32),
        ],
        in_specs=[WHOLE] * len(operands),
        out_specs=[WHOLE] * 2,
        scratch_shapes=[pltpu.VMEM((n, doubled, 2 * columns), jnp.bfloat16)],
        compiler_params=params(),
        cost_estimate=product_cost(pieces, rows),
    )(*operands)


def residual_of(mapped, basis_rows, terms):
    def kernel(mapped_ref, basis_ref, *refs):
        *term_refs, projected_ref, residual_ref = refs
        projected = tree_sum([ref[...] for ref in term_refs])
        projected_ref[...] = projected
        for tile in row_tiles(mapped.shape[0]):
            residual_ref[tile, :] = mapped_ref[tile, :] - dot_parts(basis_ref[tile, :], projected)

    return pl.pallas_call(
        kernel,
        out_shape=[
            jax.ShapeDtypeStruct(terms[0].shape, jnp.float32),
            jax.ShapeDtypeStruct(mapped.shape, jnp.float32),
        ],
        in_specs=[WHOLE] * (2 + len(terms)),
        out_specs=[WHOLE] * 2,
        compiler_params=params(),
    )(mapped, basis_rows, *terms)


def exchange(value, offset, n):
    return lax.ppermute(value, "blk", [(at, at ^ offset) for at in range(n)])


def local(n, factor, initial, bounds):
    rows, columns = initial.shape
    half = rows // 2
    coefficients = recurrence_coefficients(bounds, columns)

    if n == 4:
        own, along_x = split_factor(factor, n, (0, 1))
        rest = []

        def gather_product(halves):
            top, bottom = halves
            x_top = exchange(top, 1, n)
            y_bottom, x_bottom, y_top = exchange(bottom, 2, n), exchange(bottom, 1, n), exchange(top, 2, n)
            xy_top, xy_bottom = exchange(x_top, 2, n), exchange(y_bottom, 1, n)
            if not rest:
                rest.extend(split_factor(factor, n, (2, 3), after=(x_top, y_bottom)))
            along_y, across = rest
            total = partial_product(None, own, halves)
            total = partial_product(total, [along_x[0], along_y[1]], [x_top, y_bottom])
            total = partial_product(total, [along_x[1], along_y[0]], [x_bottom, y_top])
            return total, across, [xy_top, xy_bottom]

        def gather_whole(block):
            by_x, by_y = exchange(block, 1, n), exchange(block, 2, n)
            xy_top = exchange(rows_of(by_x, 0, half), 2, n)
            xy_bottom = exchange(rows_of(by_y, half, rows), 1, n)
            along_y, across = rest
            total = partial_product(None, own, [block])
            total = partial_product(total, [*along_x, *along_y], [by_x, by_y])
            return total, across, [xy_top, xy_bottom]

        def all_terms(term):
            return [term] + [exchange(term, offset, n) for offset in (1, 2, 3)]
    else:
        pieces = [piece for pair in split_factor(factor, n, range(n)) for piece in pair]

        def all_terms(value):
            gathered = lax.all_gather(value, "blk")
            me = lax.axis_index("blk")
            return [gathered[jnp.bitwise_xor(me, offset)] for offset in range(n)]

        def gather_product(halves):
            return gather_whole(jnp.concatenate(halves))

        def gather_whole(block):
            return None, pieces, all_terms(block)

    previous, current = None, [initial[:half], initial[half:]]
    for order_step in range(DEGREE):
        product, last = gather_product(current), order_step == DEGREE - 1
        previous, current = current, recurrence_step(coefficients, *product, current, previous, last)
    (filtered,) = current

    inverse_upper = inverse_cholesky(all_terms(gram_of([filtered])))
    basis_rows, basis_parts = times_right([filtered], inverse_upper, transposed=True)
    image, projected_term = image_and_projected(*gather_whole(filtered), inverse_upper, basis_parts)
    projected_terms = all_terms(projected_term)
    (mapped,) = times_right([image], inverse_upper)
    projected, residual = residual_of(mapped, basis_rows, projected_terms)
    return (basis_rows, projected, residual)


def solution(mesh):
    in_specs = (P(("bulk", "blk"), None), P(("bulk", "blk"), None), P("bulk"))
    out_specs = (P(("bulk", "blk"), None), P("bulk", None), P(("bulk", "blk"), None))
    return jax.shard_map(
        functools.partial(local, mesh.shape["blk"]),
        mesh=mesh,
        in_specs=in_specs,
        out_specs=out_specs,
        check_vma=False,
    )
```

```python
import functools

import jax
import jax.numpy as jnp
from jax import lax
from jax.experimental import pallas as pl
from jax.experimental.pallas import tpu as pltpu
from jax.sharding import PartitionSpec as P

DEGREE = 8
HIGHEST = lax.Precision.HIGHEST
WHOLE = pl.BlockSpec(memory_space=pltpu.VMEM)
ANYWHERE = pl.BlockSpec(memory_space=pl.ANY)
HBM = pl.BlockSpec(memory_space=pltpu.HBM)
SCALARS = pl.BlockSpec(memory_space=pltpu.SMEM)
VMEM_LIMIT = 16 * 2**20


def params():
    return pltpu.CompilerParams(vmem_limit_bytes=VMEM_LIMIT)


def high_low(values):
    high = values.astype(jnp.bfloat16)
    low = (values - high.astype(jnp.float32)).astype(jnp.bfloat16)
    return high, low


def split_factor(factor, n, offsets, after=()):
    rows, order = factor.shape
    width, count = order // (2 * n), 2 * len(offsets)

    def kernel(factor_ref, *refs):
        out_refs, (slots, arrived) = refs[len(after) : len(after) + count], refs[-2:]
        me = lax.axis_index("blk")

        def fetch(at):
            owner = jnp.bitwise_xor(me, offsets[at // 2])
            start = pl.multiple_of((2 * owner + at % 2) * width, width)
            return pltpu.make_async_copy(
                factor_ref.at[:, pl.ds(start, width)], slots.at[at % 3], arrived.at[at % 3]
            )

        fetch(0).start()
        fetch(1).start()
        for at in range(count):
            if at + 2 < count:
                fetch(at + 2).start()
            fetch(at).wait()

            @pl.loop(0, rows // 64)
            def _(tile):
                own = pl.ds(pl.multiple_of(tile * 64, 64), 64)
                high, low = high_low(slots[at % 3, own, :])
                out_refs[at][own, :width] = high
                out_refs[at][own, width:] = low

    pieces = pl.pallas_call(
        kernel,
        out_shape=[jax.ShapeDtypeStruct((rows, 2 * width), jnp.bfloat16)] * count,
        in_specs=[HBM] + [ANYWHERE] * len(after),
        out_specs=[WHOLE] * count,
        scratch_shapes=[pltpu.VMEM((3, rows, width), jnp.float32), pltpu.SemaphoreType.DMA((3,))],
        compiler_params=pltpu.CompilerParams(vmem_limit_bytes=40 * 2**20),
        cost_estimate=pl.CostEstimate(flops=0, bytes_accessed=8 * count * rows * width, transcendentals=0),
    )(factor, *after)
    return [pieces[2 * at : 2 * at + 2] for at in range(len(offsets))]


def recurrence_coefficients(bounds, columns):
    def kernel(bounds_ref, out_ref):
        centre = (bounds_ref[0] + bounds_ref[1]) / 2.0
        radius = (bounds_ref[1] - bounds_ref[0]) / 2.0
        out_ref[0:1, :] = jnp.full((1, columns), centre, jnp.float32)
        out_ref[1:2, :] = 1.0 / jnp.full((1, columns), radius, jnp.float32)

    return pl.pallas_call(
        kernel,
        out_shape=jax.ShapeDtypeStruct((2, columns), jnp.float32),
        in_specs=[SCALARS],
        out_specs=WHOLE,
        compiler_params=params(),
    )(bounds)


def stack_vectors(stacked_ref, at, vectors):
    width, columns = vectors.shape
    high, low = high_low(vectors)
    for start in (0, width):
        stacked_ref[at, start : start + width, :columns] = high
        stacked_ref[at, start : start + width, columns:] = low


def stack_all(stacked_ref, vector_refs):
    width, at = stacked_ref.shape[1] // 2, 0
    for ref in vector_refs:
        for start in range(0, ref.shape[0], width):
            stack_vectors(stacked_ref, at, ref[start : start + width, :])
            at += 1


def product_tile(pieces, stacked_ref, rows, columns):
    total = None
    for at, piece in enumerate(pieces):
        term = jnp.dot(piece[rows, :], stacked_ref[at], preferred_element_type=jnp.float32)
        total = term if total is None else total + term
    return total[:, :columns] + total[:, columns:]


def row_tiles(rows):
    tile = min(rows, 256)
    return [slice(start, start + tile) for start in range(0, rows, tile)]


def product_cost(pieces, rows):
    doubled = pieces[0].shape[1]
    return pl.CostEstimate(
        flops=2 * rows * doubled * 256 * len(pieces),
        bytes_accessed=2 * rows * doubled * len(pieces),
        transcendentals=0,
    )


def partial_product(total, pieces, vectors):
    n, m = len(pieces), len(vectors)
    (rows, doubled), columns = pieces[0].shape, vectors[0].shape[1]

    def kernel(*refs):
        piece_refs, vector_refs = refs[:n], refs[n : n + m]
        total_ref = refs[n + m] if total is not None else None
        out_ref, stacked_ref = refs[-2:]
        stack_all(stacked_ref, vector_refs)
        for tile in row_tiles(rows):
            value = product_tile(piece_refs, stacked_ref, tile, columns)
            out_ref[tile, :] = value if total_ref is None else total_ref[tile, :] + value

    operands = [*pieces, *vectors] + ([] if total is None else [total])
    return pl.pallas_call(
        kernel,
        out_shape=jax.ShapeDtypeStruct((rows, columns), jnp.float32),
        in_specs=[WHOLE] * len(operands),
        out_specs=WHOLE,
        scratch_shapes=[pltpu.VMEM((n, doubled, 2 * columns), jnp.bfloat16)],
        compiler_params=params(),
        cost_estimate=product_cost(pieces, rows),
    )(*operands)


def recurrence_step(coefficients, total, pieces, vectors, current, previous):
    n, m = len(pieces), len(vectors)
    half, columns = current[0].shape
    doubled = pieces[0].shape[1]

    def kernel(coefficient_ref, *refs):
        piece_refs, refs = refs[:n], refs[n:]
        vector_refs, refs = refs[:m], refs[m:]
        total_ref, refs = (refs[0], refs[1:]) if total is not None else (None, refs)
        current_refs, refs = refs[:2], refs[2:]
        previous_refs, refs = (refs[:2], refs[2:]) if previous else (None, refs)
        *out_refs, stacked_ref = refs
        stack_all(stacked_ref, vector_refs)
        centre, inverse_radius = coefficient_ref[0:1, :columns], coefficient_ref[1:2, :columns]
        for at in (1, 0):
            for own in row_tiles(half):
                tile = slice(at * half + own.start, at * half + own.stop)
                value = product_tile(piece_refs, stacked_ref, tile, columns)
                if total_ref is not None:
                    value = value + total_ref[tile, :]
                value = (value - centre * current_refs[at][own, :]) * inverse_radius
                if previous_refs is not None:
                    value = 2.0 * value - previous_refs[at][own, :]
                out_refs[at][own, :] = value

    operands = [*pieces, *vectors] + ([] if total is None else [total])
    operands += [*current, *(previous or ())]
    return pl.pallas_call(
        kernel,
        out_shape=[jax.ShapeDtypeStruct((half, columns), jnp.float32)] * 2,
        in_specs=[WHOLE] * (1 + len(operands)),
        out_specs=[WHOLE] * 2,
        scratch_shapes=[pltpu.VMEM((n, doubled, 2 * columns), jnp.bfloat16)],
        compiler_params=params(),
        cost_estimate=product_cost(pieces, 2 * half),
    )(coefficients, *operands)


def dot_high(left_side, right_side, contract):
    return lax.dot_general(
        left_side, right_side, (contract, ((), ())), precision=HIGHEST, preferred_element_type=jnp.float32
    )


def tree_sum(values):
    while len(values) > 1:
        values = [values[at] + values[at + 1] for at in range(0, len(values), 2)]
    return values[0]


def gram_of(halves):
    def kernel(*refs):
        *in_refs, out_ref = refs
        total = None
        for ref in in_refs:
            term = dot_high(ref[...], ref[...], ((0,), (0,)))
            total = term if total is None else total + term
        out_ref[...] = total

    columns = halves[0].shape[1]
    return pl.pallas_call(
        kernel,
        out_shape=jax.ShapeDtypeStruct((columns, columns), jnp.float32),
        in_specs=[WHOLE] * len(halves),
        out_specs=WHOLE,
        compiler_params=params(),
    )(*halves)


def three_parts(values):
    high = values.astype(jnp.bfloat16)
    return (high, *high_low(values - high.astype(jnp.float32)))


def dot_thin(left_side, right_side):
    a, b = three_parts(left_side), three_parts(right_side)
    pairs = [(a[0], b[0]), (a[0], b[1]), (a[1], b[0]), (a[1], b[1]), (a[0], b[2]), (a[2], b[0])]
    return lax.dot_general(
        jnp.concatenate([pair[0].astype(jnp.float32) for pair in pairs], axis=0).T.astype(jnp.bfloat16),
        jnp.concatenate([pair[1].astype(jnp.float32) for pair in pairs], axis=0).astype(jnp.bfloat16),
        (((1,), (0,)), ((), ())),
        preferred_element_type=jnp.float32,
    )


def inverse_cholesky(terms, after=()):
    columns = terms[0].shape[0]
    high = 16

    def kernel(*refs):
        term_refs, (out_ref, gram_ref, inverse_ref) = refs[: len(terms)], refs[-3:]
        gram_ref[...] = tree_sum([ref[...] for ref in term_refs])
        row_at = lax.broadcasted_iota(jnp.int32, (columns, columns), 0)
        column_at = lax.broadcasted_iota(jnp.int32, (columns, columns), 1)
        inverse_ref[...] = jnp.where(row_at == column_at, 1.0, 0.0)
        sub_row = lax.broadcasted_iota(jnp.int32, (high, columns), 0)
        for start in range(0, columns, high):
            stop = start + high
            own, inverse = gram_ref[start:stop, :], inverse_ref[start:stop, :]
            spread = [
                jnp.broadcast_to(own[:, start + at : start + at + 1], (high, columns)) for at in range(high)
            ]
            pivots = jnp.ones((high, columns), jnp.float32)
            reciprocals = jnp.ones((high, columns), jnp.float32)
            for at in range(high):
                pivot = jnp.broadcast_to(spread[at][at : at + 1, :], (high, columns))
                reciprocal = 1.0 / pivot
                pivots = jnp.where(sub_row == at, pivot, pivots)
                reciprocals = jnp.where(sub_row == at, reciprocal, reciprocals)
                if at + 1 == high:
                    break
                factor = jnp.where(sub_row > at, spread[at], 0.0) * reciprocal
                for later in range(at + 1, high):
                    spread[later] = spread[later] - factor * spread[later][at : at + 1, :]
                own = own - factor * own[at : at + 1, :]
                inverse = inverse - factor * inverse[at : at + 1, :]
            inverse_ref[start:stop, :] = inverse / jnp.sqrt(pivots)
            if stop < columns:
                update = dot_thin(own * reciprocals, jnp.concatenate([own, inverse], axis=1))
                gram_ref[stop:, :] = gram_ref[stop:, :] - update[stop:, :columns]
                inverse_ref[stop:, :] = inverse_ref[stop:, :] - update[stop:, columns:]
        out_ref[...] = inverse_ref[...].T

    return pl.pallas_call(
        kernel,
        out_shape=jax.ShapeDtypeStruct((columns, columns), jnp.float32),
        in_specs=[WHOLE] * len(terms) + [ANYWHERE] * len(after),
        out_specs=WHOLE,
        scratch_shapes=[pltpu.VMEM((columns, columns), jnp.float32)] * 2,
        compiler_params=params(),
        cost_estimate=pl.CostEstimate(flops=25 * 10**9, bytes_accessed=0, transcendentals=0),
    )(*terms, *after)


def two_parts(values):
    return jnp.concatenate(high_low(values), axis=1)


def dot_parts(left_side, right_side):
    columns = right_side.shape[1]
    right_parts = two_parts(right_side)
    product = jnp.dot(
        two_parts(left_side),
        jnp.concatenate([right_parts, right_parts], axis=0),
        preferred_element_type=jnp.float32,
    )
    return product[:, :columns] + product[:, columns:]


def times_right(halves, right_side, transposed=False):
    def kernel(right_ref, *refs):
        in_refs, (out_ref, *parts_ref) = refs[: len(halves)], refs[len(halves) :]
        at = 0
        for ref in in_refs:
            for tile in row_tiles(ref.shape[0]):
                own = slice(at + tile.start, at + tile.stop)
                value = dot_parts(ref[tile, :], right_ref[...])
                out_ref[own, :] = value
                if transposed:
                    parts_ref[0][:, own] = two_parts(value).T
            at += ref.shape[0]

    rows, columns = sum(half.shape[0] for half in halves), halves[0].shape[1]
    out_shape = [jax.ShapeDtypeStruct((rows, columns), jnp.float32)]
    if transposed:
        out_shape.append(jax.ShapeDtypeStruct((2 * columns, rows), jnp.bfloat16))
    return pl.pallas_call(
        kernel,
        out_shape=out_shape,
        in_specs=[WHOLE] * (1 + len(halves)),
        out_specs=[WHOLE] * len(out_shape),
        compiler_params=params(),
        cost_estimate=pl.CostEstimate(flops=2 * rows * 256 * 256, bytes_accessed=0, transcendentals=0),
    )(right_side, *halves)


def image_and_projected(total, pieces, vectors, inverse_upper, basis_parts):
    n, m = len(pieces), len(vectors)
    (rows, doubled), columns = pieces[0].shape, vectors[0].shape[1]

    def kernel(*refs):
        piece_refs, refs = refs[:n], refs[n:]
        vector_refs, refs = refs[:m], refs[m:]
        total_ref, refs = (refs[0], refs[1:]) if total is not None else (None, refs)
        inverse_ref, basis_ref, image_ref, projected_ref, stacked_ref = refs
        stack_all(stacked_ref, vector_refs)
        projected = None
        for tile in row_tiles(rows):
            image = product_tile(piece_refs, stacked_ref, tile, columns)
            if total_ref is not None:
                image = image + total_ref[tile, :]
            image_ref[tile, :] = image
            term = jnp.dot(basis_ref[:, tile], two_parts(image), preferred_element_type=jnp.float32)
            projected = term if projected is None else projected + term
        projected = projected[:columns, :] + projected[columns:, :]
        projected = projected[:, :columns] + projected[:, columns:]
        projected_ref[...] = dot_parts(projected, inverse_ref[...])

    operands = [*pieces, *vectors] + ([] if total is None else [total]) + [inverse_upper, basis_parts]
    return pl.pallas_call(
        kernel,
        out_shape=[
            jax.ShapeDtypeStruct((rows, columns), jnp.float32),
            jax.ShapeDtypeStruct((columns, columns), jnp.float32),
        ],
        in_specs=[WHOLE] * len(operands),
        out_specs=[WHOLE] * 2,
        scratch_shapes=[pltpu.VMEM((n, doubled, 2 * columns), jnp.bfloat16)],
        compiler_params=params(),
        cost_estimate=product_cost(pieces, rows),
    )(*operands)


def residual_of(mapped, basis_rows, terms):
    def kernel(mapped_ref, basis_ref, *refs):
        *term_refs, projected_ref, residual_ref = refs
        projected = tree_sum([ref[...] for ref in term_refs])
        projected_ref[...] = projected
        for tile in row_tiles(mapped.shape[0]):
            residual_ref[tile, :] = mapped_ref[tile, :] - dot_parts(basis_ref[tile, :], projected)

    return pl.pallas_call(
        kernel,
        out_shape=[
            jax.ShapeDtypeStruct(terms[0].shape, jnp.float32),
            jax.ShapeDtypeStruct(mapped.shape, jnp.float32),
        ],
        in_specs=[WHOLE] * (2 + len(terms)),
        out_specs=[WHOLE] * 2,
        compiler_params=params(),
    )(mapped, basis_rows, *terms)


def exchange(value, offset, n):
    return lax.ppermute(value, "blk", [(at, at ^ offset) for at in range(n)])


def local(n, factor, initial, bounds):
    rows, columns = initial.shape
    half = rows // 2
    coefficients = recurrence_coefficients(bounds, columns)

    if n == 4:
        own, along_x = split_factor(factor, n, (0, 1))
        rest = []

        def gather_product(halves):
            top, bottom = halves
            x_top = exchange(top, 1, n)
            y_bottom, x_bottom, y_top = exchange(bottom, 2, n), exchange(bottom, 1, n), exchange(top, 2, n)
            xy_top, xy_bottom = exchange(x_top, 2, n), exchange(y_bottom, 1, n)
            if not rest:
                rest.extend(split_factor(factor, n, (2, 3), after=(x_top, y_bottom)))
            along_y, across = rest
            total = partial_product(None, own, halves)
            total = partial_product(total, [along_x[0], along_y[1]], [x_top, y_bottom])
            total = partial_product(total, [along_x[1], along_y[0]], [x_bottom, y_top])
            total = partial_product(total, [across[1]], [xy_bottom])
            return (total, [across[0]], [xy_top]), (x_top, y_bottom)

        def all_terms(term):
            return [term] + [exchange(term, offset, n) for offset in (1, 2, 3)]
    else:
        pieces = [piece for pair in split_factor(factor, n, range(n)) for piece in pair]

        def all_terms(value):
            gathered = lax.all_gather(value, "blk")
            me = lax.axis_index("blk")
            return [gathered[jnp.bitwise_xor(me, offset)] for offset in range(n)]

        def gather_product(halves):
            return (None, pieces, all_terms(jnp.concatenate(halves))), ()

    previous, current = None, [initial[:half], initial[half:]]
    for order_step in range(DEGREE):
        product, _ = gather_product(current)
        following = recurrence_step(coefficients, *product, current, previous)
        previous, current = current, following

    gram_terms = all_terms(gram_of(current))
    product, arrived = gather_product(current)
    inverse_upper = inverse_cholesky(gram_terms, after=arrived)
    basis_rows, basis_parts = times_right(current, inverse_upper, transposed=True)
    image, projected_term = image_and_projected(*product, inverse_upper, basis_parts)
    projected_terms = all_terms(projected_term)
    (mapped,) = times_right([image], inverse_upper)
    projected, residual = residual_of(mapped, basis_rows, projected_terms)
    return (basis_rows, projected, residual)


def solution(mesh):
    in_specs = (P(("bulk", "blk"), None), P(("bulk", "blk"), None), P("bulk"))
    out_specs = (P(("bulk", "blk"), None), P("bulk", None), P(("bulk", "blk"), None))
    return jax.shard_map(
        functools.partial(local, mesh.shape["blk"]),
        mesh=mesh,
        in_specs=in_specs,
        out_specs=out_specs,
        check_vma=False,
    )
```

```python
import functools

import jax
import jax.numpy as jnp
from jax import lax
from jax.experimental import pallas as pl
from jax.experimental.pallas import tpu as pltpu
from jax.sharding import PartitionSpec as P

DEGREE = 8
HIGHEST = lax.Precision.HIGHEST
WHOLE = pl.BlockSpec(memory_space=pltpu.VMEM)
ANYWHERE = pl.BlockSpec(memory_space=pl.ANY)
HBM = pl.BlockSpec(memory_space=pltpu.HBM)
SCALARS = pl.BlockSpec(memory_space=pltpu.SMEM)
VMEM_LIMIT = 16 * 2**20


def params():
    return pltpu.CompilerParams(vmem_limit_bytes=VMEM_LIMIT)


def high_low(values):
    high = values.astype(jnp.bfloat16)
    low = (values - high.astype(jnp.float32)).astype(jnp.bfloat16)
    return high, low


def split_factor(factor, n, offsets, after=()):
    rows, order = factor.shape
    width, count = order // (2 * n), 2 * len(offsets)

    def kernel(factor_ref, *refs):
        out_refs, (slots, arrived) = refs[len(after) : len(after) + count], refs[-2:]
        me = lax.axis_index("blk")

        def fetch(at):
            owner = jnp.bitwise_xor(me, offsets[at // 2])
            start = pl.multiple_of((2 * owner + at % 2) * width, width)
            return pltpu.make_async_copy(
                factor_ref.at[:, pl.ds(start, width)], slots.at[at % 3], arrived.at[at % 3]
            )

        fetch(0).start()
        fetch(1).start()
        for at in range(count):
            if at + 2 < count:
                fetch(at + 2).start()
            fetch(at).wait()

            @pl.loop(0, rows // 64)
            def _(tile):
                own = pl.ds(pl.multiple_of(tile * 64, 64), 64)
                high, low = high_low(slots[at % 3, own, :])
                out_refs[at][own, :width] = high
                out_refs[at][own, width:] = low

    pieces = pl.pallas_call(
        kernel,
        out_shape=[jax.ShapeDtypeStruct((rows, 2 * width), jnp.bfloat16)] * count,
        in_specs=[HBM] + [ANYWHERE] * len(after),
        out_specs=[WHOLE] * count,
        scratch_shapes=[pltpu.VMEM((3, rows, width), jnp.float32), pltpu.SemaphoreType.DMA((3,))],
        compiler_params=pltpu.CompilerParams(vmem_limit_bytes=40 * 2**20),
        cost_estimate=pl.CostEstimate(flops=0, bytes_accessed=8 * count * rows * width, transcendentals=0),
    )(factor, *after)
    return [pieces[2 * at : 2 * at + 2] for at in range(len(offsets))]


def recurrence_coefficients(bounds, columns):
    def kernel(bounds_ref, out_ref):
        centre = (bounds_ref[0] + bounds_ref[1]) / 2.0
        radius = (bounds_ref[1] - bounds_ref[0]) / 2.0
        out_ref[0:1, :] = jnp.full((1, columns), centre, jnp.float32)
        out_ref[1:2, :] = 1.0 / jnp.full((1, columns), radius, jnp.float32)

    return pl.pallas_call(
        kernel,
        out_shape=jax.ShapeDtypeStruct((2, columns), jnp.float32),
        in_specs=[SCALARS],
        out_specs=WHOLE,
        compiler_params=params(),
    )(bounds)


def stack_vectors(stacked_ref, at, vectors):
    width, columns = vectors.shape
    high, low = high_low(vectors)
    for start in (0, width):
        stacked_ref[at, start : start + width, :columns] = high
        stacked_ref[at, start : start + width, columns:] = low


def stack_all(stacked_ref, vector_refs):
    width, at = stacked_ref.shape[1] // 2, 0
    for ref in vector_refs:
        for start in range(0, ref.shape[0], width):
            stack_vectors(stacked_ref, at, ref[start : start + width, :])
            at += 1


def product_tile(pieces, stacked_ref, rows, columns):
    total = None
    for at, piece in enumerate(pieces):
        term = jnp.dot(piece[rows, :], stacked_ref[at], preferred_element_type=jnp.float32)
        total = term if total is None else total + term
    return total[:, :columns] + total[:, columns:]


def row_tiles(rows, largest=256):
    tile = min(rows, largest)
    return [slice(start, start + tile) for start in range(0, rows, tile)]


def product_cost(pieces, rows):
    doubled = pieces[0].shape[1]
    return pl.CostEstimate(
        flops=2 * rows * doubled * 256 * len(pieces),
        bytes_accessed=2 * rows * doubled * len(pieces),
        transcendentals=0,
    )


def partial_product(total, pieces, vectors):
    n, m = len(pieces), len(vectors)
    (rows, doubled), columns = pieces[0].shape, vectors[0].shape[1]

    def kernel(*refs):
        piece_refs, vector_refs = refs[:n], refs[n : n + m]
        total_ref = refs[n + m] if total is not None else None
        out_ref, stacked_ref = refs[-2:]
        stack_all(stacked_ref, vector_refs)
        for tile in row_tiles(rows, 512):
            value = product_tile(piece_refs, stacked_ref, tile, columns)
            out_ref[tile, :] = value if total_ref is None else total_ref[tile, :] + value

    operands = [*pieces, *vectors] + ([] if total is None else [total])
    return pl.pallas_call(
        kernel,
        out_shape=jax.ShapeDtypeStruct((rows, columns), jnp.float32),
        in_specs=[WHOLE] * len(operands),
        out_specs=WHOLE,
        scratch_shapes=[pltpu.VMEM((n, doubled, 2 * columns), jnp.bfloat16)],
        compiler_params=params(),
        cost_estimate=product_cost(pieces, rows),
    )(*operands)


def recurrence_step(coefficients, total, pieces, vectors, current, previous):
    n, m = len(pieces), len(vectors)
    half, columns = current[0].shape
    doubled = pieces[0].shape[1]

    def kernel(coefficient_ref, *refs):
        piece_refs, refs = refs[:n], refs[n:]
        vector_refs, refs = refs[:m], refs[m:]
        total_ref, refs = (refs[0], refs[1:]) if total is not None else (None, refs)
        current_refs, refs = refs[:2], refs[2:]
        previous_refs, refs = (refs[:2], refs[2:]) if previous else (None, refs)
        *out_refs, stacked_ref = refs
        stack_all(stacked_ref, vector_refs)
        centre, inverse_radius = coefficient_ref[0:1, :columns], coefficient_ref[1:2, :columns]
        for at in (1, 0):
            for own in row_tiles(half):
                tile = slice(at * half + own.start, at * half + own.stop)
                value = product_tile(piece_refs, stacked_ref, tile, columns)
                if total_ref is not None:
                    value = value + total_ref[tile, :]
                value = (value - centre * current_refs[at][own, :]) * inverse_radius
                if previous_refs is not None:
                    value = 2.0 * value - previous_refs[at][own, :]
                out_refs[at][own, :] = value

    operands = [*pieces, *vectors] + ([] if total is None else [total])
    operands += [*current, *(previous or ())]
    return pl.pallas_call(
        kernel,
        out_shape=[jax.ShapeDtypeStruct((half, columns), jnp.float32)] * 2,
        in_specs=[WHOLE] * (1 + len(operands)),
        out_specs=[WHOLE] * 2,
        scratch_shapes=[pltpu.VMEM((n, doubled, 2 * columns), jnp.bfloat16)],
        compiler_params=params(),
        cost_estimate=product_cost(pieces, 2 * half),
    )(coefficients, *operands)


def dot_high(left_side, right_side, contract):
    return lax.dot_general(
        left_side, right_side, (contract, ((), ())), precision=HIGHEST, preferred_element_type=jnp.float32
    )


def tree_sum(values):
    while len(values) > 1:
        values = [values[at] + values[at + 1] for at in range(0, len(values), 2)]
    return values[0]


def gram_of(halves):
    def kernel(*refs):
        *in_refs, out_ref = refs
        total = None
        for ref in in_refs:
            term = dot_high(ref[...], ref[...], ((0,), (0,)))
            total = term if total is None else total + term
        out_ref[...] = total

    columns = halves[0].shape[1]
    return pl.pallas_call(
        kernel,
        out_shape=jax.ShapeDtypeStruct((columns, columns), jnp.float32),
        in_specs=[WHOLE] * len(halves),
        out_specs=WHOLE,
        compiler_params=params(),
    )(*halves)


def three_parts(values):
    high = values.astype(jnp.bfloat16)
    return (high, *high_low(values - high.astype(jnp.float32)))


def dot_thin(left_side, right_side):
    a, b = three_parts(left_side), three_parts(right_side)
    pairs = [(a[0], b[0]), (a[0], b[1]), (a[1], b[0]), (a[1], b[1]), (a[0], b[2]), (a[2], b[0])]
    return lax.dot_general(
        jnp.concatenate([pair[0].astype(jnp.float32) for pair in pairs], axis=0).T.astype(jnp.bfloat16),
        jnp.concatenate([pair[1].astype(jnp.float32) for pair in pairs], axis=0).astype(jnp.bfloat16),
        (((1,), (0,)), ((), ())),
        preferred_element_type=jnp.float32,
    )


def inverse_cholesky(terms, after=()):
    columns = terms[0].shape[0]
    high = 16

    def kernel(*refs):
        term_refs, (out_ref, gram_ref, inverse_ref) = refs[: len(terms)], refs[-3:]
        gram_ref[...] = tree_sum([ref[...] for ref in term_refs])
        row_at = lax.broadcasted_iota(jnp.int32, (columns, columns), 0)
        column_at = lax.broadcasted_iota(jnp.int32, (columns, columns), 1)
        inverse_ref[...] = jnp.where(row_at == column_at, 1.0, 0.0)
        sub_row = lax.broadcasted_iota(jnp.int32, (high, columns), 0)
        for start in range(0, columns, high):
            stop = start + high
            own, inverse = gram_ref[start:stop, :], inverse_ref[start:stop, :]
            spread = [
                jnp.broadcast_to(own[:, start + at : start + at + 1], (high, columns)) for at in range(high)
            ]
            pivots = jnp.ones((high, columns), jnp.float32)
            reciprocals = jnp.ones((high, columns), jnp.float32)
            for at in range(high):
                pivot = jnp.broadcast_to(spread[at][at : at + 1, :], (high, columns))
                reciprocal = 1.0 / pivot
                pivots = jnp.where(sub_row == at, pivot, pivots)
                reciprocals = jnp.where(sub_row == at, reciprocal, reciprocals)
                if at + 1 == high:
                    break
                factor = jnp.where(sub_row > at, spread[at], 0.0) * reciprocal
                for later in range(at + 1, high):
                    spread[later] = spread[later] - factor * spread[later][at : at + 1, :]
                own = own - factor * own[at : at + 1, :]
                inverse = inverse - factor * inverse[at : at + 1, :]
            inverse_ref[start:stop, :] = inverse / jnp.sqrt(pivots)
            if stop < columns:
                update = dot_thin(own * reciprocals, jnp.concatenate([own, inverse], axis=1))
                gram_ref[stop:, :] = gram_ref[stop:, :] - update[stop:, :columns]
                inverse_ref[stop:, :] = inverse_ref[stop:, :] - update[stop:, columns:]
        out_ref[...] = inverse_ref[...].T

    return pl.pallas_call(
        kernel,
        out_shape=jax.ShapeDtypeStruct((columns, columns), jnp.float32),
        in_specs=[WHOLE] * len(terms) + [ANYWHERE] * len(after),
        out_specs=WHOLE,
        scratch_shapes=[pltpu.VMEM((columns, columns), jnp.float32)] * 2,
        compiler_params=params(),
        cost_estimate=pl.CostEstimate(flops=25 * 10**9, bytes_accessed=0, transcendentals=0),
    )(*terms, *after)


def two_parts(values):
    return jnp.concatenate(high_low(values), axis=1)


def dot_parts(left_side, right_side):
    columns = right_side.shape[1]
    right_parts = two_parts(right_side)
    product = jnp.dot(
        two_parts(left_side),
        jnp.concatenate([right_parts, right_parts], axis=0),
        preferred_element_type=jnp.float32,
    )
    return product[:, :columns] + product[:, columns:]


def times_right(halves, right_side, transposed=False):
    def kernel(right_ref, *refs):
        in_refs, (out_ref, *parts_ref) = refs[: len(halves)], refs[len(halves) :]
        at = 0
        for ref in in_refs:
            for tile in row_tiles(ref.shape[0]):
                own = slice(at + tile.start, at + tile.stop)
                value = dot_parts(ref[tile, :], right_ref[...])
                out_ref[own, :] = value
                if transposed:
                    parts_ref[0][:, own] = two_parts(value).T
            at += ref.shape[0]

    rows, columns = sum(half.shape[0] for half in halves), halves[0].shape[1]
    out_shape = [jax.ShapeDtypeStruct((rows, columns), jnp.float32)]
    if transposed:
        out_shape.append(jax.ShapeDtypeStruct((2 * columns, rows), jnp.bfloat16))
    return pl.pallas_call(
        kernel,
        out_shape=out_shape,
        in_specs=[WHOLE] * (1 + len(halves)),
        out_specs=[WHOLE] * len(out_shape),
        compiler_params=params(),
        cost_estimate=pl.CostEstimate(flops=2 * rows * 256 * 256, bytes_accessed=0, transcendentals=0),
    )(right_side, *halves)


def image_and_projected(total, pieces, vectors, inverse_upper, basis_parts):
    n, m = len(pieces), len(vectors)
    (rows, doubled), columns = pieces[0].shape, vectors[0].shape[1]

    def kernel(*refs):
        piece_refs, refs = refs[:n], refs[n:]
        vector_refs, refs = refs[:m], refs[m:]
        total_ref, refs = (refs[0], refs[1:]) if total is not None else (None, refs)
        inverse_ref, basis_ref, image_ref, projected_ref, stacked_ref = refs
        stack_all(stacked_ref, vector_refs)
        projected = None
        for tile in row_tiles(rows):
            image = product_tile(piece_refs, stacked_ref, tile, columns)
            if total_ref is not None:
                image = image + total_ref[tile, :]
            image_ref[tile, :] = image
            term = jnp.dot(basis_ref[:, tile], two_parts(image), preferred_element_type=jnp.float32)
            projected = term if projected is None else projected + term
        projected = projected[:columns, :] + projected[columns:, :]
        projected = projected[:, :columns] + projected[:, columns:]
        projected_ref[...] = dot_parts(projected, inverse_ref[...])

    operands = [*pieces, *vectors] + ([] if total is None else [total]) + [inverse_upper, basis_parts]
    return pl.pallas_call(
        kernel,
        out_shape=[
            jax.ShapeDtypeStruct((rows, columns), jnp.float32),
            jax.ShapeDtypeStruct((columns, columns), jnp.float32),
        ],
        in_specs=[WHOLE] * len(operands),
        out_specs=[WHOLE] * 2,
        scratch_shapes=[pltpu.VMEM((n, doubled, 2 * columns), jnp.bfloat16)],
        compiler_params=params(),
        cost_estimate=product_cost(pieces, rows),
    )(*operands)


def residual_of(mapped, basis_rows, terms):
    def kernel(mapped_ref, basis_ref, *refs):
        *term_refs, projected_ref, residual_ref = refs
        projected = tree_sum([ref[...] for ref in term_refs])
        projected_ref[...] = projected
        for tile in row_tiles(mapped.shape[0]):
            residual_ref[tile, :] = mapped_ref[tile, :] - dot_parts(basis_ref[tile, :], projected)

    return pl.pallas_call(
        kernel,
        out_shape=[
            jax.ShapeDtypeStruct(terms[0].shape, jnp.float32),
            jax.ShapeDtypeStruct(mapped.shape, jnp.float32),
        ],
        in_specs=[WHOLE] * (2 + len(terms)),
        out_specs=[WHOLE] * 2,
        compiler_params=params(),
    )(mapped, basis_rows, *terms)


def exchange(value, offset, n):
    return lax.ppermute(value, "blk", [(at, at ^ offset) for at in range(n)])


def local(n, factor, initial, bounds):
    rows, columns = initial.shape
    half = rows // 2
    coefficients = recurrence_coefficients(bounds, columns)

    if n == 4:
        own, along_x = split_factor(factor, n, (0, 1))
        rest = []

        def gather_product(halves):
            top, bottom = halves
            x_top = exchange(top, 1, n)
            y_bottom, x_bottom, y_top = exchange(bottom, 2, n), exchange(bottom, 1, n), exchange(top, 2, n)
            xy_top, xy_bottom = exchange(x_top, 2, n), exchange(y_bottom, 1, n)
            if not rest:
                rest.extend(split_factor(factor, n, (2, 3), after=(x_top, y_bottom)))
            along_y, across = rest
            total = partial_product(None, own, halves)
            total = partial_product(total, [along_x[0], along_y[1]], [x_top, y_bottom])
            total = partial_product(total, [along_x[1], along_y[0]], [x_bottom, y_top])
            total = partial_product(total, [across[1]], [xy_bottom])
            return (total, [across[0]], [xy_top]), (x_top, y_bottom)

        def all_terms(term, offsets=(1, 2, 3)):
            return [term] + [exchange(term, offset, n) for offset in offsets]
    else:
        pieces = [piece for pair in split_factor(factor, n, range(n)) for piece in pair]

        def all_terms(value, offsets=None):
            gathered = lax.all_gather(value, "blk")
            me = lax.axis_index("blk")
            return [gathered[jnp.bitwise_xor(me, offset)] for offset in range(n)]

        def gather_product(halves):
            return (None, pieces, all_terms(jnp.concatenate(halves))), ()

    previous, current = None, [initial[:half], initial[half:]]
    for order_step in range(DEGREE):
        product, _ = gather_product(current)
        following = recurrence_step(coefficients, *product, current, previous)
        previous, current = current, following

    gram_terms = all_terms(gram_of(current))
    product, arrived = gather_product(current)
    inverse_upper = inverse_cholesky(gram_terms, after=arrived)
    basis_rows, basis_parts = times_right(current, inverse_upper, transposed=True)
    image, projected_term = image_and_projected(*product, inverse_upper, basis_parts)
    projected_terms = all_terms(projected_term, (3, 1, 2))
    (mapped,) = times_right([image], inverse_upper)
    projected, residual = residual_of(mapped, basis_rows, projected_terms)
    return (basis_rows, projected, residual)


def solution(mesh):
    in_specs = (P(("bulk", "blk"), None), P(("bulk", "blk"), None), P("bulk"))
    out_specs = (P(("bulk", "blk"), None), P("bulk", None), P(("bulk", "blk"), None))
    return jax.shard_map(
        functools.partial(local, mesh.shape["blk"]),
        mesh=mesh,
        in_specs=in_specs,
        out_specs=out_specs,
        check_vma=False,
    )
```

```python
import functools

import jax
import jax.numpy as jnp
from jax import lax
from jax.experimental import pallas as pl
from jax.experimental.pallas import tpu as pltpu
from jax.sharding import PartitionSpec as P

DEGREE = 8
HIGHEST = lax.Precision.HIGHEST
WHOLE = pl.BlockSpec(memory_space=pltpu.VMEM)
ANYWHERE = pl.BlockSpec(memory_space=pl.ANY)
HBM = pl.BlockSpec(memory_space=pltpu.HBM)
SCALARS = pl.BlockSpec(memory_space=pltpu.SMEM)
VMEM_LIMIT = 16 * 2**20


def params():
    return pltpu.CompilerParams(vmem_limit_bytes=VMEM_LIMIT)


def high_low(values):
    high = values.astype(jnp.bfloat16)
    low = (values - high.astype(jnp.float32)).astype(jnp.bfloat16)
    return high, low


def split_factor(factor, n, offsets, after=()):
    rows, order = factor.shape
    width, count = order // (2 * n), 2 * len(offsets)

    def kernel(factor_ref, *refs):
        out_refs, (slots, arrived) = refs[len(after) : len(after) + count], refs[-2:]
        me = lax.axis_index("blk")

        def fetch(at):
            owner = jnp.bitwise_xor(me, offsets[at // 2])
            start = pl.multiple_of((2 * owner + at % 2) * width, width)
            return pltpu.make_async_copy(
                factor_ref.at[:, pl.ds(start, width)], slots.at[at % 3], arrived.at[at % 3]
            )

        fetch(0).start()
        fetch(1).start()
        for at in range(count):
            if at + 2 < count:
                fetch(at + 2).start()
            fetch(at).wait()

            @pl.loop(0, rows // 64)
            def _(tile):
                own = pl.ds(pl.multiple_of(tile * 64, 64), 64)
                high, low = high_low(slots[at % 3, own, :])
                out_refs[at][own, :width] = high
                out_refs[at][own, width:] = low

    pieces = pl.pallas_call(
        kernel,
        out_shape=[jax.ShapeDtypeStruct((rows, 2 * width), jnp.bfloat16)] * count,
        in_specs=[HBM] + [ANYWHERE] * len(after),
        out_specs=[WHOLE] * count,
        scratch_shapes=[pltpu.VMEM((3, rows, width), jnp.float32), pltpu.SemaphoreType.DMA((3,))],
        compiler_params=pltpu.CompilerParams(vmem_limit_bytes=40 * 2**20),
        cost_estimate=pl.CostEstimate(flops=0, bytes_accessed=8 * count * rows * width, transcendentals=0),
    )(factor, *after)
    return [pieces[2 * at : 2 * at + 2] for at in range(len(offsets))]


def recurrence_coefficients(bounds, columns):
    def kernel(bounds_ref, out_ref):
        centre = (bounds_ref[0] + bounds_ref[1]) / 2.0
        radius = (bounds_ref[1] - bounds_ref[0]) / 2.0
        out_ref[0:1, :] = jnp.full((1, columns), centre, jnp.float32)
        out_ref[1:2, :] = 1.0 / jnp.full((1, columns), radius, jnp.float32)

    return pl.pallas_call(
        kernel,
        out_shape=jax.ShapeDtypeStruct((2, columns), jnp.float32),
        in_specs=[SCALARS],
        out_specs=WHOLE,
        compiler_params=params(),
    )(bounds)


def stack_vectors(stacked_ref, at, vectors):
    width, columns = vectors.shape
    high, low = high_low(vectors)
    for start in (0, width):
        stacked_ref[at, start : start + width, :columns] = high
        stacked_ref[at, start : start + width, columns:] = low


def stack_all(stacked_ref, vector_refs):
    width, at = stacked_ref.shape[1] // 2, 0
    for ref in vector_refs:
        for start in range(0, ref.shape[0], width):
            stack_vectors(stacked_ref, at, ref[start : start + width, :])
            at += 1


def product_tile(pieces, stacked_ref, rows, columns):
    total = None
    for at, piece in enumerate(pieces):
        term = jnp.dot(piece[rows, :], stacked_ref[at], preferred_element_type=jnp.float32)
        total = term if total is None else total + term
    return total[:, :columns] + total[:, columns:]


def row_tiles(rows, largest=256):
    tile = min(rows, largest)
    return [slice(start, start + tile) for start in range(0, rows, tile)]


def product_cost(pieces, rows):
    doubled = pieces[0].shape[1]
    return pl.CostEstimate(
        flops=2 * rows * doubled * 256 * len(pieces),
        bytes_accessed=2 * rows * doubled * len(pieces),
        transcendentals=0,
    )


def partial_product(total, pieces, vectors):
    n, m = len(pieces), len(vectors)
    (rows, doubled), columns = pieces[0].shape, vectors[0].shape[1]

    def kernel(*refs):
        piece_refs, vector_refs = refs[:n], refs[n : n + m]
        total_ref = refs[n + m] if total is not None else None
        out_ref, stacked_ref = refs[-2:]
        stack_all(stacked_ref, vector_refs)
        for tile in row_tiles(rows, 512):
            value = product_tile(piece_refs, stacked_ref, tile, columns)
            out_ref[tile, :] = value if total_ref is None else total_ref[tile, :] + value

    operands = [*pieces, *vectors] + ([] if total is None else [total])
    return pl.pallas_call(
        kernel,
        out_shape=jax.ShapeDtypeStruct((rows, columns), jnp.float32),
        in_specs=[WHOLE] * len(operands),
        out_specs=WHOLE,
        scratch_shapes=[pltpu.VMEM((n, doubled, 2 * columns), jnp.bfloat16)],
        compiler_params=params(),
        cost_estimate=product_cost(pieces, rows),
    )(*operands)


def forwarded(value):
    def kernel(value_ref, out_ref):
        out_ref[...] = value_ref[...]

    return pl.pallas_call(
        kernel,
        out_shape=jax.ShapeDtypeStruct(value.shape, value.dtype),
        in_specs=[WHOLE],
        out_specs=WHOLE,
        compiler_params=params(),
        cost_estimate=pl.CostEstimate(flops=3 * 10**9, bytes_accessed=0, transcendentals=0),
    )(value)


def recurrence_step(coefficients, total, pieces, vectors, current, previous):
    n, m = len(pieces), len(vectors)
    half, columns = current[0].shape
    doubled = pieces[0].shape[1]

    def kernel(coefficient_ref, *refs):
        piece_refs, refs = refs[:n], refs[n:]
        vector_refs, refs = refs[:m], refs[m:]
        total_ref, refs = (refs[0], refs[1:]) if total is not None else (None, refs)
        current_refs, refs = refs[:2], refs[2:]
        previous_refs, refs = (refs[:2], refs[2:]) if previous else (None, refs)
        *out_refs, stacked_ref = refs
        stack_all(stacked_ref, vector_refs)
        centre, inverse_radius = coefficient_ref[0:1, :columns], coefficient_ref[1:2, :columns]
        for at in (1, 0):
            for own in row_tiles(half):
                tile = slice(at * half + own.start, at * half + own.stop)
                value = product_tile(piece_refs, stacked_ref, tile, columns)
                if total_ref is not None:
                    value = value + total_ref[tile, :]
                value = (value - centre * current_refs[at][own, :]) * inverse_radius
                if previous_refs is not None:
                    value = 2.0 * value - previous_refs[at][own, :]
                out_refs[at][own, :] = value

    operands = [*pieces, *vectors] + ([] if total is None else [total])
    operands += [*current, *(previous or ())]
    return pl.pallas_call(
        kernel,
        out_shape=[jax.ShapeDtypeStruct((half, columns), jnp.float32)] * 2,
        in_specs=[WHOLE] * (1 + len(operands)),
        out_specs=[WHOLE] * 2,
        scratch_shapes=[pltpu.VMEM((n, doubled, 2 * columns), jnp.bfloat16)],
        compiler_params=params(),
        cost_estimate=product_cost(pieces, 2 * half),
    )(coefficients, *operands)


def dot_high(left_side, right_side, contract):
    return lax.dot_general(
        left_side, right_side, (contract, ((), ())), precision=HIGHEST, preferred_element_type=jnp.float32
    )


def tree_sum(values):
    while len(values) > 1:
        values = [values[at] + values[at + 1] for at in range(0, len(values), 2)]
    return values[0]


def gram_of(halves):
    def kernel(*refs):
        *in_refs, out_ref = refs
        total = None
        for ref in in_refs:
            term = dot_high(ref[...], ref[...], ((0,), (0,)))
            total = term if total is None else total + term
        out_ref[...] = total

    columns = halves[0].shape[1]
    return pl.pallas_call(
        kernel,
        out_shape=jax.ShapeDtypeStruct((columns, columns), jnp.float32),
        in_specs=[WHOLE] * len(halves),
        out_specs=WHOLE,
        compiler_params=params(),
    )(*halves)


def three_parts(values):
    high = values.astype(jnp.bfloat16)
    return (high, *high_low(values - high.astype(jnp.float32)))


def dot_thin(left_side, right_side):
    a, b = three_parts(left_side), three_parts(right_side)
    pairs = [(a[0], b[0]), (a[0], b[1]), (a[1], b[0]), (a[1], b[1]), (a[0], b[2]), (a[2], b[0])]
    return lax.dot_general(
        jnp.concatenate([pair[0].astype(jnp.float32) for pair in pairs], axis=0).T.astype(jnp.bfloat16),
        jnp.concatenate([pair[1].astype(jnp.float32) for pair in pairs], axis=0).astype(jnp.bfloat16),
        (((1,), (0,)), ((), ())),
        preferred_element_type=jnp.float32,
    )


def inverse_cholesky(terms, after=()):
    columns = terms[0].shape[0]
    high = 16

    def kernel(*refs):
        term_refs, (out_ref, gram_ref, inverse_ref) = refs[: len(terms)], refs[-3:]
        gram_ref[...] = tree_sum([ref[...] for ref in term_refs])
        row_at = lax.broadcasted_iota(jnp.int32, (columns, columns), 0)
        column_at = lax.broadcasted_iota(jnp.int32, (columns, columns), 1)
        inverse_ref[...] = jnp.where(row_at == column_at, 1.0, 0.0)
        sub_row = lax.broadcasted_iota(jnp.int32, (high, columns), 0)
        for start in range(0, columns, high):
            stop = start + high
            own, inverse = gram_ref[start:stop, :], inverse_ref[start:stop, :]
            spread = [
                jnp.broadcast_to(own[:, start + at : start + at + 1], (high, columns)) for at in range(high)
            ]
            pivots = jnp.ones((high, columns), jnp.float32)
            reciprocals = jnp.ones((high, columns), jnp.float32)
            for at in range(high):
                pivot = jnp.broadcast_to(spread[at][at : at + 1, :], (high, columns))
                reciprocal = 1.0 / pivot
                pivots = jnp.where(sub_row == at, pivot, pivots)
                reciprocals = jnp.where(sub_row == at, reciprocal, reciprocals)
                if at + 1 == high:
                    break
                factor = jnp.where(sub_row > at, spread[at], 0.0) * reciprocal
                for later in range(at + 1, high):
                    spread[later] = spread[later] - factor * spread[later][at : at + 1, :]
                own = own - factor * own[at : at + 1, :]
                inverse = inverse - factor * inverse[at : at + 1, :]
            inverse_ref[start:stop, :] = inverse / jnp.sqrt(pivots)
            if stop < columns:
                update = dot_thin(own * reciprocals, jnp.concatenate([own, inverse], axis=1))
                gram_ref[stop:, :] = gram_ref[stop:, :] - update[stop:, :columns]
                inverse_ref[stop:, :] = inverse_ref[stop:, :] - update[stop:, columns:]
        out_ref[...] = inverse_ref[...].T

    return pl.pallas_call(
        kernel,
        out_shape=jax.ShapeDtypeStruct((columns, columns), jnp.float32),
        in_specs=[WHOLE] * len(terms) + [ANYWHERE] * len(after),
        out_specs=WHOLE,
        scratch_shapes=[pltpu.VMEM((columns, columns), jnp.float32)] * 2,
        compiler_params=params(),
        cost_estimate=pl.CostEstimate(flops=25 * 10**9, bytes_accessed=0, transcendentals=0),
    )(*terms, *after)


def two_parts(values):
    return jnp.concatenate(high_low(values), axis=1)


def dot_parts(left_side, right_side):
    columns = right_side.shape[1]
    right_parts = two_parts(right_side)
    product = jnp.dot(
        two_parts(left_side),
        jnp.concatenate([right_parts, right_parts], axis=0),
        preferred_element_type=jnp.float32,
    )
    return product[:, :columns] + product[:, columns:]


def times_right(halves, right_side, transposed=False):
    def kernel(right_ref, *refs):
        in_refs, (out_ref, *parts_ref) = refs[: len(halves)], refs[len(halves) :]
        at = 0
        for ref in in_refs:
            for tile in row_tiles(ref.shape[0]):
                own = slice(at + tile.start, at + tile.stop)
                value = dot_parts(ref[tile, :], right_ref[...])
                out_ref[own, :] = value
                if transposed:
                    parts_ref[0][:, own] = two_parts(value).T
            at += ref.shape[0]

    rows, columns = sum(half.shape[0] for half in halves), halves[0].shape[1]
    out_shape = [jax.ShapeDtypeStruct((rows, columns), jnp.float32)]
    if transposed:
        out_shape.append(jax.ShapeDtypeStruct((2 * columns, rows), jnp.bfloat16))
    return pl.pallas_call(
        kernel,
        out_shape=out_shape,
        in_specs=[WHOLE] * (1 + len(halves)),
        out_specs=[WHOLE] * len(out_shape),
        compiler_params=params(),
        cost_estimate=pl.CostEstimate(flops=2 * rows * 256 * 256, bytes_accessed=0, transcendentals=0),
    )(right_side, *halves)


def image_and_projected(total, pieces, vectors, inverse_upper, basis_parts):
    n, m = len(pieces), len(vectors)
    (rows, doubled), columns = pieces[0].shape, vectors[0].shape[1]

    def kernel(*refs):
        piece_refs, refs = refs[:n], refs[n:]
        vector_refs, refs = refs[:m], refs[m:]
        total_ref, refs = (refs[0], refs[1:]) if total is not None else (None, refs)
        inverse_ref, basis_ref, image_ref, projected_ref, stacked_ref = refs
        stack_all(stacked_ref, vector_refs)
        projected = None
        for tile in row_tiles(rows):
            image = product_tile(piece_refs, stacked_ref, tile, columns)
            if total_ref is not None:
                image = image + total_ref[tile, :]
            image_ref[tile, :] = image
            term = jnp.dot(basis_ref[:, tile], two_parts(image), preferred_element_type=jnp.float32)
            projected = term if projected is None else projected + term
        projected = projected[:columns, :] + projected[columns:, :]
        projected = projected[:, :columns] + projected[:, columns:]
        projected_ref[...] = dot_parts(projected, inverse_ref[...])

    operands = [*pieces, *vectors] + ([] if total is None else [total]) + [inverse_upper, basis_parts]
    return pl.pallas_call(
        kernel,
        out_shape=[
            jax.ShapeDtypeStruct((rows, columns), jnp.float32),
            jax.ShapeDtypeStruct((columns, columns), jnp.float32),
        ],
        in_specs=[WHOLE] * len(operands),
        out_specs=[WHOLE] * 2,
        scratch_shapes=[pltpu.VMEM((n, doubled, 2 * columns), jnp.bfloat16)],
        compiler_params=params(),
        cost_estimate=product_cost(pieces, rows),
    )(*operands)


def residual_of(mapped, basis_rows, terms):
    def kernel(mapped_ref, basis_ref, *refs):
        *term_refs, projected_ref, residual_ref = refs
        projected = tree_sum([ref[...] for ref in term_refs])
        projected_ref[...] = projected
        for tile in row_tiles(mapped.shape[0]):
            residual_ref[tile, :] = mapped_ref[tile, :] - dot_parts(basis_ref[tile, :], projected)

    return pl.pallas_call(
        kernel,
        out_shape=[
            jax.ShapeDtypeStruct(terms[0].shape, jnp.float32),
            jax.ShapeDtypeStruct(mapped.shape, jnp.float32),
        ],
        in_specs=[WHOLE] * (2 + len(terms)),
        out_specs=[WHOLE] * 2,
        compiler_params=params(),
    )(mapped, basis_rows, *terms)


def exchange(value, offset, n):
    return lax.ppermute(value, "blk", [(at, at ^ offset) for at in range(n)])


def local(n, factor, initial, bounds):
    rows, columns = initial.shape
    half = rows // 2
    coefficients = recurrence_coefficients(bounds, columns)

    if n == 4:
        own, along_x = split_factor(factor, n, (0, 1))
        rest = []

        def gather_product(halves, send_on=forwarded):
            top, bottom = halves
            x_top = exchange(top, 1, n)
            y_bottom, x_bottom, y_top = exchange(bottom, 2, n), exchange(bottom, 1, n), exchange(top, 2, n)
            xy_top, xy_bottom = exchange(send_on(x_top), 2, n), exchange(y_bottom, 1, n)
            if not rest:
                rest.extend(split_factor(factor, n, (2, 3), after=(x_top, y_bottom)))
            along_y, across = rest
            total = partial_product(None, own, halves)
            total = partial_product(total, [along_x[0], along_y[1]], [x_top, y_bottom])
            total = partial_product(total, [along_x[1], along_y[0]], [x_bottom, y_top])
            total = partial_product(total, [across[1]], [xy_bottom])
            return (total, [across[0]], [xy_top]), (x_top, y_bottom)

        def all_terms(term, offsets=(1, 2, 3)):
            return [term] + [exchange(term, offset, n) for offset in offsets]
    else:
        pieces = [piece for pair in split_factor(factor, n, range(n)) for piece in pair]

        def all_terms(value, offsets=None):
            gathered = lax.all_gather(value, "blk")
            me = lax.axis_index("blk")
            return [gathered[jnp.bitwise_xor(me, offset)] for offset in range(n)]

        def gather_product(halves, send_on=None):
            return (None, pieces, all_terms(jnp.concatenate(halves))), ()

    previous, current = None, [initial[:half], initial[half:]]
    for order_step in range(DEGREE):
        product, _ = gather_product(current)
        following = recurrence_step(coefficients, *product, current, previous)
        previous, current = current, following

    gram_terms = all_terms(gram_of(current))
    product, arrived = gather_product(current, send_on=lambda value: value)
    inverse_upper = inverse_cholesky(gram_terms, after=arrived)
    basis_rows, basis_parts = times_right(current, inverse_upper, transposed=True)
    image, projected_term = image_and_projected(*product, inverse_upper, basis_parts)
    projected_terms = all_terms(projected_term, (3, 1, 2))
    (mapped,) = times_right([image], inverse_upper)
    projected, residual = residual_of(mapped, basis_rows, projected_terms)
    return (basis_rows, projected, residual)


def solution(mesh):
    in_specs = (P(("bulk", "blk"), None), P(("bulk", "blk"), None), P("bulk"))
    out_specs = (P(("bulk", "blk"), None), P("bulk", None), P(("bulk", "blk"), None))
    return jax.shard_map(
        functools.partial(local, mesh.shape["blk"]),
        mesh=mesh,
        in_specs=in_specs,
        out_specs=out_specs,
        check_vma=False,
    )
```

```python
import functools

import jax
import jax.numpy as jnp
from jax import lax
from jax.experimental import pallas as pl
from jax.experimental.pallas import tpu as pltpu
from jax.sharding import PartitionSpec as P

DEGREE = 8
HIGHEST = lax.Precision.HIGHEST
WHOLE = pl.BlockSpec(memory_space=pltpu.VMEM)
ANYWHERE = pl.BlockSpec(memory_space=pl.ANY)
HBM = pl.BlockSpec(memory_space=pltpu.HBM)
SCALARS = pl.BlockSpec(memory_space=pltpu.SMEM)
VMEM_LIMIT = 16 * 2**20


def params():
    return pltpu.CompilerParams(vmem_limit_bytes=VMEM_LIMIT)


def high_low(values):
    high = values.astype(jnp.bfloat16)
    low = (values - high.astype(jnp.float32)).astype(jnp.bfloat16)
    return high, low


def split_factor(factor, n, offsets, after=()):
    rows, order = factor.shape
    width, count = order // (2 * n), 2 * len(offsets)

    def kernel(factor_ref, *refs):
        out_refs, (slots, arrived) = refs[len(after) : len(after) + count], refs[-2:]
        me = lax.axis_index("blk")

        def fetch(at):
            owner = jnp.bitwise_xor(me, offsets[at // 2])
            start = pl.multiple_of((2 * owner + at % 2) * width, width)
            return pltpu.make_async_copy(
                factor_ref.at[:, pl.ds(start, width)], slots.at[at % 3], arrived.at[at % 3]
            )

        fetch(0).start()
        fetch(1).start()
        for at in range(count):
            if at + 2 < count:
                fetch(at + 2).start()
            fetch(at).wait()

            @pl.loop(0, rows // 64)
            def _(tile):
                own = pl.ds(pl.multiple_of(tile * 64, 64), 64)
                high, low = high_low(slots[at % 3, own, :])
                out_refs[at][own, :width] = high
                out_refs[at][own, width:] = low

    pieces = pl.pallas_call(
        kernel,
        out_shape=[jax.ShapeDtypeStruct((rows, 2 * width), jnp.bfloat16)] * count,
        in_specs=[HBM] + [ANYWHERE] * len(after),
        out_specs=[WHOLE] * count,
        scratch_shapes=[pltpu.VMEM((3, rows, width), jnp.float32), pltpu.SemaphoreType.DMA((3,))],
        compiler_params=pltpu.CompilerParams(vmem_limit_bytes=40 * 2**20),
        cost_estimate=pl.CostEstimate(flops=0, bytes_accessed=8 * count * rows * width, transcendentals=0),
    )(factor, *after)
    return [pieces[2 * at : 2 * at + 2] for at in range(len(offsets))]


def recurrence_coefficients(bounds, columns):
    def kernel(bounds_ref, out_ref):
        centre = (bounds_ref[0] + bounds_ref[1]) / 2.0
        radius = (bounds_ref[1] - bounds_ref[0]) / 2.0
        out_ref[0:1, :] = jnp.full((1, columns), centre, jnp.float32)
        out_ref[1:2, :] = 1.0 / jnp.full((1, columns), radius, jnp.float32)

    return pl.pallas_call(
        kernel,
        out_shape=jax.ShapeDtypeStruct((2, columns), jnp.float32),
        in_specs=[SCALARS],
        out_specs=WHOLE,
        compiler_params=params(),
    )(bounds)


def stack_vectors(stacked_ref, at, vectors):
    width, columns = vectors.shape
    high, low = high_low(vectors)
    for start in (0, width):
        stacked_ref[at, start : start + width, :columns] = high
        stacked_ref[at, start : start + width, columns:] = low


def stack_all(stacked_ref, vector_refs):
    width, at = stacked_ref.shape[1] // 2, 0
    for ref in vector_refs:
        for start in range(0, ref.shape[0], width):
            stack_vectors(stacked_ref, at, ref[start : start + width, :])
            at += 1


def product_tile(pieces, stacked_ref, rows, columns):
    total = None
    for at, piece in enumerate(pieces):
        term = jnp.dot(piece[rows, :], stacked_ref[at], preferred_element_type=jnp.float32)
        total = term if total is None else total + term
    return total[:, :columns] + total[:, columns:]


def row_tiles(rows, largest=256):
    tile = min(rows, largest)
    return [slice(start, start + tile) for start in range(0, rows, tile)]


def product_cost(pieces, rows):
    doubled = pieces[0].shape[1]
    return pl.CostEstimate(
        flops=2 * rows * doubled * 256 * len(pieces),
        bytes_accessed=2 * rows * doubled * len(pieces),
        transcendentals=0,
    )


def partial_product(total, pieces, vectors):
    n, m = len(pieces), len(vectors)
    (rows, doubled), columns = pieces[0].shape, vectors[0].shape[1]

    def kernel(*refs):
        piece_refs, vector_refs = refs[:n], refs[n : n + m]
        total_ref = refs[n + m] if total is not None else None
        out_ref, stacked_ref = refs[-2:]
        stack_all(stacked_ref, vector_refs)
        for tile in row_tiles(rows, 512):
            value = product_tile(piece_refs, stacked_ref, tile, columns)
            out_ref[tile, :] = value if total_ref is None else total_ref[tile, :] + value

    operands = [*pieces, *vectors] + ([] if total is None else [total])
    return pl.pallas_call(
        kernel,
        out_shape=jax.ShapeDtypeStruct((rows, columns), jnp.float32),
        in_specs=[WHOLE] * len(operands),
        out_specs=WHOLE,
        scratch_shapes=[pltpu.VMEM((n, doubled, 2 * columns), jnp.bfloat16)],
        compiler_params=params(),
        cost_estimate=product_cost(pieces, rows),
    )(*operands)


def forwarded(value):
    def kernel(value_ref, out_ref):
        out_ref[...] = value_ref[...]

    return pl.pallas_call(
        kernel,
        out_shape=jax.ShapeDtypeStruct(value.shape, value.dtype),
        in_specs=[WHOLE],
        out_specs=WHOLE,
        compiler_params=params(),
        cost_estimate=pl.CostEstimate(flops=3 * 10**9, bytes_accessed=0, transcendentals=0),
    )(value)


def recurrence_step(coefficients, total, pieces, vectors, current, previous, at):
    n, m = len(pieces), len(vectors)
    half, columns = current[at].shape
    doubled = pieces[0].shape[1]

    def kernel(coefficient_ref, *refs):
        piece_refs, refs = refs[:n], refs[n:]
        vector_refs, refs = refs[:m], refs[m:]
        total_ref, refs = (refs[0], refs[1:]) if total is not None else (None, refs)
        current_ref, refs = refs[0], refs[1:]
        previous_ref = refs[0] if previous else None
        out_ref, stacked_ref = refs[-2:]
        stack_all(stacked_ref, vector_refs)
        centre, inverse_radius = coefficient_ref[0:1, :columns], coefficient_ref[1:2, :columns]
        for own in row_tiles(half):
            tile = slice(at * half + own.start, at * half + own.stop)
            value = product_tile(piece_refs, stacked_ref, tile, columns)
            if total_ref is not None:
                value = value + total_ref[tile, :]
            value = (value - centre * current_ref[own, :]) * inverse_radius
            if previous_ref is not None:
                value = 2.0 * value - previous_ref[own, :]
            out_ref[own, :] = value

    operands = [*pieces, *vectors] + ([] if total is None else [total])
    operands += [current[at]] + ([previous[at]] if previous else [])
    return pl.pallas_call(
        kernel,
        out_shape=jax.ShapeDtypeStruct((half, columns), jnp.float32),
        in_specs=[WHOLE] * (1 + len(operands)),
        out_specs=WHOLE,
        scratch_shapes=[pltpu.VMEM((n, doubled, 2 * columns), jnp.bfloat16)],
        compiler_params=params(),
        cost_estimate=product_cost(pieces, half),
    )(coefficients, *operands)


def dot_high(left_side, right_side, contract):
    return lax.dot_general(
        left_side, right_side, (contract, ((), ())), precision=HIGHEST, preferred_element_type=jnp.float32
    )


def tree_sum(values):
    while len(values) > 1:
        values = [values[at] + values[at + 1] for at in range(0, len(values), 2)]
    return values[0]


def gram_of(halves):
    def kernel(*refs):
        *in_refs, out_ref = refs
        total = None
        for ref in in_refs:
            term = dot_high(ref[...], ref[...], ((0,), (0,)))
            total = term if total is None else total + term
        out_ref[...] = total

    columns = halves[0].shape[1]
    return pl.pallas_call(
        kernel,
        out_shape=jax.ShapeDtypeStruct((columns, columns), jnp.float32),
        in_specs=[WHOLE] * len(halves),
        out_specs=WHOLE,
        compiler_params=params(),
    )(*halves)


def three_parts(values):
    high = values.astype(jnp.bfloat16)
    return (high, *high_low(values - high.astype(jnp.float32)))


def dot_thin(left_side, right_side):
    a, b = three_parts(left_side), three_parts(right_side)
    pairs = [(a[0], b[0]), (a[0], b[1]), (a[1], b[0]), (a[1], b[1]), (a[0], b[2]), (a[2], b[0])]
    return lax.dot_general(
        jnp.concatenate([pair[0].astype(jnp.float32) for pair in pairs], axis=0).T.astype(jnp.bfloat16),
        jnp.concatenate([pair[1].astype(jnp.float32) for pair in pairs], axis=0).astype(jnp.bfloat16),
        (((1,), (0,)), ((), ())),
        preferred_element_type=jnp.float32,
    )


def inverse_cholesky(terms, after=()):
    columns = terms[0].shape[0]
    high = 16

    def kernel(*refs):
        term_refs, (out_ref, gram_ref, inverse_ref) = refs[: len(terms)], refs[-3:]
        gram_ref[...] = tree_sum([ref[...] for ref in term_refs])
        row_at = lax.broadcasted_iota(jnp.int32, (columns, columns), 0)
        column_at = lax.broadcasted_iota(jnp.int32, (columns, columns), 1)
        inverse_ref[...] = jnp.where(row_at == column_at, 1.0, 0.0)
        sub_row = lax.broadcasted_iota(jnp.int32, (high, columns), 0)
        for start in range(0, columns, high):
            stop = start + high
            own, inverse = gram_ref[start:stop, :], inverse_ref[start:stop, :]
            spread = [
                jnp.broadcast_to(own[:, start + at : start + at + 1], (high, columns)) for at in range(high)
            ]
            pivots = jnp.ones((high, columns), jnp.float32)
            reciprocals = jnp.ones((high, columns), jnp.float32)
            for at in range(high):
                pivot = jnp.broadcast_to(spread[at][at : at + 1, :], (high, columns))
                reciprocal = 1.0 / pivot
                pivots = jnp.where(sub_row == at, pivot, pivots)
                reciprocals = jnp.where(sub_row == at, reciprocal, reciprocals)
                if at + 1 == high:
                    break
                factor = jnp.where(sub_row > at, spread[at], 0.0) * reciprocal
                for later in range(at + 1, high):
                    spread[later] = spread[later] - factor * spread[later][at : at + 1, :]
                own = own - factor * own[at : at + 1, :]
                inverse = inverse - factor * inverse[at : at + 1, :]
            inverse_ref[start:stop, :] = inverse / jnp.sqrt(pivots)
            if stop < columns:
                update = dot_thin(own * reciprocals, jnp.concatenate([own, inverse], axis=1))
                gram_ref[stop:, :] = gram_ref[stop:, :] - update[stop:, :columns]
                inverse_ref[stop:, :] = inverse_ref[stop:, :] - update[stop:, columns:]
        out_ref[...] = inverse_ref[...].T

    return pl.pallas_call(
        kernel,
        out_shape=jax.ShapeDtypeStruct((columns, columns), jnp.float32),
        in_specs=[WHOLE] * len(terms) + [ANYWHERE] * len(after),
        out_specs=WHOLE,
        scratch_shapes=[pltpu.VMEM((columns, columns), jnp.float32)] * 2,
        compiler_params=params(),
        cost_estimate=pl.CostEstimate(flops=25 * 10**9, bytes_accessed=0, transcendentals=0),
    )(*terms, *after)


def two_parts(values):
    return jnp.concatenate(high_low(values), axis=1)


def dot_parts(left_side, right_side):
    columns = right_side.shape[1]
    right_parts = two_parts(right_side)
    product = jnp.dot(
        two_parts(left_side),
        jnp.concatenate([right_parts, right_parts], axis=0),
        preferred_element_type=jnp.float32,
    )
    return product[:, :columns] + product[:, columns:]


def times_right(halves, right_side, transposed=False):
    def kernel(right_ref, *refs):
        in_refs, (out_ref, *parts_ref) = refs[: len(halves)], refs[len(halves) :]
        at = 0
        for ref in in_refs:
            for tile in row_tiles(ref.shape[0]):
                own = slice(at + tile.start, at + tile.stop)
                value = dot_parts(ref[tile, :], right_ref[...])
                out_ref[own, :] = value
                if transposed:
                    parts_ref[0][:, own] = two_parts(value).T
            at += ref.shape[0]

    rows, columns = sum(half.shape[0] for half in halves), halves[0].shape[1]
    out_shape = [jax.ShapeDtypeStruct((rows, columns), jnp.float32)]
    if transposed:
        out_shape.append(jax.ShapeDtypeStruct((2 * columns, rows), jnp.bfloat16))
    return pl.pallas_call(
        kernel,
        out_shape=out_shape,
        in_specs=[WHOLE] * (1 + len(halves)),
        out_specs=[WHOLE] * len(out_shape),
        compiler_params=params(),
        cost_estimate=pl.CostEstimate(flops=2 * rows * 256 * 256, bytes_accessed=0, transcendentals=0),
    )(right_side, *halves)


def image_and_projected(total, pieces, vectors, inverse_upper, basis_parts):
    n, m = len(pieces), len(vectors)
    (rows, doubled), columns = pieces[0].shape, vectors[0].shape[1]

    def kernel(*refs):
        piece_refs, refs = refs[:n], refs[n:]
        vector_refs, refs = refs[:m], refs[m:]
        total_ref, refs = (refs[0], refs[1:]) if total is not None else (None, refs)
        inverse_ref, basis_ref, image_ref, projected_ref, stacked_ref = refs
        stack_all(stacked_ref, vector_refs)
        projected = None
        for tile in row_tiles(rows):
            image = product_tile(piece_refs, stacked_ref, tile, columns)
            if total_ref is not None:
                image = image + total_ref[tile, :]
            image_ref[tile, :] = image
            term = jnp.dot(basis_ref[:, tile], two_parts(image), preferred_element_type=jnp.float32)
            projected = term if projected is None else projected + term
        projected = projected[:columns, :] + projected[columns:, :]
        projected = projected[:, :columns] + projected[:, columns:]
        projected_ref[...] = dot_parts(projected, inverse_ref[...])

    operands = [*pieces, *vectors] + ([] if total is None else [total]) + [inverse_upper, basis_parts]
    return pl.pallas_call(
        kernel,
        out_shape=[
            jax.ShapeDtypeStruct((rows, columns), jnp.float32),
            jax.ShapeDtypeStruct((columns, columns), jnp.float32),
        ],
        in_specs=[WHOLE] * len(operands),
        out_specs=[WHOLE] * 2,
        scratch_shapes=[pltpu.VMEM((n, doubled, 2 * columns), jnp.bfloat16)],
        compiler_params=params(),
        cost_estimate=product_cost(pieces, rows),
    )(*operands)


def residual_of(mapped, basis_rows, terms):
    def kernel(mapped_ref, basis_ref, *refs):
        *term_refs, projected_ref, residual_ref = refs
        projected = tree_sum([ref[...] for ref in term_refs])
        projected_ref[...] = projected
        for tile in row_tiles(mapped.shape[0]):
            residual_ref[tile, :] = mapped_ref[tile, :] - dot_parts(basis_ref[tile, :], projected)

    return pl.pallas_call(
        kernel,
        out_shape=[
            jax.ShapeDtypeStruct(terms[0].shape, jnp.float32),
            jax.ShapeDtypeStruct(mapped.shape, jnp.float32),
        ],
        in_specs=[WHOLE] * (2 + len(terms)),
        out_specs=[WHOLE] * 2,
        compiler_params=params(),
    )(mapped, basis_rows, *terms)


def exchange(value, offset, n):
    return lax.ppermute(value, "blk", [(at, at ^ offset) for at in range(n)])


def local(n, factor, initial, bounds):
    rows, columns = initial.shape
    half = rows // 2
    coefficients = recurrence_coefficients(bounds, columns)

    if n == 4:
        own, along_x = split_factor(factor, n, (0, 1))
        rest = []

        def gather_product(halves, send_on=forwarded):
            top, bottom = halves
            x_top = exchange(top, 1, n)
            y_bottom, x_bottom, y_top = exchange(bottom, 2, n), exchange(bottom, 1, n), exchange(top, 2, n)
            xy_top, xy_bottom = exchange(send_on(x_top), 2, n), exchange(y_bottom, 1, n)
            if not rest:
                rest.extend(split_factor(factor, n, (2, 3), after=(x_top, y_bottom)))
            along_y, across = rest
            total = partial_product(None, own, halves)
            total = partial_product(total, [along_x[0], along_y[1]], [x_top, y_bottom])
            total = partial_product(total, [along_x[1], along_y[0]], [x_bottom, y_top])
            total = partial_product(total, [across[1]], [xy_bottom])
            return (total, [across[0]], [xy_top]), (x_top, y_bottom)

        def all_terms(term, offsets=(1, 2, 3)):
            return [term] + [exchange(term, offset, n) for offset in offsets]
    else:
        pieces = [piece for pair in split_factor(factor, n, range(n)) for piece in pair]

        def all_terms(value, offsets=None):
            gathered = lax.all_gather(value, "blk")
            me = lax.axis_index("blk")
            return [gathered[jnp.bitwise_xor(me, offset)] for offset in range(n)]

        def gather_product(halves, send_on=None):
            return (None, pieces, all_terms(jnp.concatenate(halves))), ()

    previous, current = None, [initial[:half], initial[half:]]
    for order_step in range(DEGREE):
        product, _ = gather_product(current)
        following = [recurrence_step(coefficients, *product, current, previous, at) for at in range(2)]
        previous, current = current, following

    gram_terms = all_terms(gram_of(current))
    product, arrived = gather_product(current, send_on=lambda value: value)
    inverse_upper = inverse_cholesky(gram_terms, after=arrived)
    basis_rows, basis_parts = times_right(current, inverse_upper, transposed=True)
    image, projected_term = image_and_projected(*product, inverse_upper, basis_parts)
    projected_terms = all_terms(projected_term, (3, 1, 2))
    (mapped,) = times_right([image], inverse_upper)
    projected, residual = residual_of(mapped, basis_rows, projected_terms)
    return (basis_rows, projected, residual)


def solution(mesh):
    in_specs = (P(("bulk", "blk"), None), P(("bulk", "blk"), None), P("bulk"))
    out_specs = (P(("bulk", "blk"), None), P("bulk", None), P(("bulk", "blk"), None))
    return jax.shard_map(
        functools.partial(local, mesh.shape["blk"]),
        mesh=mesh,
        in_specs=in_specs,
        out_specs=out_specs,
        check_vma=False,
    )
```
